32 devices in a mesh: dp: 8 (over y, x, core), mp: 4 (over z).
Axes of the slice: x: 2, y: 2, z: 4, core: 2. Of those that a mesh axis runs over, the one named last changes fastest.
Arguments:
- tokens: bfloat16 [25600, 512], P('dp'), may hold values from -6 to 6
- cotangent: bfloat16 [25600, 512], P('dp'), may hold values from -6 to 6
- group_windows: int32 [8], P('dp'), may hold values from 16 to 32, as said below
- offset_index: int32 [100, 100], replicated, may hold values from 0 to 360, as said below
- first_gain: bfloat16 [512], replicated, may hold values from 0.099609375 to 1.8984375
- first_shift: bfloat16 [512], replicated, may hold values from -3 to 3
- triple_weight: bfloat16 [512, 3, 512], P(None, None, 'mp'), may hold values from -0.25 to 0.25
- query_value_bias: bfloat16 [2, 512], P(None, 'mp'), may hold values from -3 to 3
- bias_table: bfloat16 [361, 16], P(None, 'mp'), may hold values from -4 to 4
- output_weight: bfloat16 [512, 512], P('mp'), may hold values from -1 to 1
- output_bias: bfloat16 [512], replicated, may hold values from -3 to 3
- second_gain: bfloat16 [512], replicated, may hold values from 0.099609375 to 1.8984375
- second_shift: bfloat16 [512], replicated, may hold values from -3 to 3
- expand_weight: bfloat16 [512, 2048], P(None, 'mp'), may hold values from -0.25 to 0.25
- expand_bias: bfloat16 [2048], P('mp'), may hold values from -3 to 3
- shrink_weight: bfloat16 [2048, 512], P('mp'), may hold values from -0.125 to 0.125
- shrink_bias: bfloat16 [512], replicated, may hold values from -3 to 3
Outputs:
- block_output: bfloat16 [25600, 512], P('dp')
- grad_tokens: bfloat16 [25600, 512], P('dp')
- grad_first_gain: float32 [512], replicated
- grad_first_shift: float32 [512], replicated
- grad_triple_weight: float32 [512, 3, 512], P(None, None, 'mp')
- grad_query_value_bias: float32 [2, 512], P(None, 'mp')
- grad_bias_table: float32 [361, 16], P(None, 'mp')
- grad_output_weight: float32 [512, 512], P('mp')
- grad_output_bias: float32 [512], replicated
- grad_second_gain: float32 [512], replicated
- grad_second_shift: float32 [512], replicated
- grad_expand_weight: float32 [512, 2048], P(None, 'mp')
- grad_expand_bias: float32 [2048], P('mp')
- grad_shrink_weight: float32 [2048, 512], P('mp')
- grad_shrink_bias: float32 [512], replicated
The draws below stay inside these ranges and needn't reach their ends.
Inputs may be any that keep to these rules, and one draw needn't show every extreme that they name: `group_windows`: entry g counts the windows of group g of dp; they fill its first window slots and the other slots of the 32 are empty; in every draw some group has all 32 filled. `offset_index`: entry [i, j] names the bias table row of the offset between positions i and j of a 10 x 10 window, positions row-major; equal offsets share a row and different offsets have different rows.
All inputs are finite; a program needn't handle non-finite values.
Results may differ from the reference program's by a relative error of at most 0.022.
Values may be sent and summed in bfloat16 or wider, within the bound.
A program may use at most 128 MiB of HBM per device.

```python
import jax
import jax.numpy as jnp
from jax import lax

HEADS = 16
HEAD_DIM = 32
D = 512
FF = 2048
WIN = 10
CAP = 32
AREA = 100
TABLE = 361
ROWS = 25600
N_DP = 8


def draw_group_windows(key, part):
    key = jax.random.fold_in(key, 11)
    key_count, key_full = jax.random.split(key)
    counts = jax.random.randint(key_count, (N_DP,), (CAP + 1) // 2, CAP + 1)
    busiest = jax.random.randint(key_full, (), 0, N_DP)
    return jnp.where(jnp.arange(N_DP) == busiest, CAP, counts).astype(jnp.int32)


def draw_offset_index(key, part):
    key = jax.random.fold_in(key, 23)
    ordering = jax.random.permutation(key, (2 * WIN - 1) ** 2)
    position = jnp.arange(AREA, dtype=jnp.int32)
    row_pos = position // WIN
    col_pos = position % WIN
    offset = (row_pos[:, None] - row_pos[None, :] + WIN - 1) * (2 * WIN - 1) + (col_pos[:, None] - col_pos[None, :] + WIN - 1)
    return ordering[offset].astype(jnp.int32)


def levels(rng, dims, shards, low, largest):
    loudness, own = 1.0, jax.random.fold_in(rng, 6)
    for dim, parts in shards:
        draws = jnp.exp(jax.random.uniform(jax.random.fold_in(own, dim), (parts,), jnp.float32, low / len(shards), largest / len(shards)))
        loudness = loudness * jnp.repeat(draws, dims[dim] // parts).reshape([-1 if axis == dim else 1 for axis in range(len(dims))])
    return loudness


def centred(stream_key, shape, width, bound, cuts=(), kind=jnp.bfloat16):
    values = jax.random.normal(stream_key, shape, jnp.float32) * width
    if len(cuts) > 0:
        values = levels(stream_key, shape, cuts, -0.22, 0.18) * values
    return jnp.clip(values, min=-bound, max=bound).astype(kind)


def setup_inputs(seed: int = 0) -> dict:
    arg_keys = jax.random.split(jax.random.key(seed), 18)
    tokens = centred(arg_keys[0], (ROWS, D), 1.0, 6.0, ((0, 8),))
    cotangent = centred(arg_keys[1], (ROWS, D), 1.0, 6.0, ((0, 8),))
    group_windows = draw_group_windows(jax.random.fold_in(arg_keys[17], 71), 0)
    offset_index = draw_offset_index(jax.random.fold_in(arg_keys[17], 71), 0)
    first_gain = jnp.clip(1.0 + 0.18 * jax.random.normal(arg_keys[4], (D,), jnp.float32), 0.099609375, 1.8984375).astype(jnp.bfloat16)
    first_shift = centred(arg_keys[5], (D,), 0.5, 3.0)
    triple_weight = centred(arg_keys[6], (D, 3, D), D ** -0.5, 0.25, ((2, 4),))
    query_value_bias = centred(arg_keys[7], (2, D), 0.5, 3.0, ((1, 4),))
    bias_table = centred(arg_keys[8], (TABLE, HEADS), 1.0, 4.0, ((1, 4),))
    output_weight = centred(arg_keys[9], (D, D), (D // 16) ** -0.5, 1.0, ((0, 4),))
    output_bias = centred(arg_keys[10], (D,), 0.5, 3.0)
    second_gain = jnp.clip(1.0 + 0.18 * jax.random.normal(arg_keys[11], (D,), jnp.float32), 0.099609375, 1.8984375).astype(jnp.bfloat16)
    second_shift = centred(arg_keys[12], (D,), 0.5, 3.0)
    expand_weight = centred(arg_keys[13], (D, FF), D ** -0.5, 0.25, ((1, 4),))
    expand_bias = centred(arg_keys[14], (FF,), 0.5, 3.0, ((0, 4),))
    shrink_weight = centred(arg_keys[15], (FF, D), FF ** -0.5, 0.125, ((0, 4),))
    shrink_bias = centred(arg_keys[16], (D,), 0.5, 3.0)
    return dict(tokens=tokens, cotangent=cotangent, group_windows=group_windows, offset_index=offset_index, first_gain=first_gain, first_shift=first_shift, triple_weight=triple_weight, query_value_bias=query_value_bias, bias_table=bias_table, output_weight=output_weight, output_bias=output_bias, second_gain=second_gain, second_shift=second_shift, expand_weight=expand_weight, expand_bias=expand_bias, shrink_weight=shrink_weight, shrink_bias=shrink_bias)


EPSILON = 1e-05
HIGHEST_PRECISION = lax.Precision.HIGHEST

@jax.custom_vjp
def low(v):
    return lax.optimization_barrier(v.astype(jnp.bfloat16)).astype(jnp.float32)

@jax.custom_vjp
def low_back(v):
    return v

def low_keep(v):
    return (low(v), None)

def low_pass(kept, grad):
    return (grad,)

def back_keep(v):
    return (v, None)

def back_low(kept, grad):
    return (low(grad),)
low.defvjp(low_keep, low_pass)
low_back.defvjp(back_keep, back_low)

def layer_norm(values, norm_gain, norm_shift):
    centered = values - lax.optimization_barrier(jnp.mean(values, axis=-1, keepdims=True))
    spread = lax.optimization_barrier(jnp.mean(centered * centered, axis=-1, keepdims=True))
    return centered * lax.rsqrt(spread + EPSILON) * norm_gain + norm_shift

def rounded_both(values):
    return low_back(low(values))

def block_forward(tokens, weights, offset_index):
    first_gain, first_shift, triple_weight, query_value_bias, bias_table, output_weight, output_bias, second_gain, second_shift, expand_weight, expand_bias, shrink_weight, shrink_bias = weights
    total_rows = tokens.shape[0]
    windows = total_rows // AREA
    head_shape = (windows, AREA, HEADS, HEAD_DIM)
    first_normed = low(layer_norm(tokens, first_gain, first_shift))
    triple = jnp.einsum('rd,dce->rce', first_normed, triple_weight, precision=HIGHEST_PRECISION)
    queries = rounded_both(triple[:, 0] + query_value_bias[0]).reshape(head_shape)
    key_rows = rounded_both(triple[:, 1]).reshape(head_shape)
    value_rows = rounded_both(triple[:, 2] + query_value_bias[1]).reshape(head_shape)
    relative = jnp.transpose(bias_table[offset_index], (2, 0, 1))
    raw_scores = jnp.einsum('wqhe,wkhe->whqk', queries, key_rows, precision=HIGHEST_PRECISION)
    scores = low_back(raw_scores * HEAD_DIM ** (-0.5) + relative[None])
    probs_low = low(jax.nn.softmax(scores, axis=-1))
    mixed = jnp.einsum('whqk,wkhe->wqhe', probs_low, value_rows, precision=HIGHEST_PRECISION)
    mixed = rounded_both(mixed.reshape(total_rows, D))
    branch = low_back(jnp.dot(mixed, output_weight, precision=HIGHEST_PRECISION) + output_bias)
    middle = tokens + branch
    second_normed = low(layer_norm(middle, second_gain, second_shift))
    hidden = low_back(jnp.dot(second_normed, expand_weight, precision=HIGHEST_PRECISION) + expand_bias)
    active = low(jax.nn.gelu(hidden, approximate=False))
    return middle + low_back(jnp.dot(active, shrink_weight, precision=HIGHEST_PRECISION) + shrink_bias)

def reference(tokens, cotangent, group_windows, offset_index, first_gain, first_shift, triple_weight, query_value_bias, bias_table, output_weight, output_bias, second_gain, second_shift, expand_weight, expand_bias, shrink_weight, shrink_bias):
    weights = tuple((array.astype(jnp.float32) for array in (first_gain, first_shift, triple_weight, query_value_bias, bias_table, output_weight, output_bias, second_gain, second_shift, expand_weight, expand_bias, shrink_weight, shrink_bias)))
    row_window = jnp.arange(ROWS, dtype=jnp.int32) // AREA
    owner_group = row_window // CAP
    live_mask = (row_window % CAP < group_windows[owner_group]).astype(jnp.float32)[:, None]

    def run_block(token_values, weight_values):
        return block_forward(token_values, weight_values, offset_index)
    result, pullback = jax.vjp(run_block, tokens.astype(jnp.float32), weights)
    grad_input, grad_weights = pullback(cotangent.astype(jnp.float32) * live_mask)
    return ((result * live_mask).astype(jnp.bfloat16), grad_input.astype(jnp.bfloat16), grad_weights[0], grad_weights[1], grad_weights[2], grad_weights[3], grad_weights[4], grad_weights[5], grad_weights[6], grad_weights[7], grad_weights[8], grad_weights[9], grad_weights[10], grad_weights[11], grad_weights[12])
```

```python
import jax
import jax.numpy as jnp
from jax import lax
from jax.sharding import PartitionSpec as P

AREA = 100


EPSILON = 1e-05
HALF_ROOT = 0.7071067811865476
DENSITY = 0.3989422804014327


def normalize(values):
    centered = values - jnp.mean(values, axis=-1, keepdims=True)
    inv_std = lax.rsqrt(jnp.mean(centered * centered, axis=-1, keepdims=True) + EPSILON)
    return (centered * inv_std, inv_std)


def norm_back(grad_hat, normed_hat, inv_std):
    return inv_std * (
        grad_hat
        - jnp.mean(grad_hat, axis=-1, keepdims=True)
        - normed_hat * jnp.mean(grad_hat * normed_hat, axis=-1, keepdims=True)
    )


def gelu_slope(hidden):
    return (
        0.5 * (1.0 + lax.erf(hidden * HALF_ROOT))
        + hidden * jnp.exp(-0.5 * hidden * hidden) * DENSITY
    )


def row_sums(values):
    return jnp.sum(values.astype(jnp.float32), axis=0)


def attention_scores(queries, key_rows, relative, score_scale):
    raw_scores = jnp.einsum(
        "wqhe,wkhe->whqk", queries, key_rows, preferred_element_type=jnp.float32
    )
    return raw_scores * score_scale + relative[None]


def local(
    tokens,
    cotangent,
    group_windows,
    offset_index,
    first_gain,
    first_shift,
    triple_weight,
    query_value_bias,
    bias_table,
    output_weight,
    output_bias,
    second_gain,
    second_shift,
    expand_weight,
    expand_bias,
    shrink_weight,
    shrink_bias,
):
    mp_size = lax.axis_size("mp")
    mp_index = lax.axis_index("mp")
    total_rows = tokens.shape[0] // mp_size
    first_row = mp_index * total_rows
    tokens = lax.dynamic_slice_in_dim(tokens, first_row, total_rows, 0)
    cotangent = lax.dynamic_slice_in_dim(cotangent, first_row, total_rows, 0)
    triple_weight = lax.all_gather(triple_weight, "mp", axis=2, tiled=True)
    query_value_bias = lax.all_gather(query_value_bias, "mp", axis=1, tiled=True)
    bias_table = lax.all_gather(bias_table, "mp", axis=1, tiled=True)
    output_weight = lax.all_gather(output_weight, "mp", axis=0, tiled=True)
    expand_weight = lax.all_gather(expand_weight, "mp", axis=1, tiled=True)
    expand_bias = lax.all_gather(expand_bias, "mp", axis=0, tiled=True)
    shrink_weight = lax.all_gather(shrink_weight, "mp", axis=0, tiled=True)
    local_width = triple_weight.shape[2]
    local_heads = bias_table.shape[1]
    head_size = local_width // local_heads
    windows = total_rows // AREA
    score_scale = head_size ** (-0.5)
    head_shape = (windows, AREA, local_heads, head_size)
    window_slot = (first_row + lax.broadcasted_iota(jnp.int32, (total_rows, 1), 0)) // AREA
    live_mask = (window_slot < group_windows[0]).astype(jnp.float32)
    table_rows = bias_table.shape[0]
    lookup = (
        offset_index.reshape(AREA * AREA, 1) == lax.broadcasted_iota(jnp.int32, (1, table_rows), 1)
    ).astype(jnp.float32)
    relative = jnp.dot(lookup.astype(jnp.bfloat16), bias_table, preferred_element_type=jnp.float32)
    relative = jnp.transpose(relative.reshape(AREA, AREA, local_heads), (2, 0, 1))
    gain_first = first_gain.astype(jnp.float32)
    shift_first = first_shift.astype(jnp.float32)
    gain_second = second_gain.astype(jnp.float32)
    shift_second = second_shift.astype(jnp.float32)
    tokens_wide = tokens.astype(jnp.float32)
    first_hat, first_inv = normalize(tokens_wide)
    first_normed = (first_hat * gain_first + shift_first).astype(jnp.bfloat16)
    triple = jnp.einsum(
        "rd,dce->rce", first_normed, triple_weight, preferred_element_type=jnp.float32
    )
    bias_wide = query_value_bias.astype(jnp.float32)
    queries = (triple[:, 0] + bias_wide[0]).astype(jnp.bfloat16).reshape(head_shape)
    key_rows = triple[:, 1].astype(jnp.bfloat16).reshape(head_shape)
    value_rows = (triple[:, 2] + bias_wide[1]).astype(jnp.bfloat16).reshape(head_shape)
    scores = attention_scores(queries, key_rows, relative, score_scale)
    row_top = jnp.max(scores, axis=-1, keepdims=True)
    log_total = row_top + jnp.log(jnp.sum(jnp.exp(scores - row_top), axis=-1, keepdims=True))
    probs_low = jnp.exp(scores - log_total).astype(jnp.bfloat16)
    mixed = jnp.einsum("whqk,wkhe->wqhe", probs_low, value_rows, preferred_element_type=jnp.float32)
    mixed = mixed.reshape(total_rows, local_width).astype(jnp.bfloat16)
    branch_term = jnp.dot(mixed, output_weight, preferred_element_type=jnp.float32)
    middle = (
        tokens_wide
        + branch_term
        + output_bias.astype(jnp.float32)
    )
    second_hat, second_inv = normalize(middle)
    second_normed = (second_hat * gain_second + shift_second).astype(jnp.bfloat16)
    hidden = jnp.dot(
        second_normed, expand_weight, preferred_element_type=jnp.float32
    ) + expand_bias.astype(jnp.float32)
    active = jax.nn.gelu(hidden, approximate=False).astype(jnp.bfloat16)
    shrink_term = jnp.dot(active, shrink_weight, preferred_element_type=jnp.float32)
    grad_result = cotangent.astype(jnp.float32) * live_mask
    result = (
        middle
        + shrink_term
        + shrink_bias.astype(jnp.float32)
    )
    result = result * live_mask
    grad_low = grad_result.astype(jnp.bfloat16)
    grad_shrink_weight = jnp.einsum(
        "rf,rd->fd", active, grad_low, preferred_element_type=jnp.float32
    )
    grad_shrink_bias = row_sums(grad_low)
    grad_active = jnp.einsum(
        "rd,fd->rf", grad_low, shrink_weight, preferred_element_type=jnp.float32
    )
    grad_hidden = (grad_active * gelu_slope(hidden)).astype(jnp.bfloat16)
    grad_expand_weight = jnp.einsum(
        "rd,rf->df", second_normed, grad_hidden, preferred_element_type=jnp.float32
    )
    grad_expand_bias = row_sums(grad_hidden)
    second_back = jnp.einsum(
        "rf,df->rd", grad_hidden, expand_weight, preferred_element_type=jnp.float32
    )
    grad_second = second_back
    grad_middle = grad_result + norm_back(grad_second * gain_second, second_hat, second_inv)
    grad_branch = grad_middle.astype(jnp.bfloat16)
    second_gain_term = jnp.sum(grad_second * second_hat, axis=0)
    second_shift_term = jnp.sum(grad_second, axis=0)
    grad_output_weight = jnp.einsum(
        "rc,rd->cd", mixed, grad_branch, preferred_element_type=jnp.float32
    )
    grad_output_bias = row_sums(grad_branch)
    grad_mixed = jnp.einsum(
        "rd,cd->rc", grad_branch, output_weight, preferred_element_type=jnp.float32
    )
    grad_mixed = grad_mixed.astype(jnp.bfloat16).reshape(head_shape)
    grad_value = jnp.einsum(
        "whqk,wqhe->wkhe", probs_low, grad_mixed, preferred_element_type=jnp.float32
    ).astype(jnp.bfloat16)
    attn_probs = jnp.exp(attention_scores(queries, key_rows, relative, score_scale) - log_total)
    grad_probs = jnp.einsum(
        "wqhe,wkhe->whqk", grad_mixed, value_rows, preferred_element_type=jnp.float32
    )
    grad_scores = (
        attn_probs * (grad_probs - jnp.sum(attn_probs * grad_probs, axis=-1, keepdims=True))
    ).astype(jnp.bfloat16)
    grad_query = (
        jnp.einsum("whqk,wkhe->wqhe", grad_scores, key_rows, preferred_element_type=jnp.float32)
        * score_scale
    ).astype(jnp.bfloat16)
    grad_key = (
        jnp.einsum("whqk,wqhe->wkhe", grad_scores, queries, preferred_element_type=jnp.float32)
        * score_scale
    ).astype(jnp.bfloat16)
    score_totals = jnp.sum(grad_scores.astype(jnp.float32), axis=0)
    score_totals = jnp.transpose(score_totals, (1, 2, 0)).reshape(AREA * AREA, local_heads)
    grad_bias_table = jnp.dot(lookup.T, score_totals, precision=lax.Precision.HIGHEST)
    grad_triple = jnp.stack(
        [
            grad_query.reshape(total_rows, local_width),
            grad_key.reshape(total_rows, local_width),
            grad_value.reshape(total_rows, local_width),
        ],
        axis=1,
    )
    grad_triple_weight = jnp.einsum(
        "rd,rce->dce", first_normed, grad_triple, preferred_element_type=jnp.float32
    )
    grad_query_value_bias = jnp.stack([row_sums(grad_triple[:, 0]), row_sums(grad_triple[:, 2])])
    first_back = jnp.einsum(
        "rce,dce->rd", grad_triple, triple_weight, preferred_element_type=jnp.float32
    )
    grad_first = first_back
    grad_input = grad_middle + norm_back(grad_first * gain_first, first_hat, first_inv)
    first_gain_term = jnp.sum(grad_first * first_hat, axis=0)
    first_shift_term = jnp.sum(grad_first, axis=0)
    block_output = lax.all_gather(result.astype(jnp.bfloat16), "mp", axis=0, tiled=True)
    grad_tokens = lax.all_gather(grad_input.astype(jnp.bfloat16), "mp", axis=0, tiled=True)

    def total(value, axis=None):
        value = value.astype(jnp.bfloat16)
        if axis is None:
            return lax.psum(value, ("mp", "dp")).astype(jnp.float32)
        value = lax.psum_scatter(value, "mp", scatter_dimension=axis, tiled=True)
        return lax.psum(value, "dp").astype(jnp.float32)

    summed = (
        total(first_gain_term),
        total(first_shift_term),
        total(grad_triple_weight, 2),
        total(grad_query_value_bias, 1),
        total(grad_bias_table, 1),
        total(grad_output_weight, 0),
        total(grad_output_bias),
        total(second_gain_term),
        total(second_shift_term),
        total(grad_expand_weight, 1),
        total(grad_expand_bias, 0),
        total(grad_shrink_weight, 0),
        total(grad_shrink_bias),
    )
    return (
        block_output,
        grad_tokens,
        summed[0],
        summed[1],
        summed[2],
        summed[3],
        summed[4],
        summed[5],
        summed[6],
        summed[7],
        summed[8],
        summed[9],
        summed[10],
        summed[11],
        summed[12],
    )


def solution(mesh):
    in_specs = (
        P("dp", None),
        P("dp", None),
        P("dp"),
        P(),
        P(),
        P(),
        P(None, None, "mp"),
        P(None, "mp"),
        P(None, "mp"),
        P("mp", None),
        P(),
        P(),
        P(),
        P(None, "mp"),
        P("mp"),
        P("mp", None),
        P(),
    )
    out_specs = (
        P("dp", None),
        P("dp", None),
        P(),
        P(),
        P(None, None, "mp"),
        P(None, "mp"),
        P(None, "mp"),
        P("mp", None),
        P(),
        P(),
        P(),
        P(None, "mp"),
        P("mp"),
        P("mp", None),
        P(),
    )
    return jax.shard_map(local, mesh=mesh, in_specs=in_specs, out_specs=out_specs, check_vma=False)
```

```python
import functools
import math
import jax
import jax.numpy as jnp
from jax import lax
from jax.experimental import pallas as pl
from jax.experimental.pallas import tpu as pltpu
from jax.sharding import PartitionSpec as P

AREA = 100
PAD = 104
HEAD = 32
LANES = 128
PACK = LANES // HEAD
BATCH = 4
CHUNK = BATCH * AREA
ROWS = BATCH * PAD
EPSILON = 1e-05
DENSITY = 0.3989422804014327
LOG2E = 1.4426950408889634
F32 = jnp.float32
BF16 = jnp.bfloat16
MESH = pl.DeviceIdType.MESH
VMEM_LIMIT = 60 * 2**20


def dot(a, b):
    return jnp.dot(a, b, preferred_element_type=F32)


def dot_nt(a, b):
    return lax.dot_general(a, b, (((1,), (1,)), ((), ())), preferred_element_type=F32)


def dot_tn(a, b):
    return lax.dot_general(a, b, (((0,), (0,)), ((), ())), preferred_element_type=F32)


def normalize(values):
    centered = values - jnp.mean(values, axis=-1, keepdims=True)
    inv = lax.rsqrt(jnp.mean(centered * centered, axis=-1, keepdims=True) + EPSILON)
    return centered * inv, inv


def norm_back(grad, hat, inv):
    return inv * (
        grad
        - jnp.mean(grad, axis=-1, keepdims=True)
        - hat * jnp.mean(grad * hat, axis=-1, keepdims=True)
    )


def normal_cdf(hidden):
    z = jnp.abs(hidden) * 0.7071067811865476
    t = 1.0 / (1.0 + 0.3275911 * z)
    poly = t * (
        0.127414796 + t * (-0.142248368 + t * (0.7107068705 + t * (-0.7265760135 + t * 0.5307027145)))
    )
    bell = jnp.exp2(hidden * hidden * (-0.5 * LOG2E))
    tail = poly * bell
    return jnp.where(hidden > 0.0, 1.0 - tail, tail), bell


def head_of(shape, axis):
    return lax.broadcasted_iota(jnp.int32, shape, axis) // HEAD


def pad_rows(v):
    return jnp.concatenate([v, jnp.zeros((LANES - PAD, v.shape[1]), v.dtype)], axis=0)


def spread_rows(v):
    head = head_of((LANES, LANES), 1)
    full = pad_rows(v)
    return jnp.concatenate([jnp.where(head == h, full, 0.0) for h in range(PACK)], axis=0).astype(BF16)


def spread_columns(v):
    head = head_of((LANES, LANES), 0)
    turned = pad_rows(v).T
    return jnp.concatenate([jnp.where(head == h, turned, 0.0) for h in range(PACK)], axis=1).astype(BF16)


def diagonal(full):
    head = head_of((LANES, LANES), 0)
    out = full[:, 0:LANES]
    for h in range(1, PACK):
        out = jnp.where(head == h, full[:, h * LANES : (h + 1) * LANES], out)
    return out


def span(w, size=PAD):
    return pl.ds(pl.multiple_of(w * PAD, 8), size)


def load_rows(source, wide, padded):
    wide[...] = source.astype(F32)
    for w in range(BATCH):
        padded[w * PAD : w * PAD + AREA, :] = wide[w * AREA : (w + 1) * AREA, :]


def store_rows(padded, wide, target, scales=None):
    for w in range(BATCH):
        rows = padded[w * PAD : w * PAD + AREA, :]
        wide[w * AREA : (w + 1) * AREA, :] = rows if scales is None else rows * scales[w]
    target[...] = wide[...].astype(BF16)


class Sizes:
    def __init__(self, shards, loc, units):
        self.shards, self.loc, self.units = shards, loc, units
        self.width = shards * loc
        self.groups = self.width // LANES
        self.columns = 4 * loc + 2 * units

    def attention_part(self, weights, c):
        at = slice(c * self.loc, (c + 1) * self.loc)
        return jnp.concatenate([weights[z, at, :] for z in range(self.shards)], axis=0)

    def expand_part(self, weights, i):
        return weights[i, pl.ds(4 * self.loc, self.units), :]

    def shrink_part(self, weights, i):
        return weights[i, pl.ds(4 * self.loc + self.units, self.units), :]

    def add_attention(self, dw, c, value):
        for z in range(self.shards):
            at = slice(c * self.loc, (c + 1) * self.loc)
            dw[z, :, at] += value[:, z * self.loc : (z + 1) * self.loc]


def attention(sizes, bias, vecs, wide_bias, weights, xs, work, low, qkv, mixed, middle, keep):
    width, groups = sizes.width, sizes.groups
    scale = HEAD ** (-0.5) * LOG2E
    for w in range(BATCH):
        hat, _ = normalize(xs[span(w), :])
        work[span(w), :] = hat * vecs[0:1, :] + vecs[1:2, :]
    low[...] = work[...].astype(BF16)
    for c in range(3):
        at = slice(c * width, (c + 1) * width)
        qkv[:, at] = dot_nt(low[...], sizes.attention_part(weights, c)) + wide_bias[:, at]

    def attend(w, _):
        row = span(w)
        for g in range(groups):
            col = g * LANES
            q = qkv[row, pl.ds(col, LANES)].astype(BF16)
            k = qkv[row, pl.ds(width + col, LANES)]
            v = qkv[row, pl.ds(2 * width + col, LANES)]
            scores = dot(q, spread_columns(k))
            parts = []
            for h in range(PACK):
                s = scores[:, h * LANES : (h + 1) * LANES] * scale + bias[g * PACK + h]
                e = jnp.exp2(s - jnp.max(s, axis=-1, keepdims=True))
                parts.append(e * (1.0 / jnp.sum(e, axis=-1, keepdims=True)))
            probs = jnp.concatenate(parts, axis=1).astype(BF16)
            if keep is not None:
                keep[w * groups + g] = probs
            mixed[row, pl.ds(col, LANES)] = dot(probs, spread_rows(v))
        return 0

    lax.fori_loop(0, BATCH, attend, 0)
    middle[...] = xs[...] + dot(mixed[...].astype(BF16), sizes.attention_part(weights, 3)) + vecs[2:3, :]


def second_norm(vecs, middle, work, low):
    for w in range(BATCH):
        hat, _ = normalize(middle[span(w), :])
        work[span(w), :] = hat * vecs[3:4, :] + vecs[4:5, :]
    low[...] = work[...].astype(BF16)


def feed(sizes, hid_bias, vecs, weights, middle, low, acc):
    acc[...] = middle[...] + vecs[5:6, :]

    def block(i, _):
        hidden = dot_nt(low[...], sizes.expand_part(weights, i)) + hid_bias[i]
        cdf, _ = normal_cdf(hidden)
        acc[...] += dot((hidden * cdf).astype(BF16), sizes.shrink_part(weights, i))
        return 0

    lax.fori_loop(0, sizes.shards, block, 0, unroll=4)


def column_sum(v):
    return jnp.sum(v, axis=0, keepdims=True)


def feed_both(sizes, hid_bias, vecs, weights, middle, low, glow, acc, back, dw, unit_sums):
    base, units = 4 * sizes.loc, sizes.units
    acc[...] = middle[...] + vecs[5:6, :]
    back[...] = jnp.zeros_like(back)

    def block(i, _):
        w_in, w_out = sizes.expand_part(weights, i), sizes.shrink_part(weights, i)
        hidden = dot_nt(low[...], w_in) + hid_bias[i]
        cdf, bell = normal_cdf(hidden)
        active = (hidden * cdf).astype(BF16)
        grad = (dot_nt(glow[...], w_out) * (cdf + hidden * bell * DENSITY))
        unit_sums[i] += column_sum(grad)
        grad = grad.astype(BF16)
        acc[...] += dot(active, w_out)
        back[...] += dot(grad, w_in)
        dw[i, :, base : base + units] += dot_tn(low[...], grad)
        dw[i, :, base + units : base + 2 * units] += dot_tn(glow[...], active)
        return 0

    lax.fori_loop(0, sizes.shards, block, 0, unroll=2)


def backward(sizes, vecs, weights, xs, work, low, qkv, mixed, middle, glow, back, gmid, gmix, dqkv, keep, dw, dbias, sums):
    width, groups = sizes.width, sizes.groups
    scale = HEAD ** (-0.5)
    for w in range(BATCH):
        hat, inv = normalize(middle[span(w), :])
        grad = back[span(w), :]
        sums[3:4, :] += column_sum(grad * hat)
        sums[4:5, :] += column_sum(grad)
        gmid[span(w), :] += norm_back(grad * vecs[3:4, :], hat, inv)
    branch = gmid[...].astype(BF16)
    sums[5:6, :] += column_sum(gmid[...])
    sizes.add_attention(dw, 3, dot_tn(branch, mixed[...].astype(BF16)))
    gmix[...] = dot_nt(branch, sizes.attention_part(weights, 3))

    def attend(w, _):
        row = span(w)
        for g in range(groups):
            col = g * LANES
            q = qkv[row, pl.ds(col, LANES)]
            k = qkv[row, pl.ds(width + col, LANES)]
            v = qkv[row, pl.ds(2 * width + col, LANES)]
            grad = gmix[row, pl.ds(col, LANES)]
            probs = keep[w * groups + g]
            wide_grad = dot(grad.astype(BF16), spread_columns(v))
            parts = []
            for h in range(PACK):
                p = probs[:, h * LANES : (h + 1) * LANES].astype(F32)
                t = wide_grad[:, h * LANES : (h + 1) * LANES]
                s = p * (t - jnp.sum(p * t, axis=-1, keepdims=True))
                dbias[g * PACK + h] += s
                parts.append(s)
            score = jnp.concatenate(parts, axis=1).astype(BF16)
            dqkv[row, pl.ds(col, LANES)] = dot(score, spread_rows(k)) * scale
            turned = pad_rows(q).T[:, :PAD].astype(BF16)
            dqkv[row, pl.ds(width + col, LANES)] = diagonal(dot(turned, score)).T[:PAD] * scale
            turned = pad_rows(grad).T[:, :PAD].astype(BF16)
            dqkv[row, pl.ds(2 * width + col, LANES)] = diagonal(dot(turned, probs)).T[:PAD]
        return 0

    lax.fori_loop(0, BATCH, attend, 0)
    for w in range(BATCH):
        hat, _ = normalize(xs[span(w), :])
        work[span(w), :] = hat * vecs[0:1, :] + vecs[1:2, :]
    low[...] = work[...].astype(BF16)
    back[...] = jnp.zeros_like(back)
    for c in range(3):
        at = slice(c * width, (c + 1) * width)
        grad = dqkv[:, at]
        if c != 1:
            sums[c // 2 : c // 2 + 1, :] += column_sum(grad)
        grad = grad.astype(BF16)
        back[...] += dot(grad, sizes.attention_part(weights, c))
        sizes.add_attention(dw, c, dot_tn(low[...], grad))
    for w in range(BATCH):
        hat, inv = normalize(xs[span(w), :])
        grad = back[span(w), :]
        sums[6:7, :] += column_sum(grad * hat)
        sums[7:8, :] += column_sum(grad)
        gmid[span(w), :] += norm_back(grad * vecs[0:1, :], hat, inv)


def live_scales(first, live):
    return [jnp.where(first + w < live[0], 1.0, 0.0).astype(F32) for w in range(BATCH)]


def forward_kernel(sizes, order, live, tok_ref, held, bias, vecs, wide_bias, hid_bias, weights, out_ref,
                   wide, xs, work, low, qkv, mixed, middle):
    @pl.when(pl.program_id(0) == 0)
    def _():
        xs[...] = jnp.zeros_like(xs)

    load_rows(tok_ref[...], wide, xs)
    attention(sizes, bias, vecs, wide_bias, weights, xs, work, low, qkv, mixed, middle, None)
    second_norm(vecs, middle, work, low)
    feed(sizes, hid_bias, vecs, weights, middle, low, work)
    store_rows(work, wide, out_ref, live_scales(order[pl.program_id(0)] * BATCH, live))


def own_kernel(sizes, order, live, tok_ref, cot_ref, bias, vecs, wide_bias, hid_bias, weights,
               out_ref, gtok_ref, dw_ref, dbias, sums, unit_sums,
               wide, xs, work, low, qkv, mixed, middle, glow, back, gmid, gmix, dqkv, keep, dw):
    @pl.when(pl.program_id(0) == 0)
    def _():
        xs[...] = jnp.zeros_like(xs)
        dw[...] = jnp.zeros_like(dw)
        dbias[...] = jnp.zeros_like(dbias)
        sums[...] = jnp.zeros_like(sums)
        unit_sums[...] = jnp.zeros_like(unit_sums)

    scales = live_scales(order[pl.program_id(0)] * BATCH, live)
    load_rows(tok_ref[...], wide, xs)
    attention(sizes, bias, vecs, wide_bias, weights, xs, work, low, qkv, mixed, middle, keep)
    second_norm(vecs, middle, work, low)
    wide[...] = cot_ref[...].astype(F32)
    for w in range(BATCH):
        gmid[w * PAD : w * PAD + AREA, :] = wide[w * AREA : (w + 1) * AREA, :] * scales[w]
        gmid[w * PAD + AREA : (w + 1) * PAD, :] = jnp.zeros((PAD - AREA, gmid.shape[1]), F32)
    sums[2:3, :] += column_sum(gmid[...])
    glow[...] = gmid[...].astype(BF16)
    feed_both(sizes, hid_bias, vecs, weights, middle, low, glow, work, back, dw, unit_sums)
    store_rows(work, wide, out_ref, scales)
    backward(sizes, vecs, weights, xs, work, low, qkv, mixed, middle, glow, back, gmid, gmix, dqkv, keep, dw, dbias, sums)
    store_rows(gmid, wide, gtok_ref)

    @pl.when(pl.program_id(0) == pl.num_programs(0) - 1)
    def _():
        def cast(z, _):
            dw_ref[z] = dw[z].astype(BF16)
            return 0

        lax.fori_loop(0, sizes.shards, cast, 0)


def whole_block(a):
    return pl.BlockSpec(a.shape, lambda *_: (0,) * len(a.shape), pipeline_mode=pl.Buffered(1))


def forward_scratch(sizes, d):
    return [
        pltpu.VMEM((CHUNK, d), F32),
        pltpu.VMEM((ROWS, d), F32),
        pltpu.VMEM((ROWS, d), F32),
        pltpu.VMEM((ROWS, d), BF16),
        pltpu.VMEM((ROWS, 3 * sizes.width), F32),
        pltpu.VMEM((ROWS, sizes.width), F32),
        pltpu.VMEM((ROWS, d), F32),
    ]


def run_forward(sizes, order, live, tokens, held, *params):
    d = tokens.shape[1]
    block = pl.BlockSpec((CHUNK, d), lambda i, order, live: (order[i], 0))
    return pl.pallas_call(
        functools.partial(forward_kernel, sizes),
        out_shape=jax.ShapeDtypeStruct(tokens.shape, BF16),
        grid_spec=pltpu.PrefetchScalarGridSpec(
            num_scalar_prefetch=2,
            grid=(order.shape[0],),
            in_specs=[block, pl.BlockSpec(memory_space=pl.ANY)] + [whole_block(a) for a in params],
            out_specs=block,
            scratch_shapes=forward_scratch(sizes, d),
        ),
        input_output_aliases={3: 0},
        compiler_params=pltpu.CompilerParams(vmem_limit_bytes=VMEM_LIMIT),
    )(order, live, tokens, held, *params)


def run_own(sizes, order, live, tokens, cotangent, *params):
    d = tokens.shape[1]
    chunks = order.shape[0]
    block = pl.BlockSpec((CHUNK, d), lambda i, order, live: (order[i], 0))
    outs = (
        jax.ShapeDtypeStruct(tokens.shape, BF16),
        jax.ShapeDtypeStruct((chunks * CHUNK, d), BF16),
        jax.ShapeDtypeStruct((sizes.shards, d, sizes.columns), BF16),
        jax.ShapeDtypeStruct(params[0].shape, F32),
        jax.ShapeDtypeStruct((8, d), F32),
        jax.ShapeDtypeStruct((sizes.shards, 1, sizes.units), F32),
    )
    return pl.pallas_call(
        functools.partial(own_kernel, sizes),
        out_shape=outs,
        grid_spec=pltpu.PrefetchScalarGridSpec(
            num_scalar_prefetch=2,
            grid=(chunks,),
            in_specs=[block, block] + [whole_block(a) for a in params],
            out_specs=[block, pl.BlockSpec((CHUNK, d), lambda i, *_: (i, 0))] + [whole_block(o) for o in outs[2:]],
            scratch_shapes=forward_scratch(sizes, d)
            + [
                pltpu.VMEM((ROWS, d), BF16),
                pltpu.VMEM((ROWS, d), F32),
                pltpu.VMEM((ROWS, d), F32),
                pltpu.VMEM((ROWS, sizes.width), F32),
                pltpu.VMEM((ROWS, 3 * sizes.width), F32),
                pltpu.VMEM((BATCH * sizes.groups, PAD, PACK * LANES), BF16),
                pltpu.VMEM((sizes.shards, d, sizes.columns), F32),
            ],
        ),
        compiler_params=pltpu.CompilerParams(vmem_limit_bytes=VMEM_LIMIT),
    )(order, live, tokens, cotangent, *params)


class Place:
    def __init__(self, mesh_shape):
        self.shards, self.n_dp = mesh_shape["mp"], mesh_shape["dp"]
        self.chips = self.n_dp // 2
        self.bits = int(math.log2(self.chips))
        self.dp, self.z = lax.axis_index("dp"), lax.axis_index("mp")
        self.core, self.chip = lax.rem(self.dp, 2), lax.div(self.dp, 2)

    def mate(self):
        return (self.dp + 1 - 2 * self.core, self.z)

    def flip(self, m):
        chip = self.chip
        for b in range(self.bits):
            if m >> b & 1:
                chip = chip + (1 << b) * (1 - 2 * lax.rem(lax.div(self.chip, 1 << b), 2))
        return chip

    def across(self, m):
        return (2 * self.flip(m) + self.core, self.z)

    def bit(self, b):
        return lax.rem(lax.div(self.chip, 1 << b), 2)

    def along(self, k):
        return (self.dp, lax.rem(self.z + k, self.shards))

    def greet(self, targets):
        barrier = pltpu.get_barrier_semaphore()
        for target in targets:
            pl.semaphore_signal(barrier, inc=1, device_id=target, device_id_type=MESH)
        pl.semaphore_wait(barrier, len(targets))

    def everyone(self):
        return (
            [self.mate()]
            + [self.across(m) for m in range(1, self.chips)]
            + [self.along(k) for k in range(1, self.shards)]
        )


def remote(source, target, sent, received, device):
    return pltpu.make_async_remote_copy(source, target, sent, received, device_id=device, device_id_type=MESH)


def gather_kernel(mesh_shape, shard, small, out, out_small, own_sem, z_sem, s_sem, p_sem, m_sem):
    here = Place(mesh_shape)
    rows = shard.shape[0] // here.n_dp

    def piece(dp):
        return pl.ds(pl.multiple_of(dp * rows, 16), rows)

    here.greet(here.everyone())
    keep = [
        pltpu.make_async_copy(shard, out.at[here.z], own_sem.at[0]),
        pltpu.make_async_copy(small, out_small.at[here.z], own_sem.at[1]),
    ]
    for copy in keep:
        copy.start()
    sends = []
    for k in range(1, here.shards):
        copy = remote(small, out_small.at[here.z], s_sem.at[0, k], s_sem.at[1, k], here.along(k))
        copy.start()
        sends.append(copy)
        copy = remote(
            shard.at[piece(here.dp)], out.at[here.z, piece(here.dp)], z_sem.at[0, k], z_sem.at[1, k], here.along(k)
        )
        copy.start()
        sends.append(copy)

    def from_shard(k):
        return lax.rem(here.z - k + here.shards, here.shards)

    def arrival(slot, k):
        block = out.at[from_shard(k), piece(here.dp)]
        return remote(block, block, slot.at[0], slot.at[1], here.mate())

    def spread(k):
        block = out.at[from_shard(k), piece(here.dp)]
        remote(block, block, z_sem.at[0, k], z_sem.at[1, k], here.along(k)).wait_recv()
        for m in range(1, here.chips):
            copy = remote(block, block, p_sem.at[0, k, m], p_sem.at[1, k, m], here.across(m))
            copy.start()
            sends.append(copy)
        copy = remote(block, block, m_sem.at[0, k, 0], m_sem.at[1, k, 0], here.mate())
        copy.start()
        sends.append(copy)

    def relay(k):
        for m in range(1, here.chips):
            block = out.at[from_shard(k), piece(2 * here.flip(m) + here.core)]
            remote(block, block, p_sem.at[0, k, m], p_sem.at[1, k, m], here.across(m)).wait_recv()
            copy = remote(block, block, m_sem.at[0, k, m], m_sem.at[1, k, m], here.mate())
            copy.start()
            sends.append(copy)

    order = sorted(range(1, here.shards), key=lambda k: min(k, here.shards - k))
    for k in order:
        spread(k)
    for k in order:
        relay(k)
    for k in order:
        for m in range(here.chips):
            block = out.at[from_shard(k), piece(2 * here.flip(m) + 1 - here.core)]
            remote(block, block, m_sem.at[0, k, m], m_sem.at[1, k, m], here.mate()).wait_recv()
        block = out_small.at[from_shard(k)]
        remote(block, block, s_sem.at[0, k], s_sem.at[1, k], here.along(k)).wait_recv()
    for copy in sends:
        copy.wait_send()
    for copy in keep:
        copy.wait()


def run_gather(mesh_shape, shard, small):
    shards, chips = mesh_shape["mp"], mesh_shape["dp"] // 2
    anywhere = pl.BlockSpec(memory_space=pl.ANY)
    dma = pltpu.SemaphoreType.DMA
    return pl.pallas_call(
        functools.partial(gather_kernel, mesh_shape),
        out_shape=(
            jax.ShapeDtypeStruct((shards, *shard.shape), shard.dtype),
            jax.ShapeDtypeStruct((shards, *small.shape), small.dtype),
        ),
        in_specs=[anywhere] * 2,
        out_specs=(anywhere, anywhere),
        scratch_shapes=[dma((2,)), dma((2, shards)), dma((2, shards)), dma((2, shards, chips)), dma((2, shards, chips))],
        compiler_params=pltpu.CompilerParams(collective_id=0, has_side_effects=True, vmem_limit_bytes=VMEM_LIMIT),
    )(shard, small)


def reduce_kernel(mesh_shape, gtok, dw, small, gout, final, small_out,
                  acc, half, part_a, part_b, last_a, last_b, sums, sums_in,
                  own_sem, line_sem, h_sem, q_sem, l_sem, f_sem, g_sem, t_sem):
    here = Place(mesh_shape)
    shards, chips, bits = here.shards, here.chips, here.bits
    d, columns = dw.shape[1], dw.shape[2]
    split = columns // 2
    side_a, side_b = pl.ds(0, split), pl.ds(split, split)
    sends = []

    def start(copy, when=None):
        sends.append((copy, when))
        if when is None:
            copy.start()
        else:
            pl.when(when)(copy.start)

    here.greet(here.everyone())

    block_rows = gtok.shape[0]

    def block(z):
        return gout.at[pl.ds(pl.multiple_of(z * block_rows, 16), block_rows)]

    own = pltpu.make_async_copy(gtok, block(here.z), own_sem.at[0])
    own.start()
    up, down = (here.dp, jnp.minimum(here.z + 1, shards - 1)), (here.dp, jnp.maximum(here.z - 1, 0))

    def line(step):
        for way, (target, sign) in enumerate(((up, 1), (down, -1))):
            held = here.z - sign * step
            inside = (held >= 0) & (held < shards)
            nxt = here.z + sign
            has_next = (nxt >= 0) & (nxt < shards)
            safe = jnp.clip(held, 0, shards - 1)
            if step > 0:
                arrived = remote(block(safe), block(safe), line_sem.at[0, way, step - 1], line_sem.at[1, way, step - 1], target)
                pl.when(inside)(arrived.wait_recv)
            if step < shards - 1:
                source = gtok if step == 0 else block(safe)
                copy = remote(source, block(safe), line_sem.at[0, way, step], line_sem.at[1, way, step], target)
                start(copy, inside & has_next)

    line(0)

    def rows_of(order, core, chip_bit, depth):
        size = d // 2
        first = core * size
        for b in order[:depth]:
            size //= 2
            first = first + chip_bit(b) * size
        return pl.ds(pl.multiple_of(first, 16), size)

    orders = (tuple(range(bits)), tuple(reversed(range(bits))))
    sides = (side_a, side_b)
    parts = (part_a, part_b)

    for s in range(shards):
        away = pl.ds(pl.multiple_of((1 - here.core) * (d // 2), 16), d // 2)
        start(remote(dw.at[s, away], half.at[s], h_sem.at[0, s], h_sem.at[1, s], here.mate()))

    sums[0] = small[...]
    stages = bits + 1

    def small_stage(i):
        target = here.mate() if i == 0 else here.across(1 << (i - 1))
        copy = remote(sums.at[i], sums_in.at[i], t_sem.at[0, i], t_sem.at[1, i], target)
        start(copy)

        def finish():
            copy.wait_recv()
            sums[i + 1] = sums[i] + sums_in[i]

        return finish

    small_finish = small_stage(0)

    def flipped(b):
        return lambda c: 1 - here.bit(c) if c == b else here.bit(c)

    def plane_send(s, depth):
        for side in range(2):
            b = orders[side][depth]
            rows = rows_of(orders[side], here.core, flipped(b), depth + 1)
            size = d >> (depth + 2)
            target = parts[side].at[depth, s, pl.ds(0, size)]
            start(remote(acc.at[s, rows, sides[side]], target, q_sem.at[0, side, depth, s], q_sem.at[1, side, depth, s], here.across(1 << b)))

    def plane_add(s, depth):
        for side in range(2):
            b = orders[side][depth]
            size = d >> (depth + 2)
            rows = rows_of(orders[side], here.core, here.bit, depth + 1)
            target = parts[side].at[depth, s, pl.ds(0, size)]
            remote(target, target, q_sem.at[0, side, depth, s], q_sem.at[1, side, depth, s], here.across(1 << b)).wait_recv()
            acc[s, rows, sides[side]] = (
                acc[s, rows, sides[side]].astype(F32) + parts[side][depth, s, pl.ds(0, size), :].astype(F32)
            ).astype(BF16)

    def half_add(s):
        mine = pl.ds(pl.multiple_of(here.core * (d // 2), 16), d // 2)
        remote(half.at[s], half.at[s], h_sem.at[0, s], h_sem.at[1, s], here.mate()).wait_recv()
        acc[s, mine, :] = (dw[s, mine, :].astype(F32) + half[s].astype(F32)).astype(BF16)

    lasts = (last_a, last_b)

    def mine_rows(side):
        return rows_of(orders[side], here.core, here.bit, bits)

    def shard_send(k):
        s = lax.rem(here.z + k, shards)
        for side in range(2):
            start(remote(acc.at[s, mine_rows(side), sides[side]], lasts[side].at[k], l_sem.at[0, side, k], l_sem.at[1, side, k], here.along(k)))

    for s in range(shards):
        half_add(s)
        plane_send(s, 0)
    small_finish()
    line(1)
    for depth in range(1, bits):
        small_finish = small_stage(depth)
        for s in range(shards):
            plane_add(s, depth - 1)
            plane_send(s, depth)
        small_finish()
        if depth + 1 < shards:
            line(depth + 1)
    small_finish = small_stage(bits)
    for s in range(shards):
        plane_add(s, bits - 1)
    small_finish()
    for k in range(1, shards):
        shard_send(k)
    for k in range(1, shards):
        start(remote(sums.at[stages], sums_in.at[stages + k - 1], t_sem.at[0, stages + k - 1], t_sem.at[1, stages + k - 1], here.along(k)))
    for step in range(bits + 1, shards):
        line(step)
    total = sums[stages]
    for k in range(1, shards):
        slot = stages + k - 1
        remote(sums.at[stages], sums_in.at[slot], t_sem.at[0, slot], t_sem.at[1, slot], here.along(k)).wait_recv()
        total = total + sums_in[slot]
    small_out[...] = total
    for side in range(2):
        rows = mine_rows(side)
        total = acc[here.z, rows, sides[side]].astype(F32)
        for k in range(1, shards):
            slot = lasts[side].at[k]
            remote(slot, slot, l_sem.at[0, side, k], l_sem.at[1, side, k], here.along(k)).wait_recv()
            total = total + lasts[side][k].astype(F32)
        final[rows, sides[side]] = total.astype(BF16)
    for side in range(2):
        for m in range(1, chips):
            rows = mine_rows(side)
            spot = final.at[rows, sides[side]]
            start(remote(spot, spot, f_sem.at[0, side, m], f_sem.at[1, side, m], here.across(m)))
        spot = final.at[mine_rows(side), sides[side]]
        start(remote(spot, spot, g_sem.at[0, side, 0], g_sem.at[1, side, 0], here.mate()))

    def theirs(side, m, core):
        return final.at[rows_of(orders[side], core, lambda b: 1 - here.bit(b) if m >> b & 1 else here.bit(b), bits), sides[side]]

    for side in range(2):
        for m in range(1, chips):
            spot = theirs(side, m, here.core)
            remote(spot, spot, f_sem.at[0, side, m], f_sem.at[1, side, m], here.across(m)).wait_recv()
            start(remote(spot, spot, g_sem.at[0, side, m], g_sem.at[1, side, m], here.mate()))
    for side in range(2):
        for m in range(chips):
            spot = theirs(side, m, 1 - here.core)
            remote(spot, spot, g_sem.at[0, side, m], g_sem.at[1, side, m], here.mate()).wait_recv()
    for copy, when in sends:
        if when is None:
            copy.wait_send()
        else:
            pl.when(when)(copy.wait_send)
    own.wait()


def run_reduce(mesh_shape, gtok, dw, small):
    shards, chips = mesh_shape["mp"], mesh_shape["dp"] // 2
    bits = int(math.log2(chips))
    anywhere = pl.BlockSpec(memory_space=pl.ANY)
    here = pl.BlockSpec(memory_space=pltpu.VMEM)
    dma = pltpu.SemaphoreType.DMA
    _, d, columns = dw.shape
    split = columns // 2
    finish = d // (2 * chips)
    return pl.pallas_call(
        functools.partial(reduce_kernel, mesh_shape),
        out_shape=(
            jax.ShapeDtypeStruct((shards * gtok.shape[0], d), gtok.dtype),
            jax.ShapeDtypeStruct((d, columns), BF16),
            jax.ShapeDtypeStruct(small.shape, F32),
        ),
        in_specs=[anywhere, here, here],
        out_specs=(anywhere, here, here),
        scratch_shapes=[
            pltpu.VMEM((shards, d, columns), BF16),
            pltpu.VMEM((shards, d // 2, columns), BF16),
            pltpu.VMEM((bits, shards, d // 4, split), BF16),
            pltpu.VMEM((bits, shards, d // 4, split), BF16),
            pltpu.VMEM((shards, finish, split), BF16),
            pltpu.VMEM((shards, finish, split), BF16),
            pltpu.VMEM((bits + 2, *small.shape), F32),
            pltpu.VMEM((bits + shards, *small.shape), F32),
            dma((1,)),
            dma((2, 2, shards)),
            dma((2, shards)),
            dma((2, 2, bits, shards)),
            dma((2, 2, shards)),
            dma((2, 2, chips)),
            dma((2, 2, chips)),
            dma((2, bits + shards)),
        ],
        compiler_params=pltpu.CompilerParams(collective_id=1, has_side_effects=True, vmem_limit_bytes=VMEM_LIMIT),
    )(gtok, dw, small)


def relative_bias(table, offset_index):
    onehot = (offset_index.reshape(1, AREA * AREA) == lax.broadcasted_iota(jnp.int32, (table.shape[1], 1), 0)).astype(BF16)
    values = jnp.dot(table.astype(BF16), onehot, preferred_element_type=F32) * LOG2E
    values = jnp.pad(values.reshape(-1, AREA, AREA), ((0, 0), (0, PAD - AREA), (0, 0)))
    return jnp.pad(values, ((0, 0), (0, 0), (0, LANES - AREA)), constant_values=-1e30)


def table_grad(scores, offset_index, table_rows):
    onehot = (offset_index.reshape(AREA * AREA, 1) == lax.broadcasted_iota(jnp.int32, (1, table_rows), 1)).astype(BF16)
    flat = scores[:, :AREA, :AREA].reshape(-1, AREA * AREA)
    return jnp.dot(flat.astype(BF16), onehot, preferred_element_type=F32)


def local(
    mesh_shape,
    tokens,
    cotangent,
    group_windows,
    offset_index,
    first_gain,
    first_shift,
    triple_weight,
    query_value_bias,
    bias_table,
    output_weight,
    output_bias,
    second_gain,
    second_shift,
    expand_weight,
    expand_bias,
    shrink_weight,
    shrink_bias,
):
    z = lax.axis_index("mp")
    shards = mesh_shape["mp"]
    d, _, loc = triple_weight.shape
    units = expand_weight.shape[1]
    table_rows, loc_heads = bias_table.shape
    sizes = Sizes(shards, loc, units)
    shard = jnp.concatenate(
        [triple_weight.transpose(1, 2, 0).reshape(3 * loc, d), output_weight, expand_weight.T, shrink_weight], axis=0
    )

    def widen(v):
        return jnp.pad(v, ((0, 0), (0, 512 - v.shape[1])))

    small = jnp.concatenate(
        [widen(expand_bias[None]), widen(query_value_bias.reshape(1, 2 * loc)), widen(bias_table.T)], axis=0
    ).astype(F32)
    small = jnp.pad(small, ((0, 8 - small.shape[0]), (0, 0)))
    weights, small = run_gather(mesh_shape, shard, small)
    hid_bias = small[:, 0:1, :units]
    pair = small[:, 1, : 2 * loc].reshape(shards, 2, loc)
    wide_bias = jnp.concatenate([pair[:, 0].reshape(1, -1), jnp.zeros((1, sizes.width), F32), pair[:, 1].reshape(1, -1)], axis=1)
    table = small[:, 2 : 2 + loc_heads, :table_rows].reshape(shards * loc_heads, table_rows)
    bias = relative_bias(table, offset_index)
    blank = jnp.zeros_like(first_gain)
    vecs = jnp.stack([first_gain, first_shift, output_bias, second_gain, second_shift, shrink_bias, blank, blank]).astype(F32)
    params = (bias, vecs, wide_bias, hid_bias, weights)
    chunks = tokens.shape[0] // CHUNK
    own = chunks // shards
    order = lax.rem(z * own + jnp.arange(chunks, dtype=jnp.int32), chunks)
    result, gtok, dw, dbias, sums, unit_sums = run_own(sizes, order[:own], group_windows, tokens, cotangent, *params)
    result = run_forward(sizes, order[own:], group_windows, tokens, result, *params)
    grads = table_grad(dbias, offset_index, table_rows)
    grads = jnp.pad(grads, ((0, 0), (0, 384 - table_rows)))
    packed = jnp.concatenate([sums, unit_sums.reshape(-1, d), grads.reshape(-1, d)], axis=0)
    grad_tokens, final, packed = run_reduce(mesh_shape, gtok, dw, packed)
    sums, rest = packed[:8], packed[8:]
    count = shards * units // d
    unit_total = lax.dynamic_slice_in_dim(rest[:count].reshape(-1), z * units, units)
    table_total = rest[count:].reshape(shards * loc_heads, 384)[:, :table_rows]
    table_total = lax.dynamic_slice_in_dim(table_total, z * loc_heads, loc_heads, 0).T
    pair_total = lax.dynamic_slice_in_dim(sums[0:2], z * loc, loc, 1)
    final = final.astype(F32)
    return (
        result,
        grad_tokens,
        sums[6],
        sums[7],
        final[:, : 3 * loc].reshape(d, 3, loc),
        pair_total,
        table_total,
        final[:, 3 * loc : 4 * loc].T,
        sums[5],
        sums[3],
        sums[4],
        final[:, 4 * loc : 4 * loc + units],
        unit_total,
        final[:, 4 * loc + units :].T,
        sums[2],
    )


def solution(mesh):
    in_specs = (
        P("dp", None),
        P("dp", None),
        P("dp"),
        P(),
        P(),
        P(),
        P(None, None, "mp"),
        P(None, "mp"),
        P(None, "mp"),
        P("mp", None),
        P(),
        P(),
        P(),
        P(None, "mp"),
        P("mp"),
        P("mp", None),
        P(),
    )
    out_specs = (
        P("dp", None),
        P("dp", None),
        P(),
        P(),
        P(None, None, "mp"),
        P(None, "mp"),
        P(None, "mp"),
        P("mp", None),
        P(),
        P(),
        P(),
        P(None, "mp"),
        P("mp"),
        P("mp", None),
        P(),
    )
    step = functools.partial(local, dict(mesh.shape))
    return jax.shard_map(step, mesh=mesh, in_specs=in_specs, out_specs=out_specs, check_vma=False)
```

```python
import functools
import math
import jax
import jax.numpy as jnp
from jax import lax
from jax.experimental import pallas as pl
from jax.experimental.pallas import tpu as pltpu
from jax.sharding import PartitionSpec as P

AREA = 100
PAD = 104
HEAD = 32
LANES = 128
PACK = LANES // HEAD
BATCH = 4
CHUNK = BATCH * AREA
ROWS = BATCH * PAD
EPSILON = 1e-05
DENSITY = 0.3989422804014327
LOG2E = 1.4426950408889634
F32 = jnp.float32
BF16 = jnp.bfloat16
MESH = pl.DeviceIdType.MESH
VMEM_LIMIT = 60 * 2**20


def dot(a, b):
    return jnp.dot(a, b, preferred_element_type=F32)


def dot_nt(a, b):
    return lax.dot_general(a, b, (((1,), (1,)), ((), ())), preferred_element_type=F32)


def dot_tn(a, b):
    return lax.dot_general(a, b, (((0,), (0,)), ((), ())), preferred_element_type=F32)


def normalize(values):
    centered = values - jnp.mean(values, axis=-1, keepdims=True)
    inv = lax.rsqrt(jnp.mean(centered * centered, axis=-1, keepdims=True) + EPSILON)
    return centered * inv, inv


def norm_back(grad, hat, inv):
    return inv * (
        grad
        - jnp.mean(grad, axis=-1, keepdims=True)
        - hat * jnp.mean(grad * hat, axis=-1, keepdims=True)
    )


def normal_cdf(hidden):
    z = jnp.abs(hidden) * 0.7071067811865476
    t = 1.0 / (1.0 + 0.3275911 * z)
    poly = t * (
        0.127414796 + t * (-0.142248368 + t * (0.7107068705 + t * (-0.7265760135 + t * 0.5307027145)))
    )
    bell = jnp.exp2(hidden * hidden * (-0.5 * LOG2E))
    tail = poly * bell
    return jnp.where(hidden > 0.0, 1.0 - tail, tail), bell


def head_of(shape, axis):
    return lax.broadcasted_iota(jnp.int32, shape, axis) // HEAD


def pad_rows(v):
    return jnp.concatenate([v, jnp.zeros((LANES - PAD, v.shape[1]), v.dtype)], axis=0)


def spread_rows(v):
    head = head_of((LANES, LANES), 1)
    full = pad_rows(v)
    return jnp.concatenate([jnp.where(head == h, full, 0.0) for h in range(PACK)], axis=0).astype(BF16)


def spread_columns(v):
    head = head_of((LANES, LANES), 0)
    turned = pad_rows(v).T
    return jnp.concatenate([jnp.where(head == h, turned, 0.0) for h in range(PACK)], axis=1).astype(BF16)


def diagonal(full):
    head = head_of((LANES, LANES), 0)
    out = full[:, 0:LANES]
    for h in range(1, PACK):
        out = jnp.where(head == h, full[:, h * LANES : (h + 1) * LANES], out)
    return out


def span(w, size=PAD):
    return pl.ds(pl.multiple_of(w * PAD, 8), size)


def load_rows(source, wide, padded):
    wide[...] = source.astype(F32)
    for w in range(BATCH):
        padded[w * PAD : w * PAD + AREA, :] = wide[w * AREA : (w + 1) * AREA, :]


def store_rows(padded, wide, target, scales=None):
    for w in range(BATCH):
        rows = padded[w * PAD : w * PAD + AREA, :]
        wide[w * AREA : (w + 1) * AREA, :] = rows if scales is None else rows * scales[w]
    target[...] = wide[...].astype(BF16)


class Sizes:
    def __init__(self, shards, loc, units):
        self.shards, self.loc, self.units = shards, loc, units
        self.width = shards * loc
        self.groups = self.width // LANES
        self.columns = 4 * loc + 2 * units

    def attention_part(self, weights, c):
        at = slice(c * self.loc, (c + 1) * self.loc)
        return jnp.concatenate([weights[z, at, :] for z in range(self.shards)], axis=0)

    def expand_part(self, weights, i):
        return weights[i, pl.ds(4 * self.loc, self.units), :]

    def shrink_part(self, weights, i):
        return weights[i, pl.ds(4 * self.loc + self.units, self.units), :]

    def add_attention(self, dw, c, value):
        for z in range(self.shards):
            at = slice(c * self.loc, (c + 1) * self.loc)
            dw[z, :, at] += value[:, z * self.loc : (z + 1) * self.loc]


def attention(sizes, bias, vecs, wide_bias, weights, xs, work, low, qkv, mixed, middle, keep):
    width, groups = sizes.width, sizes.groups
    scale = HEAD ** (-0.5) * LOG2E
    for w in range(BATCH):
        hat, _ = normalize(xs[span(w), :])
        work[span(w), :] = hat * vecs[0:1, :] + vecs[1:2, :]
    low[...] = work[...].astype(BF16)
    for c in range(3):
        at = slice(c * width, (c + 1) * width)
        qkv[:, at] = dot_nt(low[...], sizes.attention_part(weights, c)) + wide_bias[:, at]

    def attend(w, _):
        row = span(w)
        for g in range(groups):
            col = g * LANES
            q = qkv[row, pl.ds(col, LANES)].astype(BF16)
            k = qkv[row, pl.ds(width + col, LANES)]
            v = qkv[row, pl.ds(2 * width + col, LANES)]
            scores = dot(q, spread_columns(k))
            parts = []
            for h in range(PACK):
                s = scores[:, h * LANES : (h + 1) * LANES] * scale + bias[g * PACK + h]
                e = jnp.exp2(s - jnp.max(s, axis=-1, keepdims=True))
                parts.append(e * (1.0 / jnp.sum(e, axis=-1, keepdims=True)))
            probs = jnp.concatenate(parts, axis=1).astype(BF16)
            if keep is not None:
                keep[w * groups + g] = probs
            mixed[row, pl.ds(col, LANES)] = dot(probs, spread_rows(v))
        return 0

    lax.fori_loop(0, BATCH, attend, 0)
    middle[...] = xs[...] + dot(mixed[...].astype(BF16), sizes.attention_part(weights, 3)) + vecs[2:3, :]


def second_norm(vecs, middle, work, low):
    for w in range(BATCH):
        hat, _ = normalize(middle[span(w), :])
        work[span(w), :] = hat * vecs[3:4, :] + vecs[4:5, :]
    low[...] = work[...].astype(BF16)


def feed(sizes, hid_bias, vecs, weights, middle, low, acc):
    acc[...] = middle[...] + vecs[5:6, :]

    def block(i, _):
        hidden = dot_nt(low[...], sizes.expand_part(weights, i)) + hid_bias[i]
        cdf, _ = normal_cdf(hidden)
        acc[...] += dot((hidden * cdf).astype(BF16), sizes.shrink_part(weights, i))
        return 0

    lax.fori_loop(0, sizes.shards, block, 0, unroll=4)


def column_sum(v):
    return jnp.sum(v, axis=0, keepdims=True)


def feed_both(sizes, hid_bias, vecs, weights, middle, low, glow, acc, back, dw, unit_sums):
    base, units = 4 * sizes.loc, sizes.units
    acc[...] = middle[...] + vecs[5:6, :]
    back[...] = jnp.zeros_like(back)

    def block(i, _):
        w_in, w_out = sizes.expand_part(weights, i), sizes.shrink_part(weights, i)
        hidden = dot_nt(low[...], w_in) + hid_bias[i]
        cdf, bell = normal_cdf(hidden)
        active = (hidden * cdf).astype(BF16)
        grad = (dot_nt(glow[...], w_out) * (cdf + hidden * bell * DENSITY))
        unit_sums[i] += column_sum(grad)
        grad = grad.astype(BF16)
        acc[...] += dot(active, w_out)
        back[...] += dot(grad, w_in)
        dw[i, :, base : base + units] += dot_tn(low[...], grad)
        dw[i, :, base + units : base + 2 * units] += dot_tn(glow[...], active)
        return 0

    lax.fori_loop(0, sizes.shards, block, 0, unroll=2)


def backward(sizes, vecs, weights, xs, work, low, qkv, mixed, middle, glow, back, gmid, gmix, dqkv, keep, dw, dbias, sums):
    width, groups = sizes.width, sizes.groups
    scale = HEAD ** (-0.5)
    for w in range(BATCH):
        hat, inv = normalize(middle[span(w), :])
        grad = back[span(w), :]
        sums[3:4, :] += column_sum(grad * hat)
        sums[4:5, :] += column_sum(grad)
        gmid[span(w), :] += norm_back(grad * vecs[3:4, :], hat, inv)
    branch = gmid[...].astype(BF16)
    sums[5:6, :] += column_sum(gmid[...])
    sizes.add_attention(dw, 3, dot_tn(branch, mixed[...].astype(BF16)))
    gmix[...] = dot_nt(branch, sizes.attention_part(weights, 3))

    def attend(w, _):
        row = span(w)
        for g in range(groups):
            col = g * LANES
            q = qkv[row, pl.ds(col, LANES)]
            k = qkv[row, pl.ds(width + col, LANES)]
            v = qkv[row, pl.ds(2 * width + col, LANES)]
            grad = gmix[row, pl.ds(col, LANES)]
            probs = keep[w * groups + g]
            wide_grad = dot(grad.astype(BF16), spread_columns(v))
            parts = []
            for h in range(PACK):
                p = probs[:, h * LANES : (h + 1) * LANES].astype(F32)
                t = wide_grad[:, h * LANES : (h + 1) * LANES]
                s = p * (t - jnp.sum(p * t, axis=-1, keepdims=True))
                dbias[g * PACK + h] += s
                parts.append(s)
            score = jnp.concatenate(parts, axis=1).astype(BF16)
            dqkv[row, pl.ds(col, LANES)] = dot(score, spread_rows(k)) * scale
            turned = pad_rows(q).T[:, :PAD].astype(BF16)
            dqkv[row, pl.ds(width + col, LANES)] = diagonal(dot(turned, score)).T[:PAD] * scale
            turned = pad_rows(grad).T[:, :PAD].astype(BF16)
            dqkv[row, pl.ds(2 * width + col, LANES)] = diagonal(dot(turned, probs)).T[:PAD]
        return 0

    lax.fori_loop(0, BATCH, attend, 0)
    for w in range(BATCH):
        hat, _ = normalize(xs[span(w), :])
        work[span(w), :] = hat * vecs[0:1, :] + vecs[1:2, :]
    low[...] = work[...].astype(BF16)
    back[...] = jnp.zeros_like(back)
    for c in range(3):
        at = slice(c * width, (c + 1) * width)
        grad = dqkv[:, at]
        if c != 1:
            sums[c // 2 : c // 2 + 1, :] += column_sum(grad)
        grad = grad.astype(BF16)
        back[...] += dot(grad, sizes.attention_part(weights, c))
        sizes.add_attention(dw, c, dot_tn(low[...], grad))
    for w in range(BATCH):
        hat, inv = normalize(xs[span(w), :])
        grad = back[span(w), :]
        sums[6:7, :] += column_sum(grad * hat)
        sums[7:8, :] += column_sum(grad)
        gmid[span(w), :] += norm_back(grad * vecs[0:1, :], hat, inv)


def live_scales(first, live):
    return [jnp.where(first + w < live[0], 1.0, 0.0).astype(F32) for w in range(BATCH)]


def own_kernel(sizes, order, live, tok_ref, cot_ref, bias, vecs, wide_bias, hid_bias, weights,
               out_ref, gtok_ref, dw_ref, dbias, sums, unit_sums,
               wide, xs, work, low, qkv, mixed, middle, glow, back, gmid, gmix, dqkv, keep, dw):
    @pl.when(pl.program_id(0) == 0)
    def _():
        xs[...] = jnp.zeros_like(xs)
        dw[...] = jnp.zeros_like(dw)
        dbias[...] = jnp.zeros_like(dbias)
        sums[...] = jnp.zeros_like(sums)
        unit_sums[...] = jnp.zeros_like(unit_sums)

    scales = live_scales(order[pl.program_id(0)] * BATCH, live)
    load_rows(tok_ref[...], wide, xs)
    attention(sizes, bias, vecs, wide_bias, weights, xs, work, low, qkv, mixed, middle, keep)
    second_norm(vecs, middle, work, low)
    wide[...] = cot_ref[...].astype(F32)
    for w in range(BATCH):
        gmid[w * PAD : w * PAD + AREA, :] = wide[w * AREA : (w + 1) * AREA, :] * scales[w]
        gmid[w * PAD + AREA : (w + 1) * PAD, :] = jnp.zeros((PAD - AREA, gmid.shape[1]), F32)
    sums[2:3, :] += column_sum(gmid[...])
    glow[...] = gmid[...].astype(BF16)
    feed_both(sizes, hid_bias, vecs, weights, middle, low, glow, work, back, dw, unit_sums)
    store_rows(work, wide, out_ref, scales)
    backward(sizes, vecs, weights, xs, work, low, qkv, mixed, middle, glow, back, gmid, gmix, dqkv, keep, dw, dbias, sums)
    store_rows(gmid, wide, gtok_ref)

    @pl.when(pl.program_id(0) == pl.num_programs(0) - 1)
    def _():
        def cast(z, _):
            dw_ref[z] = dw[z].astype(BF16)
            return 0

        lax.fori_loop(0, sizes.shards, cast, 0)


def whole_block(a):
    return pl.BlockSpec(a.shape, lambda *_: (0,) * len(a.shape), pipeline_mode=pl.Buffered(1))


def forward_scratch(sizes, d):
    return [
        pltpu.VMEM((CHUNK, d), F32),
        pltpu.VMEM((ROWS, d), F32),
        pltpu.VMEM((ROWS, d), F32),
        pltpu.VMEM((ROWS, d), BF16),
        pltpu.VMEM((ROWS, 3 * sizes.width), F32),
        pltpu.VMEM((ROWS, sizes.width), F32),
        pltpu.VMEM((ROWS, d), F32),
    ]


def run_own(sizes, order, live, tokens, cotangent, *params):
    d = tokens.shape[1]
    chunks = order.shape[0]
    block = pl.BlockSpec((CHUNK, d), lambda i, order, live: (order[i], 0))
    outs = (
        jax.ShapeDtypeStruct(tokens.shape, BF16),
        jax.ShapeDtypeStruct((chunks * CHUNK, d), BF16),
        jax.ShapeDtypeStruct((sizes.shards, d, sizes.columns), BF16),
        jax.ShapeDtypeStruct(params[0].shape, F32),
        jax.ShapeDtypeStruct((8, d), F32),
        jax.ShapeDtypeStruct((sizes.shards, 1, sizes.units), F32),
    )
    return pl.pallas_call(
        functools.partial(own_kernel, sizes),
        out_shape=outs,
        grid_spec=pltpu.PrefetchScalarGridSpec(
            num_scalar_prefetch=2,
            grid=(chunks,),
            in_specs=[block, block] + [whole_block(a) for a in params],
            out_specs=[block, pl.BlockSpec((CHUNK, d), lambda i, *_: (i, 0))] + [whole_block(o) for o in outs[2:]],
            scratch_shapes=forward_scratch(sizes, d)
            + [
                pltpu.VMEM((ROWS, d), BF16),
                pltpu.VMEM((ROWS, d), F32),
                pltpu.VMEM((ROWS, d), F32),
                pltpu.VMEM((ROWS, sizes.width), F32),
                pltpu.VMEM((ROWS, 3 * sizes.width), F32),
                pltpu.VMEM((BATCH * sizes.groups, PAD, PACK * LANES), BF16),
                pltpu.VMEM((sizes.shards, d, sizes.columns), F32),
            ],
        ),
        compiler_params=pltpu.CompilerParams(vmem_limit_bytes=VMEM_LIMIT),
    )(order, live, tokens, cotangent, *params)


class Place:
    def __init__(self, mesh_shape):
        self.shards, self.n_dp = mesh_shape["mp"], mesh_shape["dp"]
        self.chips = self.n_dp // 2
        self.bits = int(math.log2(self.chips))
        self.dp, self.z = lax.axis_index("dp"), lax.axis_index("mp")
        self.core, self.chip = lax.rem(self.dp, 2), lax.div(self.dp, 2)

    def mate(self):
        return (self.dp + 1 - 2 * self.core, self.z)

    def flip(self, m):
        chip = self.chip
        for b in range(self.bits):
            if m >> b & 1:
                chip = chip + (1 << b) * (1 - 2 * lax.rem(lax.div(self.chip, 1 << b), 2))
        return chip

    def across(self, m):
        return (2 * self.flip(m) + self.core, self.z)

    def bit(self, b):
        return lax.rem(lax.div(self.chip, 1 << b), 2)

    def along(self, k):
        return (self.dp, lax.rem(self.z + k, self.shards))

    def greet(self, targets):
        barrier = pltpu.get_barrier_semaphore()
        for target in targets:
            pl.semaphore_signal(barrier, inc=1, device_id=target, device_id_type=MESH)
        pl.semaphore_wait(barrier, len(targets))

    def everyone(self):
        return (
            [self.mate()]
            + [self.across(m) for m in range(1, self.chips)]
            + [self.along(k) for k in range(1, self.shards)]
        )


def remote(source, target, sent, received, device):
    return pltpu.make_async_remote_copy(source, target, sent, received, device_id=device, device_id_type=MESH)


def gather_kernel(mesh_shape, shard, small, out, out_small, own_sem, z_sem, s_sem, p_sem, m_sem):
    here = Place(mesh_shape)
    rows = shard.shape[0] // here.n_dp

    def piece(dp):
        return pl.ds(pl.multiple_of(dp * rows, 16), rows)

    here.greet(here.everyone())
    keep = [
        pltpu.make_async_copy(shard, out.at[here.z], own_sem.at[0]),
        pltpu.make_async_copy(small, out_small.at[here.z], own_sem.at[1]),
    ]
    for copy in keep:
        copy.start()
    sends = []
    for k in range(1, here.shards):
        copy = remote(small, out_small.at[here.z], s_sem.at[0, k], s_sem.at[1, k], here.along(k))
        copy.start()
        sends.append(copy)
        copy = remote(
            shard.at[piece(here.dp)], out.at[here.z, piece(here.dp)], z_sem.at[0, k], z_sem.at[1, k], here.along(k)
        )
        copy.start()
        sends.append(copy)

    def from_shard(k):
        return lax.rem(here.z - k + here.shards, here.shards)

    def arrival(slot, k):
        block = out.at[from_shard(k), piece(here.dp)]
        return remote(block, block, slot.at[0], slot.at[1], here.mate())

    def spread(k):
        block = out.at[from_shard(k), piece(here.dp)]
        remote(block, block, z_sem.at[0, k], z_sem.at[1, k], here.along(k)).wait_recv()
        for m in range(1, here.chips):
            copy = remote(block, block, p_sem.at[0, k, m], p_sem.at[1, k, m], here.across(m))
            copy.start()
            sends.append(copy)
        copy = remote(block, block, m_sem.at[0, k, 0], m_sem.at[1, k, 0], here.mate())
        copy.start()
        sends.append(copy)

    def relay(k):
        for m in range(1, here.chips):
            block = out.at[from_shard(k), piece(2 * here.flip(m) + here.core)]
            remote(block, block, p_sem.at[0, k, m], p_sem.at[1, k, m], here.across(m)).wait_recv()
            copy = remote(block, block, m_sem.at[0, k, m], m_sem.at[1, k, m], here.mate())
            copy.start()
            sends.append(copy)

    order = sorted(range(1, here.shards), key=lambda k: min(k, here.shards - k))
    for k in order:
        spread(k)
    for k in order:
        relay(k)
    for k in order:
        for m in range(here.chips):
            block = out.at[from_shard(k), piece(2 * here.flip(m) + 1 - here.core)]
            remote(block, block, m_sem.at[0, k, m], m_sem.at[1, k, m], here.mate()).wait_recv()
        block = out_small.at[from_shard(k)]
        remote(block, block, s_sem.at[0, k], s_sem.at[1, k], here.along(k)).wait_recv()
    for copy in sends:
        copy.wait_send()
    for copy in keep:
        copy.wait()


def run_gather(mesh_shape, shard, small):
    shards, chips = mesh_shape["mp"], mesh_shape["dp"] // 2
    anywhere = pl.BlockSpec(memory_space=pl.ANY)
    dma = pltpu.SemaphoreType.DMA
    return pl.pallas_call(
        functools.partial(gather_kernel, mesh_shape),
        out_shape=(
            jax.ShapeDtypeStruct((shards, *shard.shape), shard.dtype),
            jax.ShapeDtypeStruct((shards, *small.shape), small.dtype),
        ),
        in_specs=[anywhere] * 2,
        out_specs=(anywhere, anywhere),
        scratch_shapes=[dma((2,)), dma((2, shards)), dma((2, shards)), dma((2, shards, chips)), dma((2, shards, chips))],
        compiler_params=pltpu.CompilerParams(collective_id=0, has_side_effects=True, vmem_limit_bytes=VMEM_LIMIT),
    )(shard, small)


class Reduction:
    def __init__(self, mesh_shape, gtok, gout, dw, final, small_out, scratch):
        (self.acc, self.half, self.parts, self.lasts, self.sums, self.sums_in,
         self.own_sem, self.line_sem, self.h_sem, self.q_sem, self.l_sem, self.f_sem, self.g_sem, self.t_sem) = scratch
        self.gtok, self.gout, self.dw, self.final, self.small_out = gtok, gout, dw, final, small_out
        self.here = Place(mesh_shape)
        self.d, self.columns = dw.shape[1], dw.shape[2]
        split = self.columns // 2
        self.sides = (pl.ds(0, split), pl.ds(split, split))
        bits = self.here.bits
        self.orders = (tuple(range(bits)), tuple(reversed(range(bits))))
        self.stages = bits + 1
        self.sent = []

    def send(self, make, when=None):
        self.sent.append((make, when))
        if when is None:
            make().start()
        else:
            pl.when(when())(lambda: make().start())

    def finish_sends(self):
        for make, when in self.sent:
            if when is None:
                make().wait_send()
            else:
                pl.when(when())(lambda make=make: make().wait_send())


    def block(self, z):
        rows = self.gtok.shape[0]
        return self.gout.at[pl.ds(pl.multiple_of(z * rows, 16), rows)]

    def own_copy(self):
        return pltpu.make_async_copy(self.gtok, self.block(self.here.z), self.own_sem.at[0])

    def line_copy(self, way, step, arriving=False):
        here, sign = self.here, 1 - 2 * way
        held = jnp.clip(here.z - sign * step, 0, here.shards - 1)
        at = step - 1 if arriving else step
        source = self.gtok if at == 0 and not arriving else self.block(held)
        target = (here.dp, jnp.clip(here.z + sign, 0, here.shards - 1))
        return remote(source, self.block(held), self.line_sem.at[0, way, at], self.line_sem.at[1, way, at], target)

    def line(self, step):
        here = self.here
        for way in range(2):
            sign = 1 - 2 * way

            def inside(sign=sign):
                held = here.z - sign * step
                return (held >= 0) & (held < here.shards)

            def onward(sign=sign):
                return (here.z + sign >= 0) & (here.z + sign < here.shards)

            if step > 0:
                pl.when(inside())(lambda way=way: self.line_copy(way, step, True).wait_recv())
            if step < here.shards - 1:
                self.send(
                    functools.partial(self.line_copy, way, step),
                    lambda inside=inside, onward=onward: inside() & onward(),
                )


    def rows_of(self, side, core, chip_bit, depth):
        size = self.d // 2
        first = core * size
        for b in self.orders[side][:depth]:
            size //= 2
            first = first + chip_bit(b) * size
        return pl.ds(pl.multiple_of(first, 16), size)

    def half_rows(self, core):
        return pl.ds(pl.multiple_of(core * (self.d // 2), 16), self.d // 2)

    def half_copy(self, s):
        rows = self.half_rows(1 - self.here.core)
        return remote(self.dw.at[s, rows], self.half.at[s], self.h_sem.at[0, s], self.h_sem.at[1, s], self.here.mate())

    def half_send(self, s):
        self.send(functools.partial(self.half_copy, s))

    def half_add(self, s):
        self.half_copy(s).wait_recv()
        mine = self.half_rows(self.here.core)
        self.acc[s, mine, :] = (self.dw[s, mine, :].astype(F32) + self.half[s].astype(F32)).astype(BF16)

    def plane_copy(self, s, depth, side):
        here = self.here
        b = self.orders[side][depth]
        rows = self.rows_of(side, here.core, lambda c: 1 - here.bit(c) if c == b else here.bit(c), depth + 1)
        target = self.parts[side].at[depth, s, pl.ds(0, self.d >> (depth + 2))]
        sems = self.q_sem
        return remote(
            self.acc.at[s, rows, self.sides[side]], target, sems.at[0, side, depth, s], sems.at[1, side, depth, s], here.across(1 << b)
        )

    def plane_send(self, s, depth):
        for side in range(2):
            self.send(functools.partial(self.plane_copy, s, depth, side))

    def plane_add(self, s, depth):
        for side in range(2):
            self.plane_copy(s, depth, side).wait_recv()
            rows = self.rows_of(side, self.here.core, self.here.bit, depth + 1)
            arrived = self.parts[side][depth, s, pl.ds(0, self.d >> (depth + 2)), :]
            here = self.acc[s, rows, self.sides[side]]
            self.acc[s, rows, self.sides[side]] = (here.astype(F32) + arrived.astype(F32)).astype(BF16)

    def mine(self, side):
        return self.rows_of(side, self.here.core, self.here.bit, self.here.bits)

    def shard_copy(self, side, k):
        here = self.here
        s = lax.rem(here.z + k, here.shards)
        return remote(
            self.acc.at[s, self.mine(side), self.sides[side]], self.lasts[side].at[k], self.l_sem.at[0, side, k], self.l_sem.at[1, side, k], here.along(k)
        )

    def shard_sends(self):
        for k in range(1, self.here.shards):
            for side in range(2):
                self.send(functools.partial(self.shard_copy, side, k))

    def shard_adds(self):
        for side in range(2):
            rows = self.mine(side)
            total = self.acc[self.here.z, rows, self.sides[side]].astype(F32)
            for k in range(1, self.here.shards):
                self.shard_copy(side, k).wait_recv()
                total = total + self.lasts[side][k].astype(F32)
            self.final[rows, self.sides[side]] = total.astype(BF16)

    def final_spot(self, side, m, core):
        here = self.here
        rows = self.rows_of(side, core, lambda b: 1 - here.bit(b) if m >> b & 1 else here.bit(b), here.bits)
        return self.final.at[rows, self.sides[side]]

    def final_copy(self, side, m, arriving=False):
        here = self.here
        spot = self.final_spot(side, m if arriving else 0, here.core)
        return remote(spot, spot, self.f_sem.at[0, side, m], self.f_sem.at[1, side, m], here.across(m))

    def final_relay(self, side, m, arriving=False):
        here = self.here
        spot = self.final_spot(side, m, 1 - here.core if arriving else here.core)
        return remote(spot, spot, self.g_sem.at[0, side, m], self.g_sem.at[1, side, m], here.mate())

    def final_spread(self):
        chips = self.here.chips
        for side in range(2):
            for m in range(1, chips):
                self.send(functools.partial(self.final_copy, side, m))
            self.send(functools.partial(self.final_relay, side, 0))
        for side in range(2):
            for m in range(1, chips):
                self.final_copy(side, m, True).wait_recv()
                self.send(functools.partial(self.final_relay, side, m))
        for side in range(2):
            for m in range(chips):
                self.final_relay(side, m, True).wait_recv()


    def small_copy(self, i):
        here = self.here
        target = here.mate() if i == 0 else here.across(1 << (i - 1))
        return remote(self.sums.at[i], self.sums_in.at[i], self.t_sem.at[0, i], self.t_sem.at[1, i], target)

    def small_send(self, i):
        self.send(functools.partial(self.small_copy, i))

    def small_add(self, i):
        self.small_copy(i).wait_recv()
        self.sums[i + 1] = self.sums[i] + self.sums_in[i]

    def small_along(self, k):
        slot = self.stages + k - 1
        return remote(
            self.sums.at[self.stages], self.sums_in.at[slot], self.t_sem.at[0, slot], self.t_sem.at[1, slot], self.here.along(k)
        )

    def small_sends(self):
        for k in range(1, self.here.shards):
            self.send(functools.partial(self.small_along, k))

    def small_total(self):
        total = self.sums[self.stages]
        for k in range(1, self.here.shards):
            self.small_along(k).wait_recv()
            total = total + self.sums_in[self.stages + k - 1]
        self.small_out[...] = total

    def steps(self):
        here = self.here
        shards, bits = here.shards, here.bits
        steps = []

        def first():
            self.small_add(0)
            self.small_send(1)
            for s in range(shards):
                self.half_add(s)
                self.plane_send(s, 0)

        steps.append(first)
        for depth in range(1, bits):

            def middle(depth=depth):
                self.small_add(depth)
                self.small_send(depth + 1)
                for s in range(shards):
                    self.plane_add(s, depth - 1)
                    self.plane_send(s, depth)

            steps.append(middle)

        def last():
            self.small_add(bits)
            self.small_sends()
            for s in range(shards):
                self.plane_add(s, bits - 1)
            self.shard_sends()

        steps.append(last)
        return steps

    def start(self):
        self.own_copy().start()
        self.line(0)
        self.small_send(0)
        for s in range(self.here.shards):
            self.half_send(s)

    def end(self):
        self.small_total()
        self.shard_adds()
        self.final_spread()
        self.finish_sends()
        self.own_copy().wait()


def reduce_scratch(mesh_shape, d, columns, small_shape):
    shards, chips = mesh_shape["mp"], mesh_shape["dp"] // 2
    bits = int(math.log2(chips))
    split, finish = columns // 2, d // (2 * chips)
    dma = pltpu.SemaphoreType.DMA
    return [
        pltpu.VMEM((shards, d, columns), BF16),
        pltpu.VMEM((shards, d // 2, columns), BF16),
        [pltpu.VMEM((bits, shards, d // 4, split), BF16)] * 2,
        [pltpu.VMEM((shards, finish, split), BF16)] * 2,
        pltpu.VMEM((bits + 2, *small_shape), F32),
        pltpu.VMEM((bits + shards, *small_shape), F32),
        dma((1,)),
        dma((2, 2, shards)),
        dma((2, shards)),
        dma((2, 2, bits, shards)),
        dma((2, 2, shards)),
        dma((2, 2, chips)),
        dma((2, 2, chips)),
        dma((2, bits + shards)),
    ]


def rest_kernel(sizes, mesh_shape, live, tokens, held, bias, vecs, wide_bias, hid_bias, weights, gtok, dw, small,
                result, gout, final, small_out, rows_in, rows_out, in_sem, out_sem, forward, reduction):
    wide, xs, work, low, qkv, mixed, middle = forward
    here = Place(mesh_shape)
    red = Reduction(mesh_shape, gtok, gout, dw, final, small_out, reduction)
    own = gtok.shape[0] // CHUNK
    chunks = sizes.shards * own
    extra = chunks - own
    here.greet(here.everyone())

    def chunk_of(i):
        return lax.rem((here.z + 1) * own + i, chunks)

    def rows(i):
        return pl.ds(pl.multiple_of(chunk_of(i) * CHUNK, 16), CHUNK)

    def fetch(i):
        return pltpu.make_async_copy(tokens.at[rows(i)], rows_in.at[lax.rem(i, 2)], in_sem.at[lax.rem(i, 2)])

    def put(i):
        return pltpu.make_async_copy(rows_out.at[lax.rem(i, 2)], result.at[rows(i)], out_sem.at[lax.rem(i, 2)])

    fetch(0).start()
    red.sums[0] = small[...]
    red.start()
    xs[...] = jnp.zeros_like(xs)
    steps = red.steps()
    count = len(steps) + sizes.shards - 1
    moves = {}
    for n, step in enumerate(steps):
        moves.setdefault(min(n * extra // len(steps), extra - 1), []).append(step)
    for n in range(1, sizes.shards):
        moves.setdefault(min(1 + 2 * (n - 1), extra - 1), []).append(functools.partial(red.line, n))

    def chunk(i, _):
        fetch(i).wait()
        pl.when(i + 1 < extra)(lambda: fetch(i + 1).start())
        slot = lax.rem(i, 2)
        load_rows(rows_in[slot], wide, xs)
        attention(sizes, bias, vecs, wide_bias, weights, xs, work, low, qkv, mixed, middle, None)
        second_norm(vecs, middle, work, low)
        feed(sizes, hid_bias, vecs, weights, middle, low, work)
        pl.when(i >= 2)(lambda: put(i - 2).wait())
        store_rows(work, wide, rows_out.at[slot], live_scales(chunk_of(i) * BATCH, live))
        put(i).start()
        for at in sorted(moves):

            def run(at=at):
                for move in moves[at]:
                    move()

            pl.when(i == at)(run)
        return 0

    lax.fori_loop(0, extra, chunk, 0)
    red.end()
    for i in range(max(extra - 2, 0), extra):
        put(i).wait()


def run_rest(sizes, mesh_shape, live, tokens, held, params, gtok, dw, small):
    d = tokens.shape[1]
    anywhere = pl.BlockSpec(memory_space=pl.ANY)
    here = pl.BlockSpec(memory_space=pltpu.VMEM)
    dma = pltpu.SemaphoreType.DMA
    return pl.pallas_call(
        functools.partial(rest_kernel, sizes, mesh_shape),
        out_shape=(
            jax.ShapeDtypeStruct(tokens.shape, BF16),
            jax.ShapeDtypeStruct(tokens.shape, BF16),
            jax.ShapeDtypeStruct((d, sizes.columns), BF16),
            jax.ShapeDtypeStruct(small.shape, F32),
        ),
        in_specs=[pl.BlockSpec(memory_space=pltpu.SMEM), anywhere, anywhere] + [here] * len(params) + [anywhere, here, here],
        out_specs=(anywhere, anywhere, here, here),
        scratch_shapes=[
            pltpu.VMEM((2, CHUNK, d), BF16),
            pltpu.VMEM((2, CHUNK, d), BF16),
            dma((2,)),
            dma((2,)),
            forward_scratch(sizes, d),
            reduce_scratch(mesh_shape, d, sizes.columns, small.shape),
        ],
        input_output_aliases={2: 0},
        compiler_params=pltpu.CompilerParams(collective_id=1, has_side_effects=True, vmem_limit_bytes=VMEM_LIMIT),
    )(live, tokens, held, *params, gtok, dw, small)


def relative_bias(table, offset_index):
    onehot = (offset_index.reshape(1, AREA * AREA) == lax.broadcasted_iota(jnp.int32, (table.shape[1], 1), 0)).astype(BF16)
    values = jnp.dot(table.astype(BF16), onehot, preferred_element_type=F32) * LOG2E
    values = jnp.pad(values.reshape(-1, AREA, AREA), ((0, 0), (0, PAD - AREA), (0, 0)))
    return jnp.pad(values, ((0, 0), (0, 0), (0, LANES - AREA)), constant_values=-1e30)


def table_grad(scores, offset_index, table_rows):
    onehot = (offset_index.reshape(AREA * AREA, 1) == lax.broadcasted_iota(jnp.int32, (1, table_rows), 1)).astype(BF16)
    flat = scores[:, :AREA, :AREA].reshape(-1, AREA * AREA)
    return jnp.dot(flat.astype(BF16), onehot, preferred_element_type=F32)


def local(
    mesh_shape,
    tokens,
    cotangent,
    group_windows,
    offset_index,
    first_gain,
    first_shift,
    triple_weight,
    query_value_bias,
    bias_table,
    output_weight,
    output_bias,
    second_gain,
    second_shift,
    expand_weight,
    expand_bias,
    shrink_weight,
    shrink_bias,
):
    z = lax.axis_index("mp")
    shards = mesh_shape["mp"]
    d, _, loc = triple_weight.shape
    units = expand_weight.shape[1]
    table_rows, loc_heads = bias_table.shape
    sizes = Sizes(shards, loc, units)
    shard = jnp.concatenate(
        [triple_weight.transpose(1, 2, 0).reshape(3 * loc, d), output_weight, expand_weight.T, shrink_weight], axis=0
    )

    def widen(v):
        return jnp.pad(v, ((0, 0), (0, 512 - v.shape[1])))

    small = jnp.concatenate(
        [widen(expand_bias[None]), widen(query_value_bias.reshape(1, 2 * loc)), widen(bias_table.T)], axis=0
    ).astype(F32)
    small = jnp.pad(small, ((0, 8 - small.shape[0]), (0, 0)))
    weights, small = run_gather(mesh_shape, shard, small)
    hid_bias = small[:, 0:1, :units]
    pair = small[:, 1, : 2 * loc].reshape(shards, 2, loc)
    wide_bias = jnp.concatenate([pair[:, 0].reshape(1, -1), jnp.zeros((1, sizes.width), F32), pair[:, 1].reshape(1, -1)], axis=1)
    table = small[:, 2 : 2 + loc_heads, :table_rows].reshape(shards * loc_heads, table_rows)
    bias = relative_bias(table, offset_index)
    blank = jnp.zeros_like(first_gain)
    vecs = jnp.stack([first_gain, first_shift, output_bias, second_gain, second_shift, shrink_bias, blank, blank]).astype(F32)
    params = (bias, vecs, wide_bias, hid_bias, weights)
    chunks = tokens.shape[0] // CHUNK
    own = chunks // shards
    order = lax.rem(z * own + jnp.arange(chunks, dtype=jnp.int32), chunks)
    result, gtok, dw, dbias, sums, unit_sums = run_own(sizes, order[:own], group_windows, tokens, cotangent, *params)
    grads = table_grad(dbias, offset_index, table_rows)
    grads = jnp.pad(grads, ((0, 0), (0, 384 - table_rows)))
    packed = jnp.concatenate([sums, unit_sums.reshape(-1, d), grads.reshape(-1, d)], axis=0)
    result, grad_tokens, final, packed = run_rest(sizes, mesh_shape, group_windows, tokens, result, params, gtok, dw, packed)
    sums, rest = packed[:8], packed[8:]
    count = shards * units // d
    unit_total = lax.dynamic_slice_in_dim(rest[:count].reshape(-1), z * units, units)
    table_total = rest[count:].reshape(shards * loc_heads, 384)[:, :table_rows]
    table_total = lax.dynamic_slice_in_dim(table_total, z * loc_heads, loc_heads, 0).T
    pair_total = lax.dynamic_slice_in_dim(sums[0:2], z * loc, loc, 1)
    final = final.astype(F32)
    return (
        result,
        grad_tokens,
        sums[6],
        sums[7],
        final[:, : 3 * loc].reshape(d, 3, loc),
        pair_total,
        table_total,
        final[:, 3 * loc : 4 * loc].T,
        sums[5],
        sums[3],
        sums[4],
        final[:, 4 * loc : 4 * loc + units],
        unit_total,
        final[:, 4 * loc + units :].T,
        sums[2],
    )


def solution(mesh):
    in_specs = (
        P("dp", None),
        P("dp", None),
        P("dp"),
        P(),
        P(),
        P(),
        P(None, None, "mp"),
        P(None, "mp"),
        P(None, "mp"),
        P("mp", None),
        P(),
        P(),
        P(),
        P(None, "mp"),
        P("mp"),
        P("mp", None),
        P(),
    )
    out_specs = (
        P("dp", None),
        P("dp", None),
        P(),
        P(),
        P(None, None, "mp"),
        P(None, "mp"),
        P(None, "mp"),
        P("mp", None),
        P(),
        P(),
        P(),
        P(None, "mp"),
        P("mp"),
        P("mp", None),
        P(),
    )
    step = functools.partial(local, dict(mesh.shape))
    return jax.shard_map(step, mesh=mesh, in_specs=in_specs, out_specs=out_specs, check_vma=False)
```

```python
import functools
import math
import jax
import jax.numpy as jnp
from jax import lax
from jax.experimental import pallas as pl
from jax.experimental.pallas import tpu as pltpu
from jax.sharding import PartitionSpec as P

AREA = 100
PAD = 104
HEAD = 32
LANES = 128
PACK = LANES // HEAD
BATCH = 4
CHUNK = BATCH * AREA
ROWS = BATCH * PAD
EPSILON = 1e-05
DENSITY = 0.3989422804014327
LOG2E = 1.4426950408889634
F32 = jnp.float32
BF16 = jnp.bfloat16
MESH = pl.DeviceIdType.MESH
VMEM_LIMIT = 63 * 2**20


def dot(a, b):
    return jnp.dot(a, b, preferred_element_type=F32)


def dot_nt(a, b):
    return lax.dot_general(a, b, (((1,), (1,)), ((), ())), preferred_element_type=F32)


def dot_tn(a, b):
    return lax.dot_general(a, b, (((0,), (0,)), ((), ())), preferred_element_type=F32)


def normalize(values):
    centered = values - jnp.mean(values, axis=-1, keepdims=True)
    inv = lax.rsqrt(jnp.mean(centered * centered, axis=-1, keepdims=True) + EPSILON)
    return centered * inv, inv


def norm_back(grad, hat, inv):
    return inv * (
        grad
        - jnp.mean(grad, axis=-1, keepdims=True)
        - hat * jnp.mean(grad * hat, axis=-1, keepdims=True)
    )


def normal_cdf(hidden):
    z = jnp.abs(hidden) * 0.7071067811865476
    t = 1.0 / (1.0 + 0.3275911 * z)
    poly = t * (
        0.127414796 + t * (-0.142248368 + t * (0.7107068705 + t * (-0.7265760135 + t * 0.5307027145)))
    )
    bell = jnp.exp2(hidden * hidden * (-0.5 * LOG2E))
    tail = poly * bell
    return jnp.where(hidden > 0.0, 1.0 - tail, tail), bell


def head_of(shape, axis):
    return lax.broadcasted_iota(jnp.int32, shape, axis) // HEAD


def pad_rows(v):
    return jnp.concatenate([v, jnp.zeros((LANES - PAD, v.shape[1]), v.dtype)], axis=0)


def spread_rows(v):
    head = head_of((LANES, LANES), 1)
    full = pad_rows(v)
    return jnp.concatenate([jnp.where(head == h, full, 0.0) for h in range(PACK)], axis=0).astype(BF16)


def spread_columns(v):
    head = head_of((LANES, LANES), 0)
    turned = pad_rows(v).T
    return jnp.concatenate([jnp.where(head == h, turned, 0.0) for h in range(PACK)], axis=1).astype(BF16)


def diagonal(full):
    head = head_of((LANES, LANES), 0)
    out = full[:, 0:LANES]
    for h in range(1, PACK):
        out = jnp.where(head == h, full[:, h * LANES : (h + 1) * LANES], out)
    return out


def span(w, size=PAD):
    return pl.ds(pl.multiple_of(w * PAD, 8), size)


def load_rows(source, wide, padded):
    wide[...] = source.astype(F32)
    for w in range(BATCH):
        padded[w * PAD : w * PAD + AREA, :] = wide[w * AREA : (w + 1) * AREA, :]


def store_rows(padded, wide, target, scales=None):
    for w in range(BATCH):
        rows = padded[w * PAD : w * PAD + AREA, :]
        wide[w * AREA : (w + 1) * AREA, :] = rows if scales is None else rows * scales[w]
    target[...] = wide[...].astype(BF16)


class Sizes:
    def __init__(self, shards, loc, units):
        self.shards, self.loc, self.units = shards, loc, units
        self.width = shards * loc
        self.groups = self.width // LANES
        self.columns = 4 * loc + 2 * units

    def attention_part(self, weights, c):
        at = slice(c * self.loc, (c + 1) * self.loc)
        return jnp.concatenate([weights[z, at, :] for z in range(self.shards)], axis=0)

    def expand_part(self, weights, i):
        return weights[i, pl.ds(4 * self.loc, self.units), :]

    def shrink_part(self, weights, i):
        return weights[i, pl.ds(4 * self.loc + self.units, self.units), :]

    def add_attention(self, dw, c, value):
        for z in range(self.shards):
            at = slice(c * self.loc, (c + 1) * self.loc)
            dw[z, :, at] += value[:, z * self.loc : (z + 1) * self.loc]


def attention(sizes, bias, vecs, wide_bias, weights, xs, work, low, qkv, mixed, middle, keep, between=None):
    width, groups = sizes.width, sizes.groups
    scale = HEAD ** (-0.5) * LOG2E
    for w in range(BATCH):
        hat, _ = normalize(xs[span(w), :])
        work[span(w), :] = hat * vecs[0:1, :] + vecs[1:2, :]
    low[...] = work[...].astype(BF16)
    for c in range(3):
        at = slice(c * width, (c + 1) * width)
        qkv[:, at] = dot_nt(low[...], sizes.attention_part(weights, c)) + wide_bias[:, at]

    if between is not None:
        between()

    def attend(w, _):
        row = span(w)
        for g in range(groups):
            col = g * LANES
            q = qkv[row, pl.ds(col, LANES)].astype(BF16)
            k = qkv[row, pl.ds(width + col, LANES)]
            v = qkv[row, pl.ds(2 * width + col, LANES)]
            scores = dot(q, spread_columns(k))
            parts = []
            for h in range(PACK):
                s = scores[:, h * LANES : (h + 1) * LANES] * scale + bias[g * PACK + h]
                e = jnp.exp2(s - jnp.max(s, axis=-1, keepdims=True))
                parts.append(e * (1.0 / jnp.sum(e, axis=-1, keepdims=True)))
            probs = jnp.concatenate(parts, axis=1).astype(BF16)
            if keep is not None:
                keep[w * groups + g] = probs
            mixed[row, pl.ds(col, LANES)] = dot(probs, spread_rows(v))
        return 0

    lax.fori_loop(0, BATCH, attend, 0)
    middle[...] = xs[...] + dot(mixed[...].astype(BF16), sizes.attention_part(weights, 3)) + vecs[2:3, :]


def second_norm(vecs, middle, work, low):
    for w in range(BATCH):
        hat, _ = normalize(middle[span(w), :])
        work[span(w), :] = hat * vecs[3:4, :] + vecs[4:5, :]
    low[...] = work[...].astype(BF16)


def feed(sizes, hid_bias, vecs, weights, middle, low, acc):
    acc[...] = middle[...] + vecs[5:6, :]

    def block(i, _):
        hidden = dot_nt(low[...], sizes.expand_part(weights, i)) + hid_bias[i, 0:1, 0 : sizes.units]
        cdf, _ = normal_cdf(hidden)
        acc[...] += dot((hidden * cdf).astype(BF16), sizes.shrink_part(weights, i))
        return 0

    lax.fori_loop(0, sizes.shards, block, 0, unroll=4)


def column_sum(v):
    return jnp.sum(v, axis=0, keepdims=True)


def feed_both(sizes, hid_bias, vecs, weights, middle, low, glow, acc, back, dw, unit_sums):
    base, units = 4 * sizes.loc, sizes.units
    acc[...] = middle[...] + vecs[5:6, :]
    back[...] = jnp.zeros_like(back)

    def block(i, _):
        w_in, w_out = sizes.expand_part(weights, i), sizes.shrink_part(weights, i)
        hidden = dot_nt(low[...], w_in) + hid_bias[i, 0:1, 0 : sizes.units]
        cdf, bell = normal_cdf(hidden)
        active = (hidden * cdf).astype(BF16)
        grad = (dot_nt(glow[...], w_out) * (cdf + hidden * bell * DENSITY))
        unit_sums[i] += column_sum(grad)
        grad = grad.astype(BF16)
        acc[...] += dot(active, w_out)
        back[...] += dot(grad, w_in)
        dw[i, :, base : base + units] += dot_tn(low[...], grad)
        dw[i, :, base + units : base + 2 * units] += dot_tn(glow[...], active)
        return 0

    lax.fori_loop(0, sizes.shards, block, 0, unroll=2)


def backward(sizes, vecs, weights, xs, work, low, qkv, mixed, middle, glow, back, gmid, keep, dw, dbias, sums, between):
    width, groups = sizes.width, sizes.groups
    scale = HEAD ** (-0.5)
    gmix, dqkv = work, qkv
    for w in range(BATCH):
        hat, inv = normalize(middle[span(w), :])
        grad = back[span(w), :]
        sums[3:4, :] += column_sum(grad * hat)
        sums[4:5, :] += column_sum(grad)
        gmid[span(w), :] += norm_back(grad * vecs[3:4, :], hat, inv)
    branch = gmid[...].astype(BF16)
    sums[5:6, :] += column_sum(gmid[...])
    sizes.add_attention(dw, 3, dot_tn(branch, mixed[...].astype(BF16)))
    gmix[...] = dot_nt(branch, sizes.attention_part(weights, 3))
    between()

    def attend(w, _):
        row = span(w)
        for g in range(groups):
            col = g * LANES
            q = qkv[row, pl.ds(col, LANES)]
            k = qkv[row, pl.ds(width + col, LANES)]
            v = qkv[row, pl.ds(2 * width + col, LANES)]
            grad = gmix[row, pl.ds(col, LANES)]
            probs = keep[w * groups + g]
            wide_grad = dot(grad.astype(BF16), spread_columns(v))
            parts = []
            for h in range(PACK):
                p = probs[:, h * LANES : (h + 1) * LANES].astype(F32)
                t = wide_grad[:, h * LANES : (h + 1) * LANES]
                s = p * (t - jnp.sum(p * t, axis=-1, keepdims=True))
                dbias[g * PACK + h] += s
                parts.append(s)
            score = jnp.concatenate(parts, axis=1).astype(BF16)
            turned = pad_rows(q).T[:, :PAD].astype(BF16)
            dqkv[row, pl.ds(col, LANES)] = dot(score, spread_rows(k)) * scale
            dqkv[row, pl.ds(width + col, LANES)] = diagonal(dot(turned, score)).T[:PAD] * scale
            turned = pad_rows(grad).T[:, :PAD].astype(BF16)
            dqkv[row, pl.ds(2 * width + col, LANES)] = diagonal(dot(turned, probs)).T[:PAD]
        return 0

    lax.fori_loop(0, BATCH, attend, 0)
    for w in range(BATCH):
        hat, _ = normalize(xs[span(w), :])
        work[span(w), :] = hat * vecs[0:1, :] + vecs[1:2, :]
    low[...] = work[...].astype(BF16)
    back[...] = jnp.zeros_like(back)
    for c in range(3):
        at = slice(c * width, (c + 1) * width)
        grad = dqkv[:, at]
        if c != 1:
            sums[c // 2 : c // 2 + 1, :] += column_sum(grad)
        grad = grad.astype(BF16)
        back[...] += dot(grad, sizes.attention_part(weights, c))
        sizes.add_attention(dw, c, dot_tn(low[...], grad))
    for w in range(BATCH):
        hat, inv = normalize(xs[span(w), :])
        grad = back[span(w), :]
        sums[6:7, :] += column_sum(grad * hat)
        sums[7:8, :] += column_sum(grad)
        gmid[span(w), :] += norm_back(grad * vecs[0:1, :], hat, inv)


def live_scales(first, live):
    return [jnp.where(first + w < live[0], 1.0, 0.0).astype(F32) for w in range(BATCH)]


class Place:
    def __init__(self, mesh_shape):
        self.shards, self.n_dp = mesh_shape["mp"], mesh_shape["dp"]
        self.chips = self.n_dp // 2
        self.bits = int(math.log2(self.chips))
        self.dp, self.z = lax.axis_index("dp"), lax.axis_index("mp")
        self.core, self.chip = lax.rem(self.dp, 2), lax.div(self.dp, 2)

    def mate(self):
        return (self.dp + 1 - 2 * self.core, self.z)

    def flip(self, m):
        chip = self.chip
        for b in range(self.bits):
            if m >> b & 1:
                chip = chip + (1 << b) * (1 - 2 * lax.rem(lax.div(self.chip, 1 << b), 2))
        return chip

    def across(self, m):
        return (2 * self.flip(m) + self.core, self.z)

    def bit(self, b):
        return lax.rem(lax.div(self.chip, 1 << b), 2)

    def along(self, k):
        return (self.dp, lax.rem(self.z + k, self.shards))

    def greet(self, targets):
        barrier = pltpu.get_barrier_semaphore()
        for target in targets:
            pl.semaphore_signal(barrier, inc=1, device_id=target, device_id_type=MESH)
        pl.semaphore_wait(barrier, len(targets))

    def everyone(self):
        return (
            [self.mate()]
            + [self.across(m) for m in range(1, self.chips)]
            + [self.along(k) for k in range(1, self.shards)]
        )


def remote(source, target, sent, received, device):
    return pltpu.make_async_remote_copy(source, target, sent, received, device_id=device, device_id_type=MESH)


class Sends:
    def __init__(self):
        self.sent = []

    def send(self, make, when=None):
        self.sent.append((make, when))
        if when is None:
            make().start()
        else:
            pl.when(when())(lambda: make().start())

    def finish(self):
        for make, when in self.sent:
            if when is None:
                make().wait_send()
            else:
                pl.when(when())(lambda make=make: make().wait_send())


class Gather:
    def __init__(self, here, sends, out, parts, small, scratch):
        self.here, self.sends, self.out, self.parts, self.small = here, sends, out, parts, small
        self.z_sem, self.s_sem, self.p_sem, self.m_sem = scratch
        self.order = sorted(range(1, here.shards), key=lambda k: min(k, here.shards - k))

    def spot(self, part, shard, dp):
        first, rows = self.parts[part]
        rows //= self.here.n_dp
        return self.out.at[shard, pl.ds(pl.multiple_of(first + dp * rows, 16), rows)]

    def origin(self, k):
        return lax.rem(self.here.z - k + self.here.shards, self.here.shards)

    def along(self, part, k, arriving=False):
        here = self.here
        spot = self.spot(part, self.origin(k) if arriving else here.z, here.dp)
        return remote(spot, spot, self.z_sem.at[0, part, k], self.z_sem.at[1, part, k], here.along(k))

    def small_along(self, k, arriving=False):
        spot = self.small.at[self.origin(k) if arriving else self.here.z]
        return remote(spot, spot, self.s_sem.at[0, k], self.s_sem.at[1, k], self.here.along(k))

    def start(self):
        for k in self.order:
            self.sends.send(functools.partial(self.small_along, k))
        self.start_part(0)

    def start_part(self, part):
        for k in self.order:
            self.sends.send(functools.partial(self.along, part, k))

    def across(self, part, k, m, arriving=False):
        here = self.here
        spot = self.spot(part, self.origin(k), 2 * here.flip(m if arriving else 0) + here.core)
        return remote(spot, spot, self.p_sem.at[0, part, k, m], self.p_sem.at[1, part, k, m], here.across(m))

    def mate(self, part, k, m, arriving=False):
        here = self.here
        spot = self.spot(part, self.origin(k), 2 * here.flip(m) + (1 - here.core if arriving else here.core))
        return remote(spot, spot, self.m_sem.at[0, part, k, m], self.m_sem.at[1, part, k, m], here.mate())

    def spread(self, part):
        for k in self.order:
            self.along(part, k, True).wait_recv()
            for m in range(1, self.here.chips):
                self.sends.send(functools.partial(self.across, part, k, m))
            self.sends.send(functools.partial(self.mate, part, k, 0))

    def relay(self, part):
        for k in self.order:
            for m in range(1, self.here.chips):
                self.across(part, k, m, True).wait_recv()
                self.sends.send(functools.partial(self.mate, part, k, m))

    def wait(self, part):
        for k in self.order:
            for m in range(self.here.chips):
                self.mate(part, k, m, True).wait_recv()

    def wait_small(self):
        for k in self.order:
            self.small_along(k, True).wait_recv()


def gather_scratch(mesh_shape, parts):
    shards, chips = mesh_shape["mp"], mesh_shape["dp"] // 2
    dma = pltpu.SemaphoreType.DMA
    return [dma((2, parts, shards)), dma((2, shards)), dma((2, parts, shards, chips)), dma((2, parts, shards, chips))]


class Lines:
    def __init__(self, here, sends, source, target, sem, reach):
        self.here, self.sends, self.source, self.target, self.sem, self.reach = here, sends, source, target, sem, reach

    def block(self, z, c):
        chunks = self.source.shape[0]
        return self.target.at[pl.ds(pl.multiple_of((z * chunks + c) * CHUNK, 16), CHUNK)]

    def local(self, c):
        return pltpu.make_async_copy(self.source.at[c], self.block(self.here.z, c), self.sem.at[0, c, 0, self.reach])

    def copy(self, c, way, step, reach, arriving=False):
        here, sign = self.here, 1 - 2 * way
        held = jnp.clip(here.z - sign * step, 0, here.shards - 1)
        at = step - 1 if arriving else step + reach - 1
        source = self.source.at[c] if step == 0 else self.block(held, c)
        target = (here.dp, jnp.clip(here.z + sign * reach, 0, here.shards - 1))
        return remote(source, self.block(held, c), self.sem.at[0, c, way, at], self.sem.at[1, c, way, at], target)

    def there(self, way, step, reach):
        here, sign = self.here, 1 - 2 * way
        held, onward = here.z - sign * step, here.z + sign * reach
        return (held >= 0) & (held < here.shards) & (onward >= 0) & (onward < here.shards)

    def send(self, c, step, reach):
        for way in range(2):
            self.sends.send(
                functools.partial(self.copy, c, way, step, reach), functools.partial(self.there, way, step, reach)
            )

    def start(self, c):
        for reach in range(1, min(2, self.reach) + 1):
            self.send(c, 0, reach)

    def arrive(self, c, step):
        for way in range(2):
            pl.when(self.there(way, step, 0))(lambda way=way: self.copy(c, way, step, 1, True).wait_recv())

    def forward(self, c, step):
        self.arrive(c, step)
        self.send(c, step, 1)


class Reduction:
    def __init__(self, here, sends, dw, final, span, scratch):
        (self.acc, self.half, self.parts, self.lasts, self.h_sem, self.q_sem, self.l_sem, self.f_sem, self.g_sem) = scratch
        self.dw, self.final, self.here, self.sends = dw, final, here, sends
        self.d = dw.shape[1]
        self.first, self.columns = span
        split = self.columns // 2
        self.sides = (pl.ds(0, split), pl.ds(split, split))
        self.orders = (tuple(range(here.bits)), tuple(reversed(range(here.bits))))

    def send(self, make):
        self.sends.send(make)

    def rows_of(self, side, core, chip_bit, depth):
        size = self.d // 2
        first = core * size
        for b in self.orders[side][:depth]:
            size //= 2
            first = first + chip_bit(b) * size
        return pl.ds(pl.multiple_of(first, 16), size)

    def half_rows(self, core):
        return pl.ds(pl.multiple_of(core * (self.d // 2), 16), self.d // 2)

    def half_copy(self, s):
        rows = self.half_rows(1 - self.here.core)
        return remote(self.acc.at[s, rows], self.half.at[s], self.h_sem.at[0, s], self.h_sem.at[1, s], self.here.mate())

    def half_send(self, s):
        rows = self.half_rows(1 - self.here.core)
        self.acc[s, rows, :] = self.dw[s, rows, pl.ds(self.first, self.columns)].astype(BF16)
        self.send(functools.partial(self.half_copy, s))

    def half_add(self, s):
        self.half_copy(s).wait_recv()
        mine = self.half_rows(self.here.core)
        self.acc[s, mine, :] = (self.dw[s, mine, pl.ds(self.first, self.columns)] + self.half[s].astype(F32)).astype(BF16)

    def plane_copy(self, s, depth, side):
        here = self.here
        b = self.orders[side][depth]
        rows = self.rows_of(side, here.core, lambda c: 1 - here.bit(c) if c == b else here.bit(c), depth + 1)
        target = self.parts[side][depth].at[s]
        sems = self.q_sem
        return remote(
            self.acc.at[s, rows, self.sides[side]], target, sems.at[0, side, depth, s], sems.at[1, side, depth, s], here.across(1 << b)
        )

    def plane_send(self, s, depth):
        for side in range(2):
            self.send(functools.partial(self.plane_copy, s, depth, side))

    def plane_add(self, s, depth):
        for side in range(2):
            self.plane_copy(s, depth, side).wait_recv()
            rows = self.rows_of(side, self.here.core, self.here.bit, depth + 1)
            arrived = self.parts[side][depth][s]
            here = self.acc[s, rows, self.sides[side]]
            self.acc[s, rows, self.sides[side]] = (here.astype(F32) + arrived.astype(F32)).astype(BF16)

    def mine(self, side):
        return self.rows_of(side, self.here.core, self.here.bit, self.here.bits)

    def shard_copy(self, side, k):
        here = self.here
        s = lax.rem(here.z + k, here.shards)
        return remote(
            self.acc.at[s, self.mine(side), self.sides[side]], self.lasts[side].at[k], self.l_sem.at[0, side, k], self.l_sem.at[1, side, k], here.along(k)
        )

    def shard_sends(self):
        for k in range(1, self.here.shards):
            for side in range(2):
                self.send(functools.partial(self.shard_copy, side, k))

    def shard_adds(self):
        for side in range(2):
            rows = self.mine(side)
            total = self.acc[self.here.z, rows, self.sides[side]].astype(F32)
            for k in range(1, self.here.shards):
                self.shard_copy(side, k).wait_recv()
                total = total + self.lasts[side][k].astype(F32)
            self.final[rows, self.final_side(side)] = total.astype(BF16)

    def final_side(self, side):
        split = self.columns // 2
        return pl.ds(self.first + side * split, split)

    def final_spot(self, side, m, core):
        here = self.here
        rows = self.rows_of(side, core, lambda b: 1 - here.bit(b) if m >> b & 1 else here.bit(b), here.bits)
        return self.final.at[rows, self.final_side(side)]

    def final_copy(self, side, m, arriving=False):
        here = self.here
        spot = self.final_spot(side, m if arriving else 0, here.core)
        return remote(spot, spot, self.f_sem.at[0, side, m], self.f_sem.at[1, side, m], here.across(m))

    def final_relay(self, side, m, arriving=False):
        here = self.here
        spot = self.final_spot(side, m, 1 - here.core if arriving else here.core)
        return remote(spot, spot, self.g_sem.at[0, side, m], self.g_sem.at[1, side, m], here.mate())

    def final_spread(self):
        for side in range(2):
            for m in range(1, self.here.chips):
                self.send(functools.partial(self.final_copy, side, m))
            self.send(functools.partial(self.final_relay, side, 0))

    def final_relays(self):
        for side in range(2):
            for m in range(1, self.here.chips):
                self.final_copy(side, m, True).wait_recv()
                self.send(functools.partial(self.final_relay, side, m))

    def final_wait(self):
        for side in range(2):
            for m in range(self.here.chips):
                self.final_relay(side, m, True).wait_recv()

    def start(self):
        for s in range(self.here.shards):
            self.half_send(s)

    def plane(self, depth):
        for s in range(self.here.shards):
            if depth == 0:
                self.half_add(s)
            else:
                self.plane_add(s, depth - 1)
            if depth < self.here.bits:
                self.plane_send(s, depth)
        if depth == self.here.bits:
            self.shard_sends()

    def close(self):
        self.shard_adds()
        self.final_spread()


def reduce_scratch(mesh_shape, d, columns):
    shards, chips = mesh_shape["mp"], mesh_shape["dp"] // 2
    bits = int(math.log2(chips))
    split, finish = columns // 2, d // (2 * chips)
    dma = pltpu.SemaphoreType.DMA
    return [
        pltpu.VMEM((shards, d, columns), BF16),
        pltpu.VMEM((shards, d // 2, columns), BF16),
        [[pltpu.VMEM((shards, d >> (depth + 2), split), BF16) for depth in range(bits)]] * 2,
        [pltpu.VMEM((shards, finish, split), BF16)] * 2,
        dma((2, shards)),
        dma((2, 2, bits, shards)),
        dma((2, 2, shards)),
        dma((2, 2, chips)),
        dma((2, 2, chips)),
    ]


class Totals:
    def __init__(self, here, sends, out, scratch):
        self.here, self.sends, self.small_out = here, sends, out
        self.sums, self.sums_in, self.t_sem = scratch
        self.stages = here.bits + 1

    def send(self, make):
        self.sends.send(make)

    def small_copy(self, i):
        here = self.here
        target = here.mate() if i == 0 else here.across(1 << (i - 1))
        return remote(self.sums.at[i], self.sums_in.at[i], self.t_sem.at[0, i], self.t_sem.at[1, i], target)

    def small_send(self, i):
        self.send(functools.partial(self.small_copy, i))

    def small_add(self, i):
        self.small_copy(i).wait_recv()
        self.sums[i + 1] = self.sums[i] + self.sums_in[i]

    def small_along(self, k):
        slot = self.stages + k - 1
        return remote(
            self.sums.at[self.stages], self.sums_in.at[slot], self.t_sem.at[0, slot], self.t_sem.at[1, slot], self.here.along(k)
        )

    def small_sends(self):
        for k in range(1, self.here.shards):
            self.send(functools.partial(self.small_along, k))

    def small_total(self):
        total = self.sums[self.stages]
        for k in range(1, self.here.shards):
            self.small_along(k).wait_recv()
            total = total + self.sums_in[self.stages + k - 1]
        self.small_out[...] = total


def totals_scratch(mesh_shape, shape):
    shards, chips = mesh_shape["mp"], mesh_shape["dp"] // 2
    bits = int(math.log2(chips))
    return [
        pltpu.VMEM((bits + 2, *shape), F32),
        pltpu.VMEM((bits + shards, *shape), F32),
        pltpu.SemaphoreType.DMA((2, bits + shards)),
    ]


TALL = 384
BLOCK = 8


def one_hot(index_row):
    return (lax.broadcasted_iota(jnp.int32, (TALL, LANES), 0) == index_row).astype(F32).astype(BF16)


def build_bias(index, table, bias):
    heads = table.shape[0]
    tall = jnp.broadcast_to(table[:, None, :], (heads, BLOCK, TALL)).reshape(heads * BLOCK, TALL).astype(BF16)
    row = lax.rem(lax.broadcasted_iota(jnp.int32, (heads * BLOCK, LANES), 0), BLOCK)
    blocked = jnp.where(lax.broadcasted_iota(jnp.int32, (heads * BLOCK, LANES), 1) < AREA, 0.0, -1e30)

    def block(r, _):
        at = pl.ds(pl.multiple_of(r * BLOCK, BLOCK), BLOCK)
        rows = index[at, :]
        out = blocked
        for i in range(BLOCK):
            values = dot(tall, one_hot(rows[i : i + 1, :]))
            out = jnp.where(row == i, values * LOG2E + blocked, out)
        bias[:, at, :] = out.reshape(heads, BLOCK, LANES)
        return 0

    lax.fori_loop(0, PAD // BLOCK, block, 0)


def sum_table(index, dbias, turned):
    heads = dbias.shape[0]
    row = lax.rem(lax.broadcasted_iota(jnp.int32, (heads * BLOCK, LANES), 0), BLOCK)
    turned[...] = jnp.zeros_like(turned)

    def block(r, _):
        at = pl.ds(pl.multiple_of(r * BLOCK, BLOCK), BLOCK)
        rows = index[at, :]
        values = dbias[:, at, :].reshape(heads * BLOCK, LANES)
        left = jnp.concatenate([one_hot(rows[i : i + 1, :]) for i in range(BLOCK)], axis=1)
        right = jnp.concatenate([jnp.where(row == i, values, 0.0) for i in range(BLOCK)], axis=1).astype(BF16)
        turned[...] += dot_nt(left, right)
        return 0

    lax.fori_loop(0, PAD // BLOCK, block, 0)


def block_kernel(sizes, mesh_shape, exchange, live, index, vecs, tokens, cotangent, shard, small,
                 result, gtok, final, small_out,
                 weights, smalls, wide_bias, bias, dbias, dw, xs, qkv, mixed, middle, keep,
                 wide, work, low, glow, back, gmid, sums, unit_sums, turned,
                 tok_in, cot_in, rows_in, rows_out,
                 own_sem, tok_sem, cot_sem, in_sem, out_sem, result_sem, gtok_sem,
                 gather_refs, feed_refs, attn_refs, total_refs):
    here = Place(mesh_shape)
    sends = Sends()
    own_out, own_grad = tok_in, cot_in
    shards, own = sizes.shards, tok_in.shape[0]
    chunks = shards * own
    loc, units = sizes.loc, sizes.units
    gather = Gather(here, sends, weights, ((0, 4 * loc), (4 * loc, 2 * units)), smalls, gather_refs)
    feed_sum = Reduction(here, sends, dw, final, (4 * loc, 2 * units), feed_refs)
    attn_sum = Reduction(here, sends, dw, final, (0, 4 * loc), attn_refs)
    totals = Totals(here, sends, small_out, total_refs)
    results = Lines(here, sends, own_out, result, result_sem, 1)
    grads = Lines(here, sends, own_grad, gtok, gtok_sem, shards - 1)

    def own_rows(c):
        return pl.ds(pl.multiple_of((here.z * own + c) * CHUNK, 16), CHUNK)

    def own_tokens(c):
        return pltpu.make_async_copy(tokens.at[own_rows(c)], tok_in.at[c], tok_sem.at[c])

    def own_cotangent(c):
        return pltpu.make_async_copy(cotangent.at[own_rows(c)], cot_in.at[c], cot_sem.at[c])

    mine = [
        pltpu.make_async_copy(shard, weights.at[here.z], own_sem.at[0]),
        pltpu.make_async_copy(small, smalls.at[here.z], own_sem.at[1]),
    ]
    for copy in mine:
        copy.start()
    for c in range(own):
        own_tokens(c).start()
    for c in range(own):
        own_cotangent(c).start()
    here.greet(here.everyone())
    for copy in mine:
        copy.wait()
    gather.start()
    xs[...] = jnp.zeros_like(xs)
    dbias[...] = jnp.zeros_like(dbias)
    sums[...] = jnp.zeros_like(sums)
    unit_sums[...] = jnp.zeros_like(unit_sums)
    gather.wait_small()
    heads = sizes.width // HEAD
    count = heads // shards
    for z in range(shards):
        at = slice(z * loc, (z + 1) * loc)
        wide_bias[:, at] = smalls[z, 1:2, 0:loc]
        wide_bias[:, slice(2 * sizes.width + z * loc, 2 * sizes.width + (z + 1) * loc)] = smalls[z, 1:2, loc : 2 * loc]
    wide_bias[:, sizes.width : 2 * sizes.width] = jnp.zeros((1, sizes.width), F32)
    gather.spread(0)
    gather.start_part(1)
    table = jnp.concatenate([smalls[z, 2 : 2 + count, 0:TALL] for z in range(shards)], axis=0)
    build_bias(index, table, bias)
    gather.relay(0)

    def clear(z, _):
        dw[z] = jnp.zeros_like(dw[z])
        return 0

    lax.fori_loop(0, shards, clear, 0)
    gather.wait(0)

    def attend(c, _):
        own_tokens(c).wait()
        load_rows(tok_in[c], wide, xs.at[c])

        def between():
            pl.when(c == 0)(lambda: gather.spread(1))

        attention(sizes, bias, vecs, wide_bias, weights, xs.at[c], work, low, qkv.at[c], mixed.at[c], middle.at[c], keep.at[c], between)
        pl.when(c == 0)(lambda: gather.relay(1))
        return 0

    lax.fori_loop(0, own, attend, 0)
    gather.wait(1)

    def finish(c, _):
        scales = live_scales((here.z * own + c) * BATCH, live)
        own_cotangent(c).wait()
        second_norm(vecs, middle.at[c], work, low)
        wide[...] = cot_in[c].astype(F32)
        for w in range(BATCH):
            gmid[w * PAD : w * PAD + AREA, :] = wide[w * AREA : (w + 1) * AREA, :] * scales[w]
            gmid[w * PAD + AREA : (w + 1) * PAD, :] = jnp.zeros((PAD - AREA, gmid.shape[1]), F32)
        sums[2:3, :] += column_sum(gmid[...])
        glow[...] = gmid[...].astype(BF16)
        feed_both(sizes, smalls, vecs, weights, middle.at[c], low, glow, work, back, dw, unit_sums)
        store_rows(work, wide, own_out.at[c], scales)
        for i in range(own):

            def fed(i=i):
                results.local(i).start()
                if i < exchange:
                    results.start(i)
                if i == own - 1:
                    feed_sum.start()

            pl.when(c == i)(fed)

        def between():
            pl.when(c == own - 1)(lambda: feed_sum.plane(0))

        backward(sizes, vecs, weights, xs.at[c], work, low, qkv.at[c], mixed.at[c], middle.at[c], glow, back, gmid, keep.at[c], dw, dbias, sums, between)
        store_rows(gmid, wide, own_grad.at[c])
        for i in range(own):

            def done(i=i):
                grads.local(i).start()
                grads.start(i)

            pl.when(c == i)(done)
        return 0

    lax.fori_loop(0, own, finish, 0)
    attn_sum.start()
    sum_table(index, dbias, turned)
    table = turned[...].T
    total = totals.sums
    total[0, 0:8, :] = sums[...]
    for z in range(shards):
        at = z * units % sizes.width
        line = 8 + z * units // sizes.width
        total[0, line : line + 1, at : at + units] = unit_sums[z]
    base = 8 + shards * units // sizes.width
    total[0, base : base + heads, 0:TALL] = jnp.sum(table.reshape(heads, BLOCK, TALL), axis=1)
    totals.small_send(0)

    extra = chunks - own
    before = jnp.int32(0)
    if exchange == own:
        before = jnp.maximum(here.z - 1, 0) * own
        after = jnp.maximum(shards - 2 - here.z, 0) * own
        extras, most = before + after, extra - own

        def chunk_of(i):
            return jnp.where(i < before, i, i - before + (here.z + 2) * own)
    else:
        extras, most = jnp.int32(extra), extra

        def chunk_of(i):
            return lax.rem((here.z + 1) * own + i, chunks)

    def rows(i):
        return pl.ds(pl.multiple_of(chunk_of(i) * CHUNK, 16), CHUNK)

    def fetch(i):
        return pltpu.make_async_copy(tokens.at[rows(i)], rows_in.at[lax.rem(i, 2)], in_sem.at[lax.rem(i, 2)])

    def put(i):
        return pltpu.make_async_copy(rows_out.at[lax.rem(i, 2)], result.at[rows(i)], out_sem.at[lax.rem(i, 2)])

    pl.when(extras > 0)(lambda: fetch(0).start())
    bits = here.bits
    points = 2 * most
    moves = {p: [] for p in range(points + 1)}

    def place(p, step):
        moves[max(0, min(p, points))].append(step)

    place(0, functools.partial(attn_sum.plane, 0))
    for depth in range(1, bits + 1):
        place(2 * depth - 1, functools.partial(feed_sum.plane, depth))
        place(2 * depth, functools.partial(attn_sum.plane, depth))
    for i in range(totals.stages):

        def small_step(i=i):
            totals.small_add(i)
            if i + 1 < totals.stages:
                totals.small_send(i + 1)
            else:
                totals.small_sends()

        place(2 * i + 1, small_step)
    for c in range(own):
        for n in range(2, shards - 1):
            place(2 * n - 2 + 6 * c, functools.partial(grads.forward, c, n))
    place(points - 4, feed_sum.close)
    place(points - 2, feed_sum.final_relays)
    place(points - 2, attn_sum.close)

    def run(i, half):
        for at in range(points):
            if at % 2 == half and moves[at]:

                def go(at=at):
                    for move in moves[at]:
                        move()

                pl.when(i == at // 2)(go)

    states = (xs.at[0], work, low, qkv.at[0], mixed.at[0], middle.at[0])

    def other(i, _):
        @pl.when(i < extras)
        def _():
            fetch(i).wait()
            pl.when(i + 1 < extras)(lambda: fetch(i + 1).start())
            load_rows(rows_in[lax.rem(i, 2)], wide, xs.at[0])
            attention(sizes, bias, vecs, wide_bias, weights, *states, None)

        run(i, 0)

        @pl.when(i < extras)
        def _():
            second_norm(vecs, middle.at[0], work, low)
            feed(sizes, smalls, vecs, weights, middle.at[0], low, work)
            pl.when(i >= 2)(lambda: put(i - 2).wait())
            store_rows(work, wide, rows_out.at[lax.rem(i, 2)], live_scales(chunk_of(i) * BATCH, live))
            put(i).start()

        run(i, 1)
        return 0

    lax.fori_loop(0, most, other, 0)
    for move in moves[points]:
        move()
    attn_sum.final_relays()
    totals.small_total()
    for c in range(exchange):
        results.arrive(c, 1)
    for c in range(own):
        for n in range(1, shards):
            if n < 2 or n == shards - 1:
                grads.arrive(c, n)
    attn_sum.final_wait()
    feed_sum.final_wait()
    sends.finish()
    for c in range(own):
        results.local(c).wait()
        grads.local(c).wait()
    for back_by in (2, 1):
        pl.when(extras >= back_by)(lambda back_by=back_by: put(extras - back_by).wait())


def run_block(sizes, mesh_shape, exchange, live, index, vecs, tokens, cotangent, shard, small):
    d = tokens.shape[1]
    shards, width, units, groups = sizes.shards, sizes.width, sizes.units, sizes.groups
    heads = width // HEAD
    own = tokens.shape[0] // CHUNK // shards
    anywhere = pl.BlockSpec(memory_space=pl.ANY)
    here = pl.BlockSpec(memory_space=pltpu.VMEM)
    dma = pltpu.SemaphoreType.DMA
    total_shape = (8 + shards * units // d + heads, d)
    return pl.pallas_call(
        functools.partial(block_kernel, sizes, mesh_shape, exchange),
        out_shape=(
            jax.ShapeDtypeStruct(tokens.shape, BF16),
            jax.ShapeDtypeStruct(tokens.shape, BF16),
            jax.ShapeDtypeStruct((d, sizes.columns), BF16),
            jax.ShapeDtypeStruct(total_shape, F32),
        ),
        in_specs=[pl.BlockSpec(memory_space=pltpu.SMEM), here, here, anywhere, anywhere, anywhere, anywhere],
        out_specs=(anywhere, anywhere, here, here),
        scratch_shapes=[
            pltpu.VMEM((shards, sizes.columns, d), BF16),
            pltpu.VMEM((shards, *small.shape), F32),
            pltpu.VMEM((1, 3 * width), F32),
            pltpu.VMEM((heads, PAD, LANES), F32),
            pltpu.VMEM((heads, PAD, LANES), F32),
            pltpu.VMEM((shards, d, sizes.columns), F32),
            pltpu.VMEM((own, ROWS, d), F32),
            pltpu.VMEM((own, ROWS, 3 * width), F32),
            pltpu.VMEM((own, ROWS, width), F32),
            pltpu.VMEM((own, ROWS, d), F32),
            pltpu.VMEM((own, BATCH * groups, PAD, PACK * LANES), BF16),
            pltpu.VMEM((CHUNK, d), F32),
            pltpu.VMEM((ROWS, d), F32),
            pltpu.VMEM((ROWS, d), BF16),
            pltpu.VMEM((ROWS, d), BF16),
            pltpu.VMEM((ROWS, d), F32),
            pltpu.VMEM((ROWS, d), F32),
            pltpu.VMEM((8, d), F32),
            pltpu.VMEM((shards, 1, units), F32),
            pltpu.VMEM((TALL, heads * BLOCK), F32),
            pltpu.VMEM((own, CHUNK, d), BF16),
            pltpu.VMEM((own, CHUNK, d), BF16),
            pltpu.VMEM((2, CHUNK, d), BF16),
            pltpu.VMEM((2, CHUNK, d), BF16),
            dma((2,)),
            dma((own,)),
            dma((own,)),
            dma((2,)),
            dma((2,)),
            dma((2, own, 2, 2)),
            dma((2, own, 2, shards)),
            gather_scratch(mesh_shape, 2),
            reduce_scratch(mesh_shape, d, 2 * units),
            reduce_scratch(mesh_shape, d, 4 * sizes.loc),
            totals_scratch(mesh_shape, total_shape),
        ],
        compiler_params=pltpu.CompilerParams(collective_id=0, has_side_effects=True, vmem_limit_bytes=VMEM_LIMIT),
    )(live, index, vecs, tokens, cotangent, shard, small)


def finish_kernel(sizes, z, final, packed, triple, output, expand, shrink, pair, table, unit, *singles):
    loc, units = sizes.loc, sizes.units
    d = final.shape[0]
    count = sizes.width // HEAD // sizes.shards
    triple[...] = final[:, : 3 * loc].astype(F32)
    output[...] = final[:, 3 * loc : 4 * loc].astype(F32).T
    expand[...] = final[:, 4 * loc : 4 * loc + units].astype(F32)
    shrink[...] = final[:, 4 * loc + units :].astype(F32).T
    base = 8 + sizes.shards * units // d
    for s in range(sizes.shards):

        def take(s=s):
            pair[...] = packed[0:2, s * loc : (s + 1) * loc]
            table[...] = packed[base + s * count : base + (s + 1) * count, 0:TALL]
            at = s * units % d
            line = 8 + s * units // d
            unit[...] = packed[line : line + 1, at : at + units]

        pl.when(z[0] == s)(take)
    for ref, line in zip(singles, (6, 7, 5, 3, 4, 2)):
        ref[...] = packed[line : line + 1, :]


def run_finish(sizes, z, final, packed):
    loc, units, d = sizes.loc, sizes.units, final.shape[0]
    count = sizes.width // HEAD // sizes.shards
    shapes = [(d, 3 * loc), (loc, d), (d, units), (units, d), (2, loc), (count, TALL), (1, units)] + [(1, d)] * 6
    here = pl.BlockSpec(memory_space=pltpu.VMEM)
    return pl.pallas_call(
        functools.partial(finish_kernel, sizes),
        out_shape=tuple(jax.ShapeDtypeStruct(shape, F32) for shape in shapes),
        in_specs=[pl.BlockSpec(memory_space=pltpu.SMEM), here, here],
        out_specs=tuple([here] * len(shapes)),
        compiler_params=pltpu.CompilerParams(vmem_limit_bytes=32 * 2**20),
    )(z, final, packed)


def local(
    mesh_shape,
    tokens,
    cotangent,
    group_windows,
    offset_index,
    first_gain,
    first_shift,
    triple_weight,
    query_value_bias,
    bias_table,
    output_weight,
    output_bias,
    second_gain,
    second_shift,
    expand_weight,
    expand_bias,
    shrink_weight,
    shrink_bias,
):
    z = lax.axis_index("mp")
    shards = mesh_shape["mp"]
    d, _, loc = triple_weight.shape
    units = expand_weight.shape[1]
    table_rows, loc_heads = bias_table.shape
    heads = shards * loc_heads
    sizes = Sizes(shards, loc, units)
    shard = jnp.concatenate(
        [triple_weight.transpose(1, 2, 0).reshape(3 * loc, d), output_weight, expand_weight.T, shrink_weight], axis=0
    )

    def widen(v):
        return jnp.pad(v, ((0, 0), (0, 512 - v.shape[1])))

    small = jnp.concatenate(
        [widen(expand_bias[None]), widen(query_value_bias.reshape(1, 2 * loc)), widen(bias_table.T)], axis=0
    ).astype(F32)
    small = jnp.pad(small, ((0, 8 - small.shape[0]), (0, 0)))
    blank = jnp.zeros_like(first_gain)
    vecs = jnp.stack([first_gain, first_shift, output_bias, second_gain, second_shift, shrink_bias, blank, blank]).astype(F32)
    index = jnp.pad(offset_index, ((0, PAD - AREA), (0, LANES - AREA)), constant_values=-1)
    result, grad_tokens, final, packed = run_block(
        sizes, mesh_shape, EXCHANGE, group_windows, index, vecs, tokens, cotangent, shard, small
    )
    triple, output, expand, shrink, pair, table, unit, *singles = run_finish(sizes, z.reshape(1), final, packed)
    first_gain, first_shift, output_sum, second_gain, second_shift, shrink_sum = (v.reshape(d) for v in singles)
    return (
        result,
        grad_tokens,
        first_gain,
        first_shift,
        triple.reshape(d, 3, loc),
        pair,
        table[:, :table_rows].T,
        output,
        output_sum,
        second_gain,
        second_shift,
        expand,
        unit.reshape(units),
        shrink,
        shrink_sum,
    )


EXCHANGE = 0


def solution(mesh):
    in_specs = (
        P("dp", None),
        P("dp", None),
        P("dp"),
        P(),
        P(),
        P(),
        P(None, None, "mp"),
        P(None, "mp"),
        P(None, "mp"),
        P("mp", None),
        P(),
        P(),
        P(),
        P(None, "mp"),
        P("mp"),
        P("mp", None),
        P(),
    )
    out_specs = (
        P("dp", None),
        P("dp", None),
        P(),
        P(),
        P(None, None, "mp"),
        P(None, "mp"),
        P(None, "mp"),
        P("mp", None),
        P(),
        P(),
        P(),
        P(None, "mp"),
        P("mp"),
        P("mp", None),
        P(),
    )
    step = functools.partial(local, dict(mesh.shape))
    return jax.shard_map(step, mesh=mesh, in_specs=in_specs, out_specs=out_specs, check_vma=False)
```

```python
import functools
import math
import jax
import jax.numpy as jnp
from jax import lax
from jax.experimental import pallas as pl
from jax.experimental.pallas import tpu as pltpu
from jax.sharding import PartitionSpec as P

AREA = 100
PAD = 104
HEAD = 32
LANES = 128
PACK = LANES // HEAD
BATCH = 4
CHUNK = BATCH * AREA
ROWS = BATCH * PAD
EPSILON = 1e-05
DENSITY = 0.3989422804014327
LOG2E = 1.4426950408889634
F32 = jnp.float32
BF16 = jnp.bfloat16
MESH = pl.DeviceIdType.MESH
VMEM_LIMIT = 63 * 2**20


def dot(a, b):
    return jnp.dot(a, b, preferred_element_type=F32)


def dot_nt(a, b):
    return lax.dot_general(a, b, (((1,), (1,)), ((), ())), preferred_element_type=F32)


def dot_tn(a, b):
    return lax.dot_general(a, b, (((0,), (0,)), ((), ())), preferred_element_type=F32)


def normalize(values):
    centered = values - jnp.mean(values, axis=-1, keepdims=True)
    inv = lax.rsqrt(jnp.mean(centered * centered, axis=-1, keepdims=True) + EPSILON)
    return centered * inv, inv


def norm_back(grad, hat, inv):
    return inv * (
        grad
        - jnp.mean(grad, axis=-1, keepdims=True)
        - hat * jnp.mean(grad * hat, axis=-1, keepdims=True)
    )


def normal_cdf(hidden):
    z = jnp.abs(hidden) * 0.7071067811865476
    t = 1.0 / (1.0 + 0.3275911 * z)
    poly = t * (
        0.127414796 + t * (-0.142248368 + t * (0.7107068705 + t * (-0.7265760135 + t * 0.5307027145)))
    )
    bell = jnp.exp2(hidden * hidden * (-0.5 * LOG2E))
    tail = poly * bell
    return jnp.where(hidden > 0.0, 1.0 - tail, tail), bell


def head_of(shape, axis):
    return lax.broadcasted_iota(jnp.int32, shape, axis) // HEAD


def pad_rows(v):
    return jnp.concatenate([v, jnp.zeros((LANES - PAD, v.shape[1]), v.dtype)], axis=0)


def spread_rows(v):
    head = head_of((LANES, LANES), 1)
    full = pad_rows(v)
    return jnp.concatenate([jnp.where(head == h, full, 0.0) for h in range(PACK)], axis=0).astype(BF16)


def spread_columns(v):
    head = head_of((LANES, LANES), 0)
    turned = pad_rows(v).T
    return jnp.concatenate([jnp.where(head == h, turned, 0.0) for h in range(PACK)], axis=1).astype(BF16)


def diagonal(full):
    head = head_of((LANES, LANES), 0)
    out = full[:, 0:LANES]
    for h in range(1, PACK):
        out = jnp.where(head == h, full[:, h * LANES : (h + 1) * LANES], out)
    return out


def span(w, size=PAD):
    return pl.ds(pl.multiple_of(w * PAD, 8), size)


def load_rows(source, wide, padded):
    wide[...] = source.astype(F32)
    for w in range(BATCH):
        padded[w * PAD : w * PAD + AREA, :] = wide[w * AREA : (w + 1) * AREA, :]


def store_rows(padded, wide, target, scales=None):
    for w in range(BATCH):
        rows = padded[w * PAD : w * PAD + AREA, :]
        wide[w * AREA : (w + 1) * AREA, :] = rows if scales is None else rows * scales[w]
    target[...] = wide[...].astype(BF16)


class Sizes:
    def __init__(self, shards, loc, units):
        self.shards, self.loc, self.units = shards, loc, units
        self.width = shards * loc
        self.groups = self.width // LANES
        self.columns = 4 * loc + 2 * units

    def attention_part(self, weights, c):
        at = slice(c * self.loc, (c + 1) * self.loc)
        return jnp.concatenate([weights[z, at, :] for z in range(self.shards)], axis=0)

    def expand_part(self, weights, i):
        return weights[i, pl.ds(4 * self.loc, self.units), :]

    def shrink_part(self, weights, i):
        return weights[i, pl.ds(4 * self.loc + self.units, self.units), :]

    def add_attention(self, dw, c, value):
        for z in range(self.shards):
            at = slice(c * self.loc, (c + 1) * self.loc)
            dw[z, :, at] += value[:, z * self.loc : (z + 1) * self.loc]


def attention(sizes, bias, vecs, wide_bias, weights, xs, work, low, qkv, mixed, middle, keep, between=None):
    width, groups = sizes.width, sizes.groups
    scale = HEAD ** (-0.5) * LOG2E
    for w in range(BATCH):
        hat, _ = normalize(xs[span(w), :])
        work[span(w), :] = hat * vecs[0:1, :] + vecs[1:2, :]
    low[...] = work[...].astype(BF16)
    for c in range(3):
        at = slice(c * width, (c + 1) * width)
        qkv[:, at] = dot_nt(low[...], sizes.attention_part(weights, c)) + wide_bias[:, at]

    if between is not None:
        between()

    def attend(w, _):
        row = span(w)
        for g in range(groups):
            col = g * LANES
            q = qkv[row, pl.ds(col, LANES)].astype(BF16)
            k = qkv[row, pl.ds(width + col, LANES)]
            v = qkv[row, pl.ds(2 * width + col, LANES)]
            scores = dot(q, spread_columns(k))
            parts = []
            for h in range(PACK):
                s = scores[:, h * LANES : (h + 1) * LANES] * scale + bias[g * PACK + h]
                e = jnp.exp2(s - jnp.max(s, axis=-1, keepdims=True))
                parts.append(e * (1.0 / jnp.sum(e, axis=-1, keepdims=True)))
            probs = jnp.concatenate(parts, axis=1).astype(BF16)
            if keep is not None:
                keep[w * groups + g] = probs
            mixed[row, pl.ds(col, LANES)] = dot(probs, spread_rows(v))
        return 0

    lax.fori_loop(0, BATCH, attend, 0)
    middle[...] = xs[...] + dot(mixed[...].astype(BF16), sizes.attention_part(weights, 3)) + vecs[2:3, :]


def second_norm(vecs, middle, work, low):
    for w in range(BATCH):
        hat, _ = normalize(middle[span(w), :])
        work[span(w), :] = hat * vecs[3:4, :] + vecs[4:5, :]
    low[...] = work[...].astype(BF16)


def feed(sizes, hid_bias, vecs, weights, middle, low, acc):
    acc[...] = middle[...] + vecs[5:6, :]

    def block(i, _):
        hidden = dot_nt(low[...], sizes.expand_part(weights, i)) + hid_bias[i, 0:1, 0 : sizes.units]
        cdf, _ = normal_cdf(hidden)
        acc[...] += dot((hidden * cdf).astype(BF16), sizes.shrink_part(weights, i))
        return 0

    lax.fori_loop(0, sizes.shards, block, 0, unroll=4)


def column_sum(v):
    return jnp.sum(v, axis=0, keepdims=True)


def feed_both(sizes, hid_bias, vecs, weights, middle, low, glow, acc, back, dw, unit_sums):
    base, units = 4 * sizes.loc, sizes.units
    acc[...] = middle[...] + vecs[5:6, :]
    back[...] = jnp.zeros_like(back)

    def block(i, _):
        w_in, w_out = sizes.expand_part(weights, i), sizes.shrink_part(weights, i)
        hidden = dot_nt(low[...], w_in) + hid_bias[i, 0:1, 0 : sizes.units]
        cdf, bell = normal_cdf(hidden)
        active = (hidden * cdf).astype(BF16)
        grad = (dot_nt(glow[...], w_out) * (cdf + hidden * bell * DENSITY))
        unit_sums[i] += column_sum(grad)
        grad = grad.astype(BF16)
        acc[...] += dot(active, w_out)
        back[...] += dot(grad, w_in)
        dw[i, :, base : base + units] += dot_tn(low[...], grad)
        dw[i, :, base + units : base + 2 * units] += dot_tn(glow[...], active)
        return 0

    lax.fori_loop(0, sizes.shards, block, 0, unroll=2)


def backward(sizes, vecs, weights, xs, work, low, qkv, mixed, middle, glow, back, gmid, keep, dw, dbias, sums, between):
    width, groups = sizes.width, sizes.groups
    scale = HEAD ** (-0.5)
    gmix, dqkv = work, qkv
    for w in range(BATCH):
        hat, inv = normalize(middle[span(w), :])
        grad = back[span(w), :]
        sums[3:4, :] += column_sum(grad * hat)
        sums[4:5, :] += column_sum(grad)
        gmid[span(w), :] += norm_back(grad * vecs[3:4, :], hat, inv)
    branch = gmid[...].astype(BF16)
    sums[5:6, :] += column_sum(gmid[...])
    sizes.add_attention(dw, 3, dot_tn(branch, mixed[...].astype(BF16)))
    gmix[...] = dot_nt(branch, sizes.attention_part(weights, 3))
    between()

    def attend(w, _):
        row = span(w)
        for g in range(groups):
            col = g * LANES
            q = qkv[row, pl.ds(col, LANES)]
            k = qkv[row, pl.ds(width + col, LANES)]
            v = qkv[row, pl.ds(2 * width + col, LANES)]
            grad = gmix[row, pl.ds(col, LANES)]
            probs = keep[w * groups + g]
            wide_grad = dot(grad.astype(BF16), spread_columns(v))
            parts = []
            for h in range(PACK):
                p = probs[:, h * LANES : (h + 1) * LANES].astype(F32)
                t = wide_grad[:, h * LANES : (h + 1) * LANES]
                s = p * (t - jnp.sum(p * t, axis=-1, keepdims=True))
                dbias[g * PACK + h] += s
                parts.append(s)
            score = jnp.concatenate(parts, axis=1).astype(BF16)
            turned = pad_rows(q).T[:, :PAD].astype(BF16)
            dqkv[row, pl.ds(col, LANES)] = dot(score, spread_rows(k)) * scale
            dqkv[row, pl.ds(width + col, LANES)] = diagonal(dot(turned, score)).T[:PAD] * scale
            turned = pad_rows(grad).T[:, :PAD].astype(BF16)
            dqkv[row, pl.ds(2 * width + col, LANES)] = diagonal(dot(turned, probs)).T[:PAD]
        return 0

    lax.fori_loop(0, BATCH, attend, 0)
    for w in range(BATCH):
        hat, _ = normalize(xs[span(w), :])
        work[span(w), :] = hat * vecs[0:1, :] + vecs[1:2, :]
    low[...] = work[...].astype(BF16)
    back[...] = jnp.zeros_like(back)
    for c in range(3):
        at = slice(c * width, (c + 1) * width)
        grad = dqkv[:, at]
        if c != 1:
            sums[c // 2 : c // 2 + 1, :] += column_sum(grad)
        grad = grad.astype(BF16)
        back[...] += dot(grad, sizes.attention_part(weights, c))
        sizes.add_attention(dw, c, dot_tn(low[...], grad))
    for w in range(BATCH):
        hat, inv = normalize(xs[span(w), :])
        grad = back[span(w), :]
        sums[6:7, :] += column_sum(grad * hat)
        sums[7:8, :] += column_sum(grad)
        gmid[span(w), :] += norm_back(grad * vecs[0:1, :], hat, inv)


def live_scales(first, live):
    return [jnp.where(first + w < live[0], 1.0, 0.0).astype(F32) for w in range(BATCH)]


class Place:
    def __init__(self, mesh_shape):
        self.shards, self.n_dp = mesh_shape["mp"], mesh_shape["dp"]
        self.chips = self.n_dp // 2
        self.bits = int(math.log2(self.chips))
        self.dp, self.z = lax.axis_index("dp"), lax.axis_index("mp")
        self.core, self.chip = lax.rem(self.dp, 2), lax.div(self.dp, 2)
        self.bit_values = [lax.rem(lax.div(self.chip, 1 << b), 2) for b in range(self.bits)]
        self.flips = [
            self.chip + sum((1 << b) * (1 - 2 * self.bit_values[b]) for b in range(self.bits) if m >> b & 1)
            for m in range(self.chips)
        ]
        self.rounds = [lax.rem(self.z + k, self.shards) for k in range(self.shards)]

    def mate(self):
        return (self.dp + 1 - 2 * self.core, self.z)

    def flip(self, m):
        return self.flips[m]

    def across(self, m):
        return (2 * self.flip(m) + self.core, self.z)

    def bit(self, b):
        return self.bit_values[b]

    def along(self, k):
        return (self.dp, self.rounds[k])

    def greet(self, targets):
        barrier = pltpu.get_barrier_semaphore()
        for target in targets:
            pl.semaphore_signal(barrier, inc=1, device_id=target, device_id_type=MESH)
        pl.semaphore_wait(barrier, len(targets))

    def everyone(self):
        return (
            [self.mate()]
            + [self.across(m) for m in range(1, self.chips)]
            + [self.along(k) for k in range(1, self.shards)]
        )


def remote(source, target, sent, received, device):
    return pltpu.make_async_remote_copy(source, target, sent, received, device_id=device, device_id_type=MESH)


class Sends:
    def __init__(self):
        self.sent = []

    def send(self, make, when=None):
        self.sent.append((make, when))
        if when is None:
            make().start()
        else:
            pl.when(when())(lambda: make().start())

    def finish(self):
        for make, when in self.sent:
            if when is None:
                make().wait_send()
            else:
                pl.when(when())(lambda make=make: make().wait_send())


class Gather:
    def __init__(self, here, sends, out, parts, small, scratch):
        self.here, self.sends, self.out, self.parts, self.small = here, sends, out, parts, small
        self.z_sem, self.s_sem, self.p_sem, self.m_sem = scratch

    def spot(self, part, shard, dp):
        first, rows = self.parts[part]
        rows //= self.here.n_dp
        return self.out.at[shard, pl.ds(pl.multiple_of(first + dp * rows, 16), rows)]

    def origin(self, way, step):
        return jnp.clip(self.here.z - (1 - 2 * way) * step, 0, self.here.shards - 1)

    def there(self, way, step, reach=0):
        held, onward = self.here.z - (1 - 2 * way) * step, self.here.z + (1 - 2 * way) * reach
        return (held >= 0) & (held < self.here.shards) & (onward >= 0) & (onward < self.here.shards)

    def along(self, part, way, step, arriving=False):
        here = self.here
        spot = self.spot(part, self.origin(way, step), here.dp)
        at = step - 1 if arriving else step
        target = (here.dp, jnp.clip(here.z + 1 - 2 * way, 0, here.shards - 1))
        return remote(spot, spot, self.z_sem.at[0, part, way, at], self.z_sem.at[1, part, way, at], target)

    def along_send(self, part, way, step):
        self.sends.send(functools.partial(self.along, part, way, step), functools.partial(self.there, way, step, 1))

    def small_along(self, k, arriving=False):
        here = self.here
        spot = self.small.at[here.rounds[here.shards - k] if arriving else here.z]
        return remote(spot, spot, self.s_sem.at[0, k], self.s_sem.at[1, k], here.along(k))

    def start(self):
        for k in range(1, self.here.shards):
            self.sends.send(functools.partial(self.small_along, k))

    def wait_small(self):
        for k in range(1, self.here.shards):
            self.small_along(k, True).wait_recv()

    def start_part(self, part):
        for way in range(2):
            self.along_send(part, way, 0)

    def piece(self, part, way, step, m, core, side=None):
        spot = self.spot(part, self.origin(way, step), 2 * self.here.flip(m) + core)
        if side is None:
            return spot
        half = self.out.shape[2] // 2
        return spot.at[:, pl.ds(side * half, half)]

    def hop(self, part, way, step, m, side, bit, arriving=False):
        here = self.here
        spot = self.piece(part, way, step, m | bit if arriving else m, here.core, side)
        slot = (part, way, step, m | bit, side or 0)
        return remote(spot, spot, self.p_sem.at[0, *slot], self.p_sem.at[1, *slot], here.across(bit))

    def mate(self, part, way, step, m, side, arriving=False):
        here = self.here
        spot = self.piece(part, way, step, m, 1 - here.core if arriving else here.core, side)
        slot = (part, way, step, m, side or 0)
        return remote(spot, spot, self.m_sem.at[0, *slot], self.m_sem.at[1, *slot], here.mate())

    def both(self, step, body):
        for way in range(2):
            makes = []

            def run(way=way, makes=makes):
                for make in body(way):
                    if make is not None:
                        make().start()
                        makes.append(make)

            pl.when(self.there(way, step))(run)
            for make in makes:
                self.sends.sent.append((make, functools.partial(self.there, way, step)))

    def advance(self, part, step):
        for way in range(2):
            pl.when(self.there(way, step))(lambda way=way: self.along(part, way, step, True).wait_recv())
            if step < self.here.shards - 1:
                self.along_send(part, way, step)

        def body(way):
            for b in range(self.here.bits):
                yield functools.partial(self.hop, part, way, step, 0, None, 1 << b)
            yield functools.partial(self.mate, part, way, step, 0, None)

        self.both(step, body)

    def pieces(self):
        bits = self.here.bits
        orders = (tuple(range(bits)), tuple(reversed(range(bits))))
        for m in sorted(range(1, self.here.chips), key=lambda m: m.bit_count()):
            if m.bit_count() == 1:
                yield m, None, m, [(s, [1 << b for b in o[o.index(m.bit_length() - 1) + 1 :]]) for s, o in enumerate(orders)]
            else:
                for s, o in enumerate(orders):
                    last = max(o.index(b) for b in range(bits) if m >> b & 1)
                    yield m, s, 1 << o[last], [(s, [1 << b for b in o[last + 1 :]])]

    def relay(self, part, step, far):
        def body(way):
            for m, side, bit, onward in self.pieces():
                if (m.bit_count() > 1) != far:
                    continue
                self.hop(part, way, step, m - bit, side, bit, True).wait_recv()
                for s, later in onward:
                    for nxt in later:
                        yield functools.partial(self.hop, part, way, step, m, s, nxt)
                yield functools.partial(self.mate, part, way, step, m, side)

        self.both(step, body)

    def wait(self, part):
        for step in range(1, self.here.shards):

            def body(way, step=step):
                self.mate(part, way, step, 0, None, True).wait_recv()
                for m, side, _, _ in self.pieces():
                    self.mate(part, way, step, m, side, True).wait_recv()
                return ()

            self.both(step, body)


def gather_scratch(mesh_shape, parts):
    shards, chips = mesh_shape["mp"], mesh_shape["dp"] // 2
    dma = pltpu.SemaphoreType.DMA
    return [
        dma((2, parts, 2, shards)),
        dma((2, shards)),
        dma((2, parts, 2, shards, chips, 2)),
        dma((2, parts, 2, shards, chips, 2)),
    ]


class Lines:
    def __init__(self, here, sends, source, target, sem, reach):
        self.here, self.sends, self.source, self.target, self.sem, self.reach = here, sends, source, target, sem, reach

    def block(self, z, c):
        chunks = self.source.shape[0]
        return self.target.at[pl.ds(pl.multiple_of((z * chunks + c) * CHUNK, 16), CHUNK)]

    def local(self, c):
        return pltpu.make_async_copy(self.source.at[c], self.block(self.here.z, c), self.sem.at[0, c, 0, self.reach])

    def copy(self, c, way, step, reach, arriving=False):
        here, sign = self.here, 1 - 2 * way
        held = jnp.clip(here.z - sign * step, 0, here.shards - 1)
        at = step - 1 if arriving else step + reach - 1
        source = self.source.at[c] if step == 0 else self.block(held, c)
        target = (here.dp, jnp.clip(here.z + sign * reach, 0, here.shards - 1))
        return remote(source, self.block(held, c), self.sem.at[0, c, way, at], self.sem.at[1, c, way, at], target)

    def there(self, way, step, reach):
        here, sign = self.here, 1 - 2 * way
        held, onward = here.z - sign * step, here.z + sign * reach
        return (held >= 0) & (held < here.shards) & (onward >= 0) & (onward < here.shards)

    def send(self, c, step, reach):
        for way in range(2):
            self.sends.send(
                functools.partial(self.copy, c, way, step, reach), functools.partial(self.there, way, step, reach)
            )

    def start(self, c):
        for reach in range(1, min(2, self.reach) + 1):
            self.send(c, 0, reach)

    def arrive(self, c, step):
        for way in range(2):
            pl.when(self.there(way, step, 0))(lambda way=way: self.copy(c, way, step, 1, True).wait_recv())

    def forward(self, c, step):
        self.arrive(c, step)
        self.send(c, step, 1)


class Reduction:
    def __init__(self, here, sends, dw, final, span, scratch):
        (self.acc, self.half, self.parts, self.lasts, self.h_sem, self.q_sem, self.l_sem, self.f_sem, self.g_sem) = scratch
        self.dw, self.final, self.here, self.sends = dw, final, here, sends
        self.d = dw.shape[1]
        self.first, self.columns = span
        split = self.columns // 2
        self.sides = (pl.ds(0, split), pl.ds(split, split))
        self.orders = (tuple(range(here.bits)), tuple(reversed(range(here.bits))))

    def send(self, make):
        self.sends.send(make)

    def rows_of(self, side, core, chip_bit, depth):
        size = self.d // 2
        first = core * size
        for b in self.orders[side][:depth]:
            size //= 2
            first = first + chip_bit(b) * size
        return pl.ds(pl.multiple_of(first, 16), size)

    def half_rows(self, core):
        return pl.ds(pl.multiple_of(core * (self.d // 2), 16), self.d // 2)

    def half_copy(self, s):
        rows = self.half_rows(1 - self.here.core)
        return remote(self.acc.at[s, rows], self.half.at[s], self.h_sem.at[0, s], self.h_sem.at[1, s], self.here.mate())

    def half_send(self, s):
        rows = self.half_rows(1 - self.here.core)
        self.acc[s, rows, :] = self.dw[s, rows, pl.ds(self.first, self.columns)].astype(BF16)
        self.send(functools.partial(self.half_copy, s))

    def half_add(self, s):
        self.half_copy(s).wait_recv()
        mine = self.half_rows(self.here.core)
        self.acc[s, mine, :] = (self.dw[s, mine, pl.ds(self.first, self.columns)] + self.half[s].astype(F32)).astype(BF16)

    def plane_copy(self, s, depth, side):
        here = self.here
        b = self.orders[side][depth]
        rows = self.rows_of(side, here.core, lambda c: 1 - here.bit(c) if c == b else here.bit(c), depth + 1)
        target = self.parts[side][depth].at[s]
        sems = self.q_sem
        return remote(
            self.acc.at[s, rows, self.sides[side]], target, sems.at[0, side, depth, s], sems.at[1, side, depth, s], here.across(1 << b)
        )

    def plane_send(self, s, depth):
        for side in range(2):
            self.send(functools.partial(self.plane_copy, s, depth, side))

    def plane_add(self, s, depth):
        for side in range(2):
            self.plane_copy(s, depth, side).wait_recv()
            rows = self.rows_of(side, self.here.core, self.here.bit, depth + 1)
            arrived = self.parts[side][depth][s]
            here = self.acc[s, rows, self.sides[side]]
            self.acc[s, rows, self.sides[side]] = (here.astype(F32) + arrived.astype(F32)).astype(BF16)

    def mine(self, side):
        return self.rows_of(side, self.here.core, self.here.bit, self.here.bits)

    def shard_copy(self, side, k):
        here = self.here
        s = here.rounds[k]
        return remote(
            self.acc.at[s, self.mine(side), self.sides[side]], self.lasts[side].at[k], self.l_sem.at[0, side, k], self.l_sem.at[1, side, k], here.along(k)
        )

    def shard_sends(self):
        for k in range(1, self.here.shards):
            for side in range(2):
                self.send(functools.partial(self.shard_copy, side, k))

    def shard_adds(self):
        for side in range(2):
            rows = self.mine(side)
            total = self.acc[self.here.z, rows, self.sides[side]].astype(F32)
            for k in range(1, self.here.shards):
                self.shard_copy(side, k).wait_recv()
                total = total + self.lasts[side][k].astype(F32)
            self.final[rows, self.final_side(side)] = total.astype(BF16)

    def final_side(self, side):
        split = self.columns // 2
        return pl.ds(self.first + side * split, split)

    def final_spot(self, side, m, core):
        here = self.here
        rows = self.rows_of(side, core, lambda b: 1 - here.bit(b) if m >> b & 1 else here.bit(b), here.bits)
        return self.final.at[rows, self.final_side(side)]

    def final_copy(self, side, m, arriving=False):
        here = self.here
        spot = self.final_spot(side, m if arriving else 0, here.core)
        return remote(spot, spot, self.f_sem.at[0, side, m], self.f_sem.at[1, side, m], here.across(m))

    def final_relay(self, side, m, arriving=False):
        here = self.here
        spot = self.final_spot(side, m, 1 - here.core if arriving else here.core)
        return remote(spot, spot, self.g_sem.at[0, side, m], self.g_sem.at[1, side, m], here.mate())

    def final_spread(self):
        for side in range(2):
            for m in range(1, self.here.chips):
                self.send(functools.partial(self.final_copy, side, m))
            self.send(functools.partial(self.final_relay, side, 0))

    def final_relays(self):
        for side in range(2):
            for m in range(1, self.here.chips):
                self.final_copy(side, m, True).wait_recv()
                self.send(functools.partial(self.final_relay, side, m))

    def final_wait(self):
        for side in range(2):
            for m in range(self.here.chips):
                self.final_relay(side, m, True).wait_recv()

    def start(self):
        for s in range(self.here.shards):
            self.half_send(s)

    def plane(self, depth):
        for s in range(self.here.shards):
            if depth == 0:
                self.half_add(s)
            else:
                self.plane_add(s, depth - 1)
            if depth < self.here.bits:
                self.plane_send(s, depth)
        if depth == self.here.bits:
            self.shard_sends()

    def close(self):
        self.shard_adds()
        self.final_spread()


def reduce_scratch(mesh_shape, d, columns):
    shards, chips = mesh_shape["mp"], mesh_shape["dp"] // 2
    bits = int(math.log2(chips))
    split, finish = columns // 2, d // (2 * chips)
    dma = pltpu.SemaphoreType.DMA
    return [
        pltpu.VMEM((shards, d, columns), BF16),
        pltpu.VMEM((shards, d // 2, columns), BF16),
        [[pltpu.VMEM((shards, d >> (depth + 2), split), BF16) for depth in range(bits)]] * 2,
        [pltpu.VMEM((shards, finish, split), BF16)] * 2,
        dma((2, shards)),
        dma((2, 2, bits, shards)),
        dma((2, 2, shards)),
        dma((2, 2, chips)),
        dma((2, 2, chips)),
    ]


class Totals:
    def __init__(self, here, sends, out, scratch):
        self.here, self.sends, self.small_out = here, sends, out
        self.sums, self.sums_in, self.t_sem = scratch
        self.stages = here.bits + 1

    def send(self, make):
        self.sends.send(make)

    def small_copy(self, i):
        here = self.here
        target = here.mate() if i == 0 else here.across(1 << (i - 1))
        return remote(self.sums.at[i], self.sums_in.at[i], self.t_sem.at[0, i], self.t_sem.at[1, i], target)

    def small_send(self, i):
        self.send(functools.partial(self.small_copy, i))

    def small_add(self, i):
        self.small_copy(i).wait_recv()
        self.sums[i + 1] = self.sums[i] + self.sums_in[i]

    def small_along(self, k):
        slot = self.stages + k - 1
        return remote(
            self.sums.at[self.stages], self.sums_in.at[slot], self.t_sem.at[0, slot], self.t_sem.at[1, slot], self.here.along(k)
        )

    def small_sends(self):
        for k in range(1, self.here.shards):
            self.send(functools.partial(self.small_along, k))

    def small_total(self):
        total = self.sums[self.stages]
        for k in range(1, self.here.shards):
            self.small_along(k).wait_recv()
            total = total + self.sums_in[self.stages + k - 1]
        self.small_out[...] = total


def totals_scratch(mesh_shape, shape):
    shards, chips = mesh_shape["mp"], mesh_shape["dp"] // 2
    bits = int(math.log2(chips))
    return [
        pltpu.VMEM((bits + 2, *shape), F32),
        pltpu.VMEM((bits + shards, *shape), F32),
        pltpu.SemaphoreType.DMA((2, bits + shards)),
    ]


TALL = 384
BLOCK = 8


def one_hot(index_row):
    return (lax.broadcasted_iota(jnp.int32, (TALL, LANES), 0) == index_row).astype(F32).astype(BF16)


def build_bias(index, table, bias):
    heads = table.shape[0]
    tall = jnp.broadcast_to(table[:, None, :], (heads, BLOCK, TALL)).reshape(heads * BLOCK, TALL).astype(BF16)
    row = lax.rem(lax.broadcasted_iota(jnp.int32, (heads * BLOCK, LANES), 0), BLOCK)
    blocked = jnp.where(lax.broadcasted_iota(jnp.int32, (heads * BLOCK, LANES), 1) < AREA, 0.0, -1e30)

    def block(r, _):
        at = pl.ds(pl.multiple_of(r * BLOCK, BLOCK), BLOCK)
        rows = index[at, :]
        out = blocked
        for i in range(BLOCK):
            values = dot(tall, one_hot(rows[i : i + 1, :]))
            out = jnp.where(row == i, values * LOG2E + blocked, out)
        bias[:, at, :] = out.reshape(heads, BLOCK, LANES)
        return 0

    lax.fori_loop(0, PAD // BLOCK, block, 0)


def sum_table(index, dbias, turned):
    heads = dbias.shape[0]
    row = lax.rem(lax.broadcasted_iota(jnp.int32, (heads * BLOCK, LANES), 0), BLOCK)
    turned[...] = jnp.zeros_like(turned)

    def block(r, _):
        at = pl.ds(pl.multiple_of(r * BLOCK, BLOCK), BLOCK)
        rows = index[at, :]
        values = dbias[:, at, :].reshape(heads * BLOCK, LANES)
        left = jnp.concatenate([one_hot(rows[i : i + 1, :]) for i in range(BLOCK)], axis=1)
        right = jnp.concatenate([jnp.where(row == i, values, 0.0) for i in range(BLOCK)], axis=1).astype(BF16)
        turned[...] += dot_nt(left, right)
        return 0

    lax.fori_loop(0, PAD // BLOCK, block, 0)


def block_kernel(sizes, mesh_shape, exchange, early, live, offsets, singles, pair, table_in, unit_in, tokens, cotangent,
                 triple_in, output_in, expand_in, shrink_in,
                 result, gtok, final, small_out,
                 index, vecs, saved, weights, smalls, wide_bias, bias, dbias, dw, xs, qkv, mixed, middle, keep,
                 wide, work, low, glow, back, gmid, sums, unit_sums, turned,
                 tok_in, cot_in, rows_in, rows_out,
                 own_sem, tok_sem, cot_sem, in_sem, out_sem, result_sem, gtok_sem,
                 gather_refs, feed_refs, attn_refs, total_refs):
    here = Place(mesh_shape)
    sends = Sends()
    own_out, own_grad = tok_in, cot_in
    shards, own = sizes.shards, tok_in.shape[0]
    chunks = shards * own
    loc, units = sizes.loc, sizes.units
    gather = Gather(here, sends, weights, ((0, 4 * loc), (4 * loc, 2 * units)), smalls, gather_refs)
    feed_sum = Reduction(here, sends, dw, final, (4 * loc, 2 * units), feed_refs)
    attn_sum = Reduction(here, sends, dw, final, (0, 4 * loc), attn_refs)
    totals = Totals(here, sends, small_out, total_refs)
    results = Lines(here, sends, own_out, result, result_sem, 1)
    grads = Lines(here, sends, own_grad, gtok, gtok_sem, shards - 1)

    def own_rows(c):
        return pl.ds(pl.multiple_of((here.z * own + c) * CHUNK, 16), CHUNK)

    def own_tokens(c):
        return pltpu.make_async_copy(tokens.at[own_rows(c)], tok_in.at[c], tok_sem.at[c])

    def own_cotangent(c):
        return pltpu.make_async_copy(cotangent.at[own_rows(c)], cot_in.at[c], cot_sem.at[c])

    mine = [
        pltpu.make_async_copy(output_in, weights.at[here.z, pl.ds(3 * loc, loc)], own_sem.at[0]),
        pltpu.make_async_copy(shrink_in, weights.at[here.z, pl.ds(4 * loc + units, units)], own_sem.at[1]),
    ]
    for copy in mine:
        copy.start()
    for c in range(own):
        own_tokens(c).start()
    for c in range(own):
        own_cotangent(c).start()
    for c in range(3):
        weights[here.z, c * loc : (c + 1) * loc, :] = triple_in[c].astype(F32).T.astype(BF16)
    heads = sizes.width // HEAD
    count = heads // shards
    smalls[here.z, 0:1, 0:units] = unit_in[...].astype(F32).reshape(1, units)
    smalls[here.z, 1:2, 0:loc] = pair[0:1, :].astype(F32)
    smalls[here.z, 1:2, loc : 2 * loc] = pair[1:2, :].astype(F32)
    smalls[here.z, 2 : 2 + count, 0:TALL] = jnp.zeros((count, TALL), F32)
    smalls[here.z, 2 : 2 + count, 0 : table_in.shape[1]] = table_in[...].astype(F32)
    here.greet(here.everyone())
    mine[0].wait()
    gather.start_part(0)
    gather.start()
    weights[here.z, 4 * loc : 4 * loc + units, :] = expand_in[...].astype(F32).T.astype(BF16)
    mine[1].wait()
    index[...] = jnp.full(index.shape, -1, jnp.int32)
    index[0:AREA, 0:AREA] = offsets[...]
    for line, single in enumerate(singles):
        vecs[line : line + 1, :] = single[...].astype(F32).reshape(1, vecs.shape[1])
    steps = range(1, shards)
    for step in steps:
        gather.advance(0, step)
        if step == 1:
            gather.start_part(1)
    for step in steps:
        gather.relay(0, step, False)
    gather.advance(1, 1)
    xs[...] = jnp.zeros_like(xs)
    dbias[...] = jnp.zeros_like(dbias)
    sums[...] = jnp.zeros_like(sums)
    unit_sums[...] = jnp.zeros_like(unit_sums)
    gather.wait_small()
    for z in range(shards):
        at = slice(z * loc, (z + 1) * loc)
        wide_bias[:, at] = smalls[z, 1:2, 0:loc]
        wide_bias[:, slice(2 * sizes.width + z * loc, 2 * sizes.width + (z + 1) * loc)] = smalls[z, 1:2, loc : 2 * loc]
    wide_bias[:, sizes.width : 2 * sizes.width] = jnp.zeros((1, sizes.width), F32)
    table = jnp.concatenate([smalls[z, 2 : 2 + count, 0:TALL] for z in range(shards)], axis=0)
    build_bias(index, table, bias)
    for step in steps:
        gather.relay(0, step, True)
    for step in steps[1:-1]:
        gather.advance(1, step)
    gather.wait(0)
    jobs = {}
    if shards > 2:
        jobs.setdefault(0, []).append(functools.partial(gather.advance, 1, shards - 1))
    for step in steps:
        at = min((step - 1) // 2, 2 * own - 2)
        jobs.setdefault(at, []).append(functools.partial(gather.relay, 1, step, False))
        jobs.setdefault(at + 1, []).append(functools.partial(gather.relay, 1, step, True))

    extra = chunks - own
    before = jnp.int32(0)
    if exchange == own:
        before = jnp.maximum(here.z - 1, 0) * own
        after = jnp.maximum(shards - 2 - here.z, 0) * own
        extras, most = before + after, extra - own

        def chunk_of(i):
            return jnp.where(i < before, i, i - before + (here.z + 2) * own)
    else:
        extras, most = jnp.int32(extra), extra

        def chunk_of(i):
            return lax.rem((here.z + 1) * own + i, chunks)

    def rows(i):
        return pl.ds(pl.multiple_of(chunk_of(i) * CHUNK, 16), CHUNK)

    def fetch(i):
        return pltpu.make_async_copy(tokens.at[rows(i)], rows_in.at[lax.rem(i, 2)], in_sem.at[lax.rem(i, 2)])

    def put(i):
        return pltpu.make_async_copy(rows_out.at[lax.rem(i, 2)], result.at[rows(i)], out_sem.at[lax.rem(i, 2)])

    def attend(c, _):
        own_tokens(c).wait()
        load_rows(tok_in[c], wide, xs.at[c])

        def relays(point):
            for at in sorted(jobs):
                if at % 2 == point:

                    def run(at=at):
                        for job in jobs[at]:
                            job()

                    pl.when(c == at // 2)(run)

        attention(
            sizes, bias, vecs, wide_bias, weights, xs.at[c], work, low, qkv.at[c], mixed.at[c], middle.at[c], keep.at[c],
            functools.partial(relays, 0),
        )
        relays(1)
        return 0

    lax.fori_loop(0, own, attend, 0)
    def clear(z, _):
        dw[z] = jnp.zeros_like(dw[z])
        return 0

    lax.fori_loop(0, shards, clear, 0)


    if early:
        first = dw.at[0, pl.ds(0, ROWS)], dw.at[1, pl.ds(0, ROWS), pl.ds(0, 512)], dw.at[1, pl.ds(0, ROWS), pl.ds(512, 512)]

        def ahead(e, _):
            at = most - early + e
            fetch(at).start()
            fetch(at).wait()
            load_rows(rows_in[lax.rem(at, 2)], wide, first[1])
            attention(sizes, bias, vecs, wide_bias, weights, first[1], work, low, first[0], first[2], saved.at[e], None)
            return 0

        lax.fori_loop(0, early, ahead, 0)
        for z in range(2):
            dw[z] = jnp.zeros_like(dw[z])
    gather.wait(1)

    def finish(c, _):
        scales = live_scales((here.z * own + c) * BATCH, live)
        own_cotangent(c).wait()
        second_norm(vecs, middle.at[c], work, low)
        wide[...] = cot_in[c].astype(F32)
        for w in range(BATCH):
            gmid[w * PAD : w * PAD + AREA, :] = wide[w * AREA : (w + 1) * AREA, :] * scales[w]
            gmid[w * PAD + AREA : (w + 1) * PAD, :] = jnp.zeros((PAD - AREA, gmid.shape[1]), F32)
        sums[2:3, :] += column_sum(gmid[...])
        glow[...] = gmid[...].astype(BF16)
        feed_both(sizes, smalls, vecs, weights, middle.at[c], low, glow, work, back, dw, unit_sums)
        store_rows(work, wide, own_out.at[c], scales)
        for i in range(own):

            def fed(i=i):
                results.local(i).start()
                if i < exchange:
                    results.start(i)
                if i == own - 1:
                    feed_sum.start()

            pl.when(c == i)(fed)

        def between():
            pl.when(c == own - 1)(lambda: feed_sum.plane(0))

        backward(sizes, vecs, weights, xs.at[c], work, low, qkv.at[c], mixed.at[c], middle.at[c], glow, back, gmid, keep.at[c], dw, dbias, sums, between)
        store_rows(gmid, wide, own_grad.at[c])
        for i in range(own):

            def done(i=i):
                grads.local(i).start()
                grads.send(i, 0, 1)
                grads.send(i, 0, 2)

            pl.when(c == i)(done)
        return 0

    lax.fori_loop(0, own, finish, 0)
    attn_sum.start()
    sum_table(index, dbias, turned)
    table = turned[...].T
    total = totals.sums
    total[0, 0:8, :] = sums[...]
    for z in range(shards):
        at = z * units % sizes.width
        line = 8 + z * units // sizes.width
        total[0, line : line + 1, at : at + units] = unit_sums[z]
    base = 8 + shards * units // sizes.width
    total[0, base : base + heads, 0:TALL] = jnp.sum(table.reshape(heads, BLOCK, TALL), axis=1)
    totals.small_send(0)

    pl.when(extras > 0)(lambda: fetch(0).start())
    bits = here.bits
    points = 2 * most
    moves = {p: [] for p in range(points + 1)}

    def place(p, step):
        moves[max(0, min(p, points))].append(step)

    place(0, functools.partial(attn_sum.plane, 0))
    for depth in range(1, bits + 1):
        place(3 * depth - 2, functools.partial(feed_sum.plane, depth))
        place(3 * depth - 1, functools.partial(attn_sum.plane, depth))
    for i in range(totals.stages):

        def small_step(i=i):
            totals.small_add(i)
            if i + 1 < totals.stages:
                totals.small_send(i + 1)
            else:
                totals.small_sends()

        place(2 * i + 1, small_step)
    for n in range(2, shards - 1):
        for c in range(own):
            place(2 * n - 2 + 8 * c, functools.partial(grads.forward, c, n))
    place(points - 4, feed_sum.close)
    place(points - 2, feed_sum.final_relays)
    place(points - 2, attn_sum.close)

    def run(i, half):
        for at in range(points):
            if at % 2 == half and moves[at]:

                def go(at=at):
                    for move in moves[at]:
                        move()

                pl.when(i == at // 2)(go)

    states = (xs.at[0], work, low, qkv.at[0], mixed.at[0], middle.at[0])

    def other(i, _):
        @pl.when(i < extras - early)
        def _():
            fetch(i).wait()
            pl.when(i + 1 < extras - early)(lambda: fetch(i + 1).start())
            load_rows(rows_in[lax.rem(i, 2)], wide, xs.at[0])
            attention(sizes, bias, vecs, wide_bias, weights, *states, None)

        run(i, 0)
        if early:

            @pl.when(i >= most - early)
            def _():
                middle[0] = saved[i - (most - early)]

        @pl.when(i < extras)
        def _():
            second_norm(vecs, middle.at[0], work, low)
            feed(sizes, smalls, vecs, weights, middle.at[0], low, work)
            pl.when(i >= 2)(lambda: put(i - 2).wait())
            store_rows(work, wide, rows_out.at[lax.rem(i, 2)], live_scales(chunk_of(i) * BATCH, live))
            put(i).start()

        run(i, 1)
        return 0

    lax.fori_loop(0, most, other, 0)
    for move in moves[points]:
        move()
    attn_sum.final_relays()
    totals.small_total()
    for c in range(exchange):
        results.arrive(c, 1)
    for c in range(own):
        for n in range(1, shards):
            if n < 2 or n == shards - 1:
                grads.arrive(c, n)
    attn_sum.final_wait()
    feed_sum.final_wait()
    sends.finish()
    for c in range(own):
        results.local(c).wait()
        grads.local(c).wait()
    for back_by in (2, 1):
        pl.when(extras >= back_by)(lambda back_by=back_by: put(extras - back_by).wait())


def run_block(sizes, mesh_shape, exchange, early, live, offsets, singles, pair, table, unit, tokens, cotangent, *raw):
    d = tokens.shape[1]
    shards, width, units, groups = sizes.shards, sizes.width, sizes.units, sizes.groups
    heads = width // HEAD
    own = tokens.shape[0] // CHUNK // shards
    anywhere = pl.BlockSpec(memory_space=pl.ANY)
    here = pl.BlockSpec(memory_space=pltpu.VMEM)
    dma = pltpu.SemaphoreType.DMA
    total_shape = (8 + shards * units // d + heads, d)
    return pl.pallas_call(
        functools.partial(block_kernel, sizes, mesh_shape, exchange, early),
        out_shape=(
            jax.ShapeDtypeStruct(tokens.shape, BF16),
            jax.ShapeDtypeStruct(tokens.shape, BF16),
            jax.ShapeDtypeStruct((d, sizes.columns), BF16),
            jax.ShapeDtypeStruct(total_shape, F32),
        ),
        in_specs=[pl.BlockSpec(memory_space=pltpu.SMEM), here, [here] * 6, here, here, here, anywhere, anywhere, here, anywhere, here, anywhere],
        out_specs=(anywhere, anywhere, here, here),
        scratch_shapes=[
            pltpu.VMEM((PAD, LANES), jnp.int32),
            pltpu.VMEM((8, d), F32),
            pltpu.VMEM((max(early, 1), ROWS, d) if early else (1, 8, LANES), F32),
            pltpu.VMEM((shards, sizes.columns, d), BF16),
            pltpu.VMEM((shards, 8, d), F32),
            pltpu.VMEM((1, 3 * width), F32),
            pltpu.VMEM((heads, PAD, LANES), F32),
            pltpu.VMEM((heads, PAD, LANES), F32),
            pltpu.VMEM((shards, d, sizes.columns), F32),
            pltpu.VMEM((own, ROWS, d), F32),
            pltpu.VMEM((own, ROWS, 3 * width), F32),
            pltpu.VMEM((own, ROWS, width), F32),
            pltpu.VMEM((own, ROWS, d), F32),
            pltpu.VMEM((own, BATCH * groups, PAD, PACK * LANES), BF16),
            pltpu.VMEM((CHUNK, d), F32),
            pltpu.VMEM((ROWS, d), F32),
            pltpu.VMEM((ROWS, d), BF16),
            pltpu.VMEM((ROWS, d), BF16),
            pltpu.VMEM((ROWS, d), F32),
            pltpu.VMEM((ROWS, d), F32),
            pltpu.VMEM((8, d), F32),
            pltpu.VMEM((shards, 1, units), F32),
            pltpu.VMEM((TALL, heads * BLOCK), F32),
            pltpu.VMEM((own, CHUNK, d), BF16),
            pltpu.VMEM((own, CHUNK, d), BF16),
            pltpu.VMEM((2, CHUNK, d), BF16),
            pltpu.VMEM((2, CHUNK, d), BF16),
            dma((2,)),
            dma((own,)),
            dma((own,)),
            dma((2,)),
            dma((2,)),
            dma((2, own, 2, 2)),
            dma((2, own, 2, shards)),
            gather_scratch(mesh_shape, 2),
            reduce_scratch(mesh_shape, d, 2 * units),
            reduce_scratch(mesh_shape, d, 4 * sizes.loc),
            totals_scratch(mesh_shape, total_shape),
        ],
        compiler_params=pltpu.CompilerParams(collective_id=0, has_side_effects=True, vmem_limit_bytes=VMEM_LIMIT),
    )(live, offsets, singles, pair, table, unit, tokens, cotangent, *raw)


def finish_kernel(sizes, z, final, packed, *refs):
    triple, output, expand, shrink, pair, table, unit, *singles = refs
    loc, units = sizes.loc, sizes.units
    d = final.shape[0]
    count = sizes.width // HEAD // sizes.shards
    for c in range(3):
        triple[c] = final[:, c * loc : (c + 1) * loc].astype(F32)
    output[...] = final[:, 3 * loc : 4 * loc].astype(F32).T
    expand[...] = final[:, 4 * loc : 4 * loc + units].astype(F32)
    shrink[...] = final[:, 4 * loc + units :].astype(F32).T
    base = 8 + sizes.shards * units // d
    for s in range(sizes.shards):

        def take(s=s):
            pair[...] = packed[0:2, s * loc : (s + 1) * loc]
            table[...] = packed[base + s * count : base + (s + 1) * count, 0 : table.shape[1]]
            at = s * units % d
            line = 8 + s * units // d
            unit[...] = packed[line : line + 1, at : at + units]

        pl.when(z[0] == s)(take)
    for ref, line in zip(singles, (6, 7, 5, 3, 4, 2)):
        ref[...] = packed[line : line + 1, :]


def run_finish(sizes, table_rows, z, final, packed):
    loc, units, d = sizes.loc, sizes.units, final.shape[0]
    count = sizes.width // HEAD // sizes.shards
    shapes = [(3, d, loc), (loc, d), (d, units), (units, d), (2, loc), (count, table_rows), (1, units)] + [(1, d)] * 6
    here = pl.BlockSpec(memory_space=pltpu.VMEM)
    return pl.pallas_call(
        functools.partial(finish_kernel, sizes),
        out_shape=tuple(jax.ShapeDtypeStruct(shape, F32) for shape in shapes),
        in_specs=[pl.BlockSpec(memory_space=pltpu.SMEM), here, here],
        out_specs=tuple([here] * len(shapes)),
        compiler_params=pltpu.CompilerParams(vmem_limit_bytes=VMEM_LIMIT),
    )(z, final, packed)


def local(
    mesh_shape,
    tokens,
    cotangent,
    group_windows,
    offset_index,
    first_gain,
    first_shift,
    triple_weight,
    query_value_bias,
    bias_table,
    output_weight,
    output_bias,
    second_gain,
    second_shift,
    expand_weight,
    expand_bias,
    shrink_weight,
    shrink_bias,
):
    z = lax.axis_index("mp")
    shards = mesh_shape["mp"]
    d, _, loc = triple_weight.shape
    units = expand_weight.shape[1]
    table_rows, loc_heads = bias_table.shape
    heads = shards * loc_heads
    sizes = Sizes(shards, loc, units)
    early = EARLY if sizes.columns == 3 * sizes.width else 0
    singles = [first_gain, first_shift, output_bias, second_gain, second_shift, shrink_bias]
    result, grad_tokens, final, packed = run_block(
        sizes,
        mesh_shape,
        EXCHANGE,
        early,
        group_windows,
        offset_index,
        singles,
        query_value_bias,
        bias_table.T,
        expand_bias,
        tokens,
        cotangent,
        triple_weight.transpose(1, 0, 2),
        output_weight,
        expand_weight,
        shrink_weight,
    )
    triple, output, expand, shrink, pair, table, unit, *singles = run_finish(sizes, table_rows, z.reshape(1), final, packed)
    first_gain, first_shift, output_sum, second_gain, second_shift, shrink_sum = (v.reshape(d) for v in singles)
    return (
        result,
        grad_tokens,
        first_gain,
        first_shift,
        triple.transpose(1, 0, 2),
        pair,
        table.T,
        output,
        output_sum,
        second_gain,
        second_shift,
        expand,
        unit.reshape(units),
        shrink,
        shrink_sum,
    )


EXCHANGE = 0
EARLY = 0


def solution(mesh):
    in_specs = (
        P("dp", None),
        P("dp", None),
        P("dp"),
        P(),
        P(),
        P(),
        P(None, None, "mp"),
        P(None, "mp"),
        P(None, "mp"),
        P("mp", None),
        P(),
        P(),
        P(),
        P(None, "mp"),
        P("mp"),
        P("mp", None),
        P(),
    )
    out_specs = (
        P("dp", None),
        P("dp", None),
        P(),
        P(),
        P(None, None, "mp"),
        P(None, "mp"),
        P(None, "mp"),
        P("mp", None),
        P(),
        P(),
        P(),
        P(None, "mp"),
        P("mp"),
        P("mp", None),
        P(),
    )
    step = functools.partial(local, dict(mesh.shape))
    return jax.shard_map(step, mesh=mesh, in_specs=in_specs, out_specs=out_specs, check_vma=False)
```

```python
import functools
import math
import jax
import jax.numpy as jnp
from jax import lax
from jax.experimental import pallas as pl
from jax.experimental.pallas import tpu as pltpu
from jax.sharding import PartitionSpec as P

AREA = 100
PAD = 104
HEAD = 32
LANES = 128
PACK = LANES // HEAD
BATCH = 4
CHUNK = BATCH * AREA
ROWS = BATCH * PAD
EPSILON = 1e-05
DENSITY = 0.3989422804014327
LOG2E = 1.4426950408889634
F32 = jnp.float32
BF16 = jnp.bfloat16
MESH = pl.DeviceIdType.MESH
VMEM_LIMIT = 63 * 2**20


def dot(a, b):
    return jnp.dot(a, b, preferred_element_type=F32)


def dot_nt(a, b):
    return lax.dot_general(a, b, (((1,), (1,)), ((), ())), preferred_element_type=F32)


def dot_tn(a, b):
    return lax.dot_general(a, b, (((0,), (0,)), ((), ())), preferred_element_type=F32)


def normalize(values):
    centered = values - jnp.mean(values, axis=-1, keepdims=True)
    inv = lax.rsqrt(jnp.mean(centered * centered, axis=-1, keepdims=True) + EPSILON)
    return centered * inv, inv


def norm_back(grad, hat, inv):
    return inv * (
        grad
        - jnp.mean(grad, axis=-1, keepdims=True)
        - hat * jnp.mean(grad * hat, axis=-1, keepdims=True)
    )


def normal_cdf(hidden):
    bell = jnp.exp2(hidden * hidden * (-0.5 * LOG2E))
    return 0.5 + 0.5 * lax.erf(hidden * 0.7071067811865476), bell


def head_of(shape, axis):
    return lax.broadcasted_iota(jnp.int32, shape, axis) // HEAD


def pad_rows(v):
    return jnp.concatenate([v, jnp.zeros((LANES - PAD, v.shape[1]), v.dtype)], axis=0)


def spread_rows(v):
    head = head_of((LANES, LANES), 1)
    full = pad_rows(v)
    return jnp.concatenate([jnp.where(head == h, full, 0.0) for h in range(PACK)], axis=0).astype(BF16)


def spread_columns(v):
    head = head_of((LANES, LANES), 0)
    turned = pad_rows(v).T
    return jnp.concatenate([jnp.where(head == h, turned, 0.0) for h in range(PACK)], axis=1).astype(BF16)


def diagonal(full):
    head = head_of((LANES, LANES), 0)
    out = full[:, 0:LANES]
    for h in range(1, PACK):
        out = jnp.where(head == h, full[:, h * LANES : (h + 1) * LANES], out)
    return out


def span(w, size=PAD):
    return pl.ds(pl.multiple_of(w * PAD, 8), size)


def load_rows(source, wide, padded):
    wide[...] = source.astype(F32)
    for w in range(BATCH):
        padded[w * PAD : w * PAD + AREA, :] = wide[w * AREA : (w + 1) * AREA, :]


def store_rows(padded, wide, target, scales=None):
    for w in range(BATCH):
        rows = padded[w * PAD : w * PAD + AREA, :]
        wide[w * AREA : (w + 1) * AREA, :] = rows if scales is None else rows * scales[w]
    target[...] = wide[...].astype(BF16)


class Sizes:
    def __init__(self, shards, loc, units):
        self.shards, self.loc, self.units = shards, loc, units
        self.width = shards * loc
        self.groups = self.width // LANES
        self.columns = 4 * loc + 2 * units

    def attention_part(self, weights, c):
        at = slice(c * self.loc, (c + 1) * self.loc)
        return jnp.concatenate([weights[z, at, :] for z in range(self.shards)], axis=0)

    def expand_part(self, weights, i):
        return weights[i, pl.ds(4 * self.loc, self.units), :]

    def shrink_part(self, weights, i):
        return weights[i, pl.ds(4 * self.loc + self.units, self.units), :]

    def add_attention(self, dw, c, value):
        for z in range(self.shards):
            at = slice(c * self.loc, (c + 1) * self.loc)
            dw[z, :, at] += value[:, z * self.loc : (z + 1) * self.loc]


def attention(sizes, bias, vecs, wide_bias, weights, xs, work, low, qkv, mixed, middle, keep, between=None):
    width, groups = sizes.width, sizes.groups
    scale = HEAD ** (-0.5) * LOG2E
    for w in range(BATCH):
        hat, _ = normalize(xs[span(w), :])
        work[span(w), :] = hat * vecs[0:1, :] + vecs[1:2, :]
    low[...] = work[...].astype(BF16)
    for c in range(3):
        at = slice(c * width, (c + 1) * width)
        qkv[:, at] = dot_nt(low[...], sizes.attention_part(weights, c)) + wide_bias[:, at]

    if between is not None:
        between()

    def attend(w, _):
        row = span(w)
        for g in range(groups):
            col = g * LANES
            q = qkv[row, pl.ds(col, LANES)].astype(BF16)
            k = qkv[row, pl.ds(width + col, LANES)]
            v = qkv[row, pl.ds(2 * width + col, LANES)]
            scores = dot(q, spread_columns(k))
            parts = []
            for h in range(PACK):
                s = scores[:, h * LANES : (h + 1) * LANES] * scale + bias[g * PACK + h]
                e = jnp.exp2(s - jnp.max(s, axis=-1, keepdims=True))
                parts.append(e * (1.0 / jnp.sum(e, axis=-1, keepdims=True)))
            probs = jnp.concatenate(parts, axis=1).astype(BF16)
            if keep is not None:
                keep[w * groups + g] = probs
            mixed[row, pl.ds(col, LANES)] = dot(probs, spread_rows(v))
        return 0

    lax.fori_loop(0, BATCH, attend, 0)
    middle[...] = xs[...] + dot(mixed[...].astype(BF16), sizes.attention_part(weights, 3)) + vecs[2:3, :]


def second_norm(vecs, middle, work, low):
    for w in range(BATCH):
        hat, _ = normalize(middle[span(w), :])
        work[span(w), :] = hat * vecs[3:4, :] + vecs[4:5, :]
    low[...] = work[...].astype(BF16)


def feed(sizes, hid_bias, vecs, weights, middle, low, acc):
    acc[...] = middle[...] + vecs[5:6, :]

    def block(i, _):
        hidden = dot_nt(low[...], sizes.expand_part(weights, i)) + hid_bias[i, 0:1, 0 : sizes.units]
        cdf, _ = normal_cdf(hidden)
        acc[...] += dot((hidden * cdf).astype(BF16), sizes.shrink_part(weights, i))
        return 0

    lax.fori_loop(0, sizes.shards, block, 0, unroll=4)


def column_sum(v):
    return jnp.sum(v, axis=0, keepdims=True)


def feed_both(sizes, hid_bias, vecs, weights, middle, low, glow, acc, back, dw, unit_sums):
    base, units = 4 * sizes.loc, sizes.units
    acc[...] = middle[...] + vecs[5:6, :]
    back[...] = jnp.zeros_like(back)

    def block(i, _):
        w_in, w_out = sizes.expand_part(weights, i), sizes.shrink_part(weights, i)
        hidden = dot_nt(low[...], w_in) + hid_bias[i, 0:1, 0 : sizes.units]
        cdf, bell = normal_cdf(hidden)
        active = (hidden * cdf).astype(BF16)
        grad = (dot_nt(glow[...], w_out) * (cdf + hidden * bell * DENSITY))
        unit_sums[i] += column_sum(grad)
        grad = grad.astype(BF16)
        acc[...] += dot(active, w_out)
        back[...] += dot(grad, w_in)
        dw[i, :, base : base + units] += dot_tn(low[...], grad)
        dw[i, :, base + units : base + 2 * units] += dot_tn(glow[...], active)
        return 0

    lax.fori_loop(0, sizes.shards, block, 0, unroll=4)


def backward(sizes, vecs, weights, xs, work, low, qkv, mixed, middle, glow, back, gmid, keep, dw, dbias, sums, between):
    width, groups = sizes.width, sizes.groups
    scale = HEAD ** (-0.5)
    gmix, dqkv = work, qkv
    for w in range(BATCH):
        hat, inv = normalize(middle[span(w), :])
        grad = back[span(w), :]
        sums[3:4, :] += column_sum(grad * hat)
        sums[4:5, :] += column_sum(grad)
        gmid[span(w), :] += norm_back(grad * vecs[3:4, :], hat, inv)
    branch = gmid[...].astype(BF16)
    sums[5:6, :] += column_sum(gmid[...])
    sizes.add_attention(dw, 3, dot_tn(branch, mixed[...].astype(BF16)))
    gmix[...] = dot_nt(branch, sizes.attention_part(weights, 3))
    between()

    def attend(w, _):
        row = span(w)
        for g in range(groups):
            col = g * LANES
            q = qkv[row, pl.ds(col, LANES)]
            k = qkv[row, pl.ds(width + col, LANES)]
            v = qkv[row, pl.ds(2 * width + col, LANES)]
            grad = gmix[row, pl.ds(col, LANES)]
            probs = keep[w * groups + g]
            wide_grad = dot(grad.astype(BF16), spread_columns(v))
            parts = []
            for h in range(PACK):
                p = probs[:, h * LANES : (h + 1) * LANES].astype(F32)
                t = wide_grad[:, h * LANES : (h + 1) * LANES]
                s = p * (t - jnp.sum(p * t, axis=-1, keepdims=True))
                dbias[g * PACK + h] += s
                parts.append(s)
            score = jnp.concatenate(parts, axis=1).astype(BF16)
            turned = pad_rows(q).T[:, :PAD].astype(BF16)
            dqkv[row, pl.ds(col, LANES)] = dot(score, spread_rows(k)) * scale
            dqkv[row, pl.ds(width + col, LANES)] = diagonal(dot(turned, score)).T[:PAD] * scale
            turned = pad_rows(grad).T[:, :PAD].astype(BF16)
            dqkv[row, pl.ds(2 * width + col, LANES)] = diagonal(dot(turned, probs)).T[:PAD]
        return 0

    lax.fori_loop(0, BATCH, attend, 0)
    for w in range(BATCH):
        hat, _ = normalize(xs[span(w), :])
        work[span(w), :] = hat * vecs[0:1, :] + vecs[1:2, :]
    low[...] = work[...].astype(BF16)
    back[...] = jnp.zeros_like(back)
    for c in range(3):
        at = slice(c * width, (c + 1) * width)
        grad = dqkv[:, at]
        if c != 1:
            sums[c // 2 : c // 2 + 1, :] += column_sum(grad)
        grad = grad.astype(BF16)
        back[...] += dot(grad, sizes.attention_part(weights, c))
        sizes.add_attention(dw, c, dot_tn(low[...], grad))
    for w in range(BATCH):
        hat, inv = normalize(xs[span(w), :])
        grad = back[span(w), :]
        sums[6:7, :] += column_sum(grad * hat)
        sums[7:8, :] += column_sum(grad)
        gmid[span(w), :] += norm_back(grad * vecs[0:1, :], hat, inv)


def live_scales(first, live):
    return [jnp.where(first + w < live[0], 1.0, 0.0).astype(F32) for w in range(BATCH)]


class Place:
    def __init__(self, mesh_shape):
        self.shards, self.n_dp = mesh_shape["mp"], mesh_shape["dp"]
        self.chips = self.n_dp // 2
        self.bits = int(math.log2(self.chips))
        self.dp, self.z = lax.axis_index("dp"), lax.axis_index("mp")
        self.core, self.chip = lax.rem(self.dp, 2), lax.div(self.dp, 2)
        self.bit_values = [lax.rem(lax.div(self.chip, 1 << b), 2) for b in range(self.bits)]
        self.flips = [
            self.chip + sum((1 << b) * (1 - 2 * self.bit_values[b]) for b in range(self.bits) if m >> b & 1)
            for m in range(self.chips)
        ]
        self.rounds = [lax.rem(self.z + k, self.shards) for k in range(self.shards)]

    def mate(self):
        return (self.dp + 1 - 2 * self.core, self.z)

    def flip(self, m):
        return self.flips[m]

    def across(self, m):
        return (2 * self.flip(m) + self.core, self.z)

    def bit(self, b):
        return self.bit_values[b]

    def along(self, k):
        return (self.dp, self.rounds[k])

    def greet(self, targets):
        barrier = pltpu.get_barrier_semaphore()
        for target in targets:
            pl.semaphore_signal(barrier, inc=1, device_id=target, device_id_type=MESH)
        pl.semaphore_wait(barrier, len(targets))

    def everyone(self):
        return (
            [self.mate()]
            + [self.across(m) for m in range(1, self.chips)]
            + [self.along(k) for k in range(1, self.shards)]
        )


def remote(source, target, sent, received, device):
    return pltpu.make_async_remote_copy(source, target, sent, received, device_id=device, device_id_type=MESH)


class Sends:
    def __init__(self):
        self.sent = []

    def send(self, make, when=None):
        self.sent.append((make, when))
        if when is None:
            make().start()
        else:
            pl.when(when())(lambda: make().start())

    def finish(self):
        for make, when in self.sent:
            if when is None:
                make().wait_send()
            else:
                pl.when(when())(lambda make=make: make().wait_send())


class Gather:
    def __init__(self, here, sends, out, parts, small, scratch):
        self.here, self.sends, self.out, self.parts, self.small = here, sends, out, parts, small
        self.z_sem, self.s_sem, self.p_sem, self.m_sem = scratch

    def spot(self, part, shard, dp):
        first, rows = self.parts[part]
        rows //= self.here.n_dp
        return self.out.at[shard, pl.ds(pl.multiple_of(first + dp * rows, 16), rows)]

    def origin(self, way, step):
        return jnp.clip(self.here.z - (1 - 2 * way) * step, 0, self.here.shards - 1)

    def there(self, way, step, reach=0):
        held, onward = self.here.z - (1 - 2 * way) * step, self.here.z + (1 - 2 * way) * reach
        return (held >= 0) & (held < self.here.shards) & (onward >= 0) & (onward < self.here.shards)

    def along(self, part, way, step, arriving=False):
        here = self.here
        spot = self.spot(part, self.origin(way, step), here.dp)
        at = step - 1 if arriving else step
        target = (here.dp, jnp.clip(here.z + 1 - 2 * way, 0, here.shards - 1))
        return remote(spot, spot, self.z_sem.at[0, part, way, at], self.z_sem.at[1, part, way, at], target)

    def along_send(self, part, way, step):
        self.sends.send(functools.partial(self.along, part, way, step), functools.partial(self.there, way, step, 1))

    def small_along(self, k, arriving=False):
        here = self.here
        spot = self.small.at[here.rounds[here.shards - k] if arriving else here.z]
        return remote(spot, spot, self.s_sem.at[0, k], self.s_sem.at[1, k], here.along(k))

    def start(self):
        for k in range(1, self.here.shards):
            self.sends.send(functools.partial(self.small_along, k))

    def wait_small(self):
        for k in range(1, self.here.shards):
            self.small_along(k, True).wait_recv()

    def start_part(self, part):
        for way in range(2):
            self.along_send(part, way, 0)

    def piece(self, part, way, step, m, core, side=None):
        spot = self.spot(part, self.origin(way, step), 2 * self.here.flip(m) + core)
        if side is None:
            return spot
        half = self.out.shape[2] // 2
        return spot.at[:, pl.ds(side * half, half)]

    def hop(self, part, way, step, m, side, bit, arriving=False):
        here = self.here
        spot = self.piece(part, way, step, m | bit if arriving else m, here.core, side)
        slot = (part, way, step, m | bit, side or 0)
        return remote(spot, spot, self.p_sem.at[0, *slot], self.p_sem.at[1, *slot], here.across(bit))

    def mate(self, part, way, step, m, side, arriving=False):
        here = self.here
        spot = self.piece(part, way, step, m, 1 - here.core if arriving else here.core, side)
        slot = (part, way, step, m, side or 0)
        return remote(spot, spot, self.m_sem.at[0, *slot], self.m_sem.at[1, *slot], here.mate())

    def both(self, step, body):
        for way in range(2):
            makes = []

            def run(way=way, makes=makes):
                for make in body(way):
                    if make is not None:
                        make().start()
                        makes.append(make)

            pl.when(self.there(way, step))(run)
            for make in makes:
                self.sends.sent.append((make, functools.partial(self.there, way, step)))

    def advance(self, part, step):
        for way in range(2):
            pl.when(self.there(way, step))(lambda way=way: self.along(part, way, step, True).wait_recv())
            if step < self.here.shards - 1:
                self.along_send(part, way, step)

        def body(way):
            for b in range(self.here.bits):
                yield functools.partial(self.hop, part, way, step, 0, None, 1 << b)
            yield functools.partial(self.mate, part, way, step, 0, None)

        self.both(step, body)

    def pieces(self):
        bits = self.here.bits
        orders = (tuple(range(bits)), tuple(reversed(range(bits))))
        for m in sorted(range(1, self.here.chips), key=lambda m: m.bit_count()):
            if m.bit_count() == 1:
                yield m, None, m, [(s, [1 << b for b in o[o.index(m.bit_length() - 1) + 1 :]]) for s, o in enumerate(orders)]
            else:
                for s, o in enumerate(orders):
                    last = max(o.index(b) for b in range(bits) if m >> b & 1)
                    yield m, s, 1 << o[last], [(s, [1 << b for b in o[last + 1 :]])]

    def relay(self, part, step, far):
        def body(way):
            for m, side, bit, onward in self.pieces():
                if (m.bit_count() > 1) != far:
                    continue
                self.hop(part, way, step, m - bit, side, bit, True).wait_recv()
                for s, later in onward:
                    for nxt in later:
                        yield functools.partial(self.hop, part, way, step, m, s, nxt)
                yield functools.partial(self.mate, part, way, step, m, side)

        self.both(step, body)

    def wait(self, part):
        for step in range(1, self.here.shards):

            def body(way, step=step):
                self.mate(part, way, step, 0, None, True).wait_recv()
                for m, side, _, _ in self.pieces():
                    self.mate(part, way, step, m, side, True).wait_recv()
                return ()

            self.both(step, body)


def gather_scratch(mesh_shape, parts):
    shards, chips = mesh_shape["mp"], mesh_shape["dp"] // 2
    dma = pltpu.SemaphoreType.DMA
    return [
        dma((2, parts, 2, shards)),
        dma((2, shards)),
        dma((2, parts, 2, shards, chips, 2)),
        dma((2, parts, 2, shards, chips, 2)),
    ]


class Lines:
    def __init__(self, here, sends, source, target, sem, reach):
        self.here, self.sends, self.source, self.target, self.sem, self.reach = here, sends, source, target, sem, reach

    def block(self, z, c):
        chunks = self.source.shape[0]
        return self.target.at[pl.ds(pl.multiple_of((z * chunks + c) * CHUNK, 16), CHUNK)]

    def local(self, c):
        return pltpu.make_async_copy(self.source.at[c], self.block(self.here.z, c), self.sem.at[0, c, 0, self.reach])

    def copy(self, c, way, step, reach, arriving=False):
        here, sign = self.here, 1 - 2 * way
        held = jnp.clip(here.z - sign * step, 0, here.shards - 1)
        at = step - 1 if arriving else step + reach - 1
        source = self.source.at[c] if step == 0 else self.block(held, c)
        target = (here.dp, jnp.clip(here.z + sign * reach, 0, here.shards - 1))
        return remote(source, self.block(held, c), self.sem.at[0, c, way, at], self.sem.at[1, c, way, at], target)

    def there(self, way, step, reach):
        here, sign = self.here, 1 - 2 * way
        held, onward = here.z - sign * step, here.z + sign * reach
        return (held >= 0) & (held < here.shards) & (onward >= 0) & (onward < here.shards)

    def send(self, c, step, reach):
        for way in range(2):
            self.sends.send(
                functools.partial(self.copy, c, way, step, reach), functools.partial(self.there, way, step, reach)
            )

    def start(self, c):
        for reach in range(1, min(2, self.reach) + 1):
            self.send(c, 0, reach)

    def arrive(self, c, step):
        for way in range(2):
            pl.when(self.there(way, step, 0))(lambda way=way: self.copy(c, way, step, 1, True).wait_recv())

    def forward(self, c, step):
        self.arrive(c, step)
        self.send(c, step, 1)


class Reduction:
    def __init__(self, here, sends, dw, final, span, scratch):
        (self.acc, self.half, self.parts, self.lasts, self.h_sem, self.q_sem, self.l_sem, self.f_sem, self.g_sem) = scratch
        self.dw, self.final, self.here, self.sends = dw, final, here, sends
        self.d = dw.shape[1]
        self.first, self.columns = span
        split = self.columns // 2
        self.sides = (pl.ds(0, split), pl.ds(split, split))
        self.orders = (tuple(range(here.bits)), tuple(reversed(range(here.bits))))

    def send(self, make):
        self.sends.send(make)

    def rows_of(self, side, core, chip_bit, depth):
        size = self.d // 2
        first = core * size
        for b in self.orders[side][:depth]:
            size //= 2
            first = first + chip_bit(b) * size
        return pl.ds(pl.multiple_of(first, 16), size)

    def half_rows(self, core):
        return pl.ds(pl.multiple_of(core * (self.d // 2), 16), self.d // 2)

    def half_copy(self, s):
        rows = self.half_rows(1 - self.here.core)
        return remote(self.acc.at[s, rows], self.half.at[s], self.h_sem.at[0, s], self.h_sem.at[1, s], self.here.mate())

    def half_send(self, s):
        rows = self.half_rows(1 - self.here.core)
        self.acc[s, rows, :] = self.dw[s, rows, pl.ds(self.first, self.columns)].astype(BF16)
        self.send(functools.partial(self.half_copy, s))

    def half_add(self, s):
        self.half_copy(s).wait_recv()
        mine = self.half_rows(self.here.core)
        self.acc[s, mine, :] = (self.dw[s, mine, pl.ds(self.first, self.columns)] + self.half[s].astype(F32)).astype(BF16)

    def plane_copy(self, s, depth, side):
        here = self.here
        b = self.orders[side][depth]
        rows = self.rows_of(side, here.core, lambda c: 1 - here.bit(c) if c == b else here.bit(c), depth + 1)
        target = self.parts[side][depth].at[s]
        sems = self.q_sem
        return remote(
            self.acc.at[s, rows, self.sides[side]], target, sems.at[0, side, depth, s], sems.at[1, side, depth, s], here.across(1 << b)
        )

    def plane_send(self, s, depth):
        for side in range(2):
            self.send(functools.partial(self.plane_copy, s, depth, side))

    def plane_add(self, s, depth):
        for side in range(2):
            self.plane_copy(s, depth, side).wait_recv()
            rows = self.rows_of(side, self.here.core, self.here.bit, depth + 1)
            arrived = self.parts[side][depth][s]
            here = self.acc[s, rows, self.sides[side]]
            self.acc[s, rows, self.sides[side]] = (here.astype(F32) + arrived.astype(F32)).astype(BF16)

    def mine(self, side):
        return self.rows_of(side, self.here.core, self.here.bit, self.here.bits)

    def shard_copy(self, side, k):
        here = self.here
        s = here.rounds[k]
        return remote(
            self.acc.at[s, self.mine(side), self.sides[side]], self.lasts[side].at[k], self.l_sem.at[0, side, k], self.l_sem.at[1, side, k], here.along(k)
        )

    def shard_sends(self):
        for k in range(1, self.here.shards):
            for side in range(2):
                self.send(functools.partial(self.shard_copy, side, k))

    def shard_adds(self):
        for side in range(2):
            rows = self.mine(side)
            total = self.acc[self.here.z, rows, self.sides[side]].astype(F32)
            for k in range(1, self.here.shards):
                self.shard_copy(side, k).wait_recv()
                total = total + self.lasts[side][k].astype(F32)
            self.final[rows, self.final_side(side)] = total.astype(BF16)

    def final_side(self, side):
        split = self.columns // 2
        return pl.ds(self.first + side * split, split)

    def final_spot(self, side, m, core):
        here = self.here
        rows = self.rows_of(side, core, lambda b: 1 - here.bit(b) if m >> b & 1 else here.bit(b), here.bits)
        return self.final.at[rows, self.final_side(side)]

    def final_copy(self, side, m, arriving=False):
        here = self.here
        spot = self.final_spot(side, m if arriving else 0, here.core)
        return remote(spot, spot, self.f_sem.at[0, side, m], self.f_sem.at[1, side, m], here.across(m))

    def final_relay(self, side, m, arriving=False):
        here = self.here
        spot = self.final_spot(side, m, 1 - here.core if arriving else here.core)
        return remote(spot, spot, self.g_sem.at[0, side, m], self.g_sem.at[1, side, m], here.mate())

    def final_spread(self):
        for side in range(2):
            for m in range(1, self.here.chips):
                self.send(functools.partial(self.final_copy, side, m))
            self.send(functools.partial(self.final_relay, side, 0))

    def final_relays(self):
        for side in range(2):
            for m in range(1, self.here.chips):
                self.final_copy(side, m, True).wait_recv()
                self.send(functools.partial(self.final_relay, side, m))

    def final_wait(self):
        for side in range(2):
            for m in range(self.here.chips):
                self.final_relay(side, m, True).wait_recv()

    def start(self):
        for s in range(self.here.shards):
            self.half_send(s)

    def plane(self, depth):
        for s in range(self.here.shards):
            if depth == 0:
                self.half_add(s)
            else:
                self.plane_add(s, depth - 1)
            if depth < self.here.bits:
                self.plane_send(s, depth)
        if depth == self.here.bits:
            self.shard_sends()

    def close(self):
        self.shard_adds()
        self.final_spread()


def reduce_scratch(mesh_shape, d, columns):
    shards, chips = mesh_shape["mp"], mesh_shape["dp"] // 2
    bits = int(math.log2(chips))
    split, finish = columns // 2, d // (2 * chips)
    dma = pltpu.SemaphoreType.DMA
    return [
        pltpu.VMEM((shards, d, columns), BF16),
        pltpu.VMEM((shards, d // 2, columns), BF16),
        [[pltpu.VMEM((shards, d >> (depth + 2), split), BF16) for depth in range(bits)]] * 2,
        [pltpu.VMEM((shards, finish, split), BF16)] * 2,
        dma((2, shards)),
        dma((2, 2, bits, shards)),
        dma((2, 2, shards)),
        dma((2, 2, chips)),
        dma((2, 2, chips)),
    ]


class Totals:
    def __init__(self, here, sends, out, scratch):
        self.here, self.sends, self.small_out = here, sends, out
        self.sums, self.sums_in, self.t_sem = scratch
        self.stages = here.bits + 1

    def send(self, make):
        self.sends.send(make)

    def small_copy(self, i):
        here = self.here
        target = here.mate() if i == 0 else here.across(1 << (i - 1))
        return remote(self.sums.at[i], self.sums_in.at[i], self.t_sem.at[0, i], self.t_sem.at[1, i], target)

    def small_send(self, i):
        self.send(functools.partial(self.small_copy, i))

    def small_add(self, i):
        self.small_copy(i).wait_recv()
        self.sums[i + 1] = self.sums[i] + self.sums_in[i]

    def small_along(self, k):
        slot = self.stages + k - 1
        return remote(
            self.sums.at[self.stages], self.sums_in.at[slot], self.t_sem.at[0, slot], self.t_sem.at[1, slot], self.here.along(k)
        )

    def small_sends(self):
        for k in range(1, self.here.shards):
            self.send(functools.partial(self.small_along, k))

    def small_total(self):
        total = self.sums[self.stages]
        for k in range(1, self.here.shards):
            self.small_along(k).wait_recv()
            total = total + self.sums_in[self.stages + k - 1]
        self.small_out[...] = total


def totals_scratch(mesh_shape, shape):
    shards, chips = mesh_shape["mp"], mesh_shape["dp"] // 2
    bits = int(math.log2(chips))
    return [
        pltpu.VMEM((bits + 2, *shape), F32),
        pltpu.VMEM((bits + shards, *shape), F32),
        pltpu.SemaphoreType.DMA((2, bits + shards)),
    ]


TALL = 384
BLOCK = 8


def one_hot(index_row):
    return (lax.broadcasted_iota(jnp.int32, (TALL, LANES), 0) == index_row).astype(F32).astype(BF16)


def build_bias(index, table, bias):
    heads = table.shape[0]
    tall = jnp.broadcast_to(table[:, None, :], (heads, BLOCK, TALL)).reshape(heads * BLOCK, TALL).astype(BF16)
    row = lax.rem(lax.broadcasted_iota(jnp.int32, (heads * BLOCK, LANES), 0), BLOCK)
    blocked = jnp.where(lax.broadcasted_iota(jnp.int32, (heads * BLOCK, LANES), 1) < AREA, 0.0, -1e30)

    def block(r, _):
        at = pl.ds(pl.multiple_of(r * BLOCK, BLOCK), BLOCK)
        rows = index[at, :]
        out = blocked
        for i in range(BLOCK):
            values = dot(tall, one_hot(rows[i : i + 1, :]))
            out = jnp.where(row == i, values * LOG2E + blocked, out)
        bias[:, at, :] = out.reshape(heads, BLOCK, LANES)
        return 0

    lax.fori_loop(0, PAD // BLOCK, block, 0)


def sum_table(index, dbias, turned):
    heads = dbias.shape[0]
    row = lax.rem(lax.broadcasted_iota(jnp.int32, (heads * BLOCK, LANES), 0), BLOCK)
    turned[...] = jnp.zeros_like(turned)

    def block(r, _):
        at = pl.ds(pl.multiple_of(r * BLOCK, BLOCK), BLOCK)
        rows = index[at, :]
        values = dbias[:, at, :].reshape(heads * BLOCK, LANES)
        left = jnp.concatenate([one_hot(rows[i : i + 1, :]) for i in range(BLOCK)], axis=1)
        right = jnp.concatenate([jnp.where(row == i, values, 0.0) for i in range(BLOCK)], axis=1).astype(BF16)
        turned[...] += dot_nt(left, right)
        return 0

    lax.fori_loop(0, PAD // BLOCK, block, 0)


def block_kernel(sizes, mesh_shape, exchange, early, live, offsets, singles, pair, table_in, unit_in, tokens, cotangent,
                 triple_in, output_in, expand_in, shrink_in,
                 result, gtok, final, small_out,
                 index, vecs, saved, weights, smalls, wide_bias, bias, dbias, dw, xs, qkv, mixed, middle, keep,
                 wide, work, low, glow, back, gmid, sums, unit_sums, turned,
                 tok_in, cot_in, rows_in, rows_out,
                 own_sem, tok_sem, cot_sem, in_sem, out_sem, result_sem, gtok_sem,
                 gather_refs, feed_refs, attn_refs, total_refs):
    here = Place(mesh_shape)
    sends = Sends()
    own_out, own_grad = tok_in, cot_in
    shards, own = sizes.shards, tok_in.shape[0]
    chunks = shards * own
    loc, units = sizes.loc, sizes.units
    gather = Gather(here, sends, weights, ((0, 4 * loc), (4 * loc, 2 * units)), smalls, gather_refs)
    feed_sum = Reduction(here, sends, dw, final, (4 * loc, 2 * units), feed_refs)
    attn_sum = Reduction(here, sends, dw, final, (0, 4 * loc), attn_refs)
    totals = Totals(here, sends, small_out, total_refs)
    results = Lines(here, sends, own_out, result, result_sem, 1)
    grads = Lines(here, sends, own_grad, gtok, gtok_sem, shards - 1)

    def own_rows(c):
        return pl.ds(pl.multiple_of((here.z * own + c) * CHUNK, 16), CHUNK)

    def own_tokens(c):
        return pltpu.make_async_copy(tokens.at[own_rows(c)], tok_in.at[c], tok_sem.at[c])

    def own_cotangent(c):
        return pltpu.make_async_copy(cotangent.at[own_rows(c)], cot_in.at[c], cot_sem.at[c])

    mine = [
        pltpu.make_async_copy(output_in, weights.at[here.z, pl.ds(3 * loc, loc)], own_sem.at[0]),
        pltpu.make_async_copy(shrink_in, weights.at[here.z, pl.ds(4 * loc + units, units)], own_sem.at[1]),
    ]
    for copy in mine:
        copy.start()
    for c in range(own):
        own_tokens(c).start()
    for c in range(own):
        own_cotangent(c).start()
    for c in range(3):
        weights[here.z, c * loc : (c + 1) * loc, :] = triple_in[c].astype(F32).T.astype(BF16)
    heads = sizes.width // HEAD
    count = heads // shards
    smalls[here.z, 0:1, 0:units] = unit_in[...].astype(F32).reshape(1, units)
    smalls[here.z, 1:2, 0:loc] = pair[0:1, :].astype(F32)
    smalls[here.z, 1:2, loc : 2 * loc] = pair[1:2, :].astype(F32)
    smalls[here.z, 2 : 2 + count, 0:TALL] = jnp.zeros((count, TALL), F32)
    smalls[here.z, 2 : 2 + count, 0 : table_in.shape[1]] = table_in[...].astype(F32)
    here.greet(here.everyone())
    mine[0].wait()
    gather.start_part(0)
    gather.start()
    weights[here.z, 4 * loc : 4 * loc + units, :] = expand_in[...].astype(F32).T.astype(BF16)
    mine[1].wait()
    index[...] = jnp.full(index.shape, -1, jnp.int32)
    index[0:AREA, 0:AREA] = offsets[...]
    for line, single in enumerate(singles):
        vecs[line : line + 1, :] = single[...].astype(F32).reshape(1, vecs.shape[1])
    steps = range(1, shards)
    for step in steps:
        gather.advance(0, step)
        if step == 1:
            gather.start_part(1)
    for step in steps:
        gather.relay(0, step, False)
    gather.advance(1, 1)
    xs[...] = jnp.zeros_like(xs)
    dbias[...] = jnp.zeros_like(dbias)
    sums[...] = jnp.zeros_like(sums)
    unit_sums[...] = jnp.zeros_like(unit_sums)
    gather.wait_small()
    for z in range(shards):
        at = slice(z * loc, (z + 1) * loc)
        wide_bias[:, at] = smalls[z, 1:2, 0:loc]
        wide_bias[:, slice(2 * sizes.width + z * loc, 2 * sizes.width + (z + 1) * loc)] = smalls[z, 1:2, loc : 2 * loc]
    wide_bias[:, sizes.width : 2 * sizes.width] = jnp.zeros((1, sizes.width), F32)
    table = jnp.concatenate([smalls[z, 2 : 2 + count, 0:TALL] for z in range(shards)], axis=0)
    build_bias(index, table, bias)
    for step in steps:
        gather.relay(0, step, True)
    for step in steps[1:-1]:
        gather.advance(1, step)
    gather.wait(0)
    jobs = {}
    if shards > 2:
        jobs.setdefault(0, []).append(functools.partial(gather.advance, 1, shards - 1))
    for step in steps:
        at = min((step - 1) // 2, 2 * own - 2)
        jobs.setdefault(at, []).append(functools.partial(gather.relay, 1, step, False))
        jobs.setdefault(at + 1, []).append(functools.partial(gather.relay, 1, step, True))

    extra = chunks - own
    before = jnp.int32(0)
    if exchange == own:
        before = jnp.maximum(here.z - 1, 0) * own
        after = jnp.maximum(shards - 2 - here.z, 0) * own
        extras, most = before + after, extra - own

        def chunk_of(i):
            return jnp.where(i < before, i, i - before + (here.z + 2) * own)
    else:
        extras, most = jnp.int32(extra), extra

        def chunk_of(i):
            return lax.rem((here.z + 1) * own + i, chunks)

    def rows(i):
        return pl.ds(pl.multiple_of(chunk_of(i) * CHUNK, 16), CHUNK)

    def fetch(i):
        return pltpu.make_async_copy(tokens.at[rows(i)], rows_in.at[lax.rem(i, 2)], in_sem.at[lax.rem(i, 2)])

    def put(i):
        return pltpu.make_async_copy(rows_out.at[lax.rem(i, 2)], result.at[rows(i)], out_sem.at[lax.rem(i, 2)])

    def attend(c, _):
        own_tokens(c).wait()
        load_rows(tok_in[c], wide, xs.at[c])

        def relays(point):
            for at in sorted(jobs):
                if at % 2 == point:

                    def run(at=at):
                        for job in jobs[at]:
                            job()

                    pl.when(c == at // 2)(run)

        attention(
            sizes, bias, vecs, wide_bias, weights, xs.at[c], work, low, qkv.at[c], mixed.at[c], middle.at[c], keep.at[c],
            functools.partial(relays, 0),
        )
        relays(1)
        return 0

    lax.fori_loop(0, own, attend, 0)
    def clear(z, _):
        dw[z] = jnp.zeros_like(dw[z])
        return 0

    lax.fori_loop(0, shards, clear, 0)


    if early:
        first = dw.at[0, pl.ds(0, ROWS)], dw.at[1, pl.ds(0, ROWS), pl.ds(0, 512)], dw.at[1, pl.ds(0, ROWS), pl.ds(512, 512)]

        def ahead(e, _):
            at = most - early + e
            fetch(at).start()
            fetch(at).wait()
            load_rows(rows_in[lax.rem(at, 2)], wide, first[1])
            attention(sizes, bias, vecs, wide_bias, weights, first[1], work, low, first[0], first[2], saved.at[e], None)
            return 0

        lax.fori_loop(0, early, ahead, 0)
        for z in range(2):
            dw[z] = jnp.zeros_like(dw[z])
    gather.wait(1)

    def finish(c, _):
        scales = live_scales((here.z * own + c) * BATCH, live)
        own_cotangent(c).wait()
        second_norm(vecs, middle.at[c], work, low)
        wide[...] = cot_in[c].astype(F32)
        for w in range(BATCH):
            gmid[w * PAD : w * PAD + AREA, :] = wide[w * AREA : (w + 1) * AREA, :] * scales[w]
            gmid[w * PAD + AREA : (w + 1) * PAD, :] = jnp.zeros((PAD - AREA, gmid.shape[1]), F32)
        sums[2:3, :] += column_sum(gmid[...])
        glow[...] = gmid[...].astype(BF16)
        feed_both(sizes, smalls, vecs, weights, middle.at[c], low, glow, work, back, dw, unit_sums)
        store_rows(work, wide, own_out.at[c], scales)
        for i in range(own):

            def fed(i=i):
                results.local(i).start()
                if i < exchange:
                    results.start(i)
                if i == own - 1:
                    feed_sum.start()

            pl.when(c == i)(fed)

        def between():
            pl.when(c == own - 1)(lambda: feed_sum.plane(0))

        backward(sizes, vecs, weights, xs.at[c], work, low, qkv.at[c], mixed.at[c], middle.at[c], glow, back, gmid, keep.at[c], dw, dbias, sums, between)
        store_rows(gmid, wide, own_grad.at[c])
        for i in range(own):

            def done(i=i):
                grads.local(i).start()
                grads.send(i, 0, 1)
                grads.send(i, 0, 2)

            pl.when(c == i)(done)
        return 0

    lax.fori_loop(0, own, finish, 0)
    attn_sum.start()
    sum_table(index, dbias, turned)
    table = turned[...].T
    total = totals.sums
    total[0, 0:8, :] = sums[...]
    for z in range(shards):
        at = z * units % sizes.width
        line = 8 + z * units // sizes.width
        total[0, line : line + 1, at : at + units] = unit_sums[z]
    base = 8 + shards * units // sizes.width
    total[0, base : base + heads, 0:TALL] = jnp.sum(table.reshape(heads, BLOCK, TALL), axis=1)
    totals.small_send(0)

    pl.when(extras > 0)(lambda: fetch(0).start())
    bits = here.bits
    points = 2 * most
    moves = {p: [] for p in range(points + 1)}

    def place(p, step):
        moves[max(0, min(p, points))].append(step)

    place(0, functools.partial(attn_sum.plane, 0))
    for depth in range(1, bits + 1):
        place(3 * depth - 2, functools.partial(feed_sum.plane, depth))
        place(3 * depth - 1, functools.partial(attn_sum.plane, depth))
    for i in range(totals.stages):

        def small_step(i=i):
            totals.small_add(i)
            if i + 1 < totals.stages:
                totals.small_send(i + 1)
            else:
                totals.small_sends()

        place(2 * i + 1, small_step)
    for n in range(2, shards - 1):
        for c in range(own):
            place(2 * n - 2 + 8 * c, functools.partial(grads.forward, c, n))
    place(points - 4, feed_sum.close)
    place(points - 2, feed_sum.final_relays)
    place(points - 2, attn_sum.close)

    def run(i, half):
        for at in range(points):
            if at % 2 == half and moves[at]:

                def go(at=at):
                    for move in moves[at]:
                        move()

                pl.when(i == at // 2)(go)

    states = (xs.at[0], work, low, qkv.at[0], mixed.at[0], middle.at[0])

    def other(i, _):
        @pl.when(i < extras - early)
        def _():
            fetch(i).wait()
            pl.when(i + 1 < extras - early)(lambda: fetch(i + 1).start())
            load_rows(rows_in[lax.rem(i, 2)], wide, xs.at[0])
            attention(sizes, bias, vecs, wide_bias, weights, *states, None)

        run(i, 0)
        if early:

            @pl.when(i >= most - early)
            def _():
                middle[0] = saved[i - (most - early)]

        @pl.when(i < extras)
        def _():
            second_norm(vecs, middle.at[0], work, low)
            feed(sizes, smalls, vecs, weights, middle.at[0], low, work)
            pl.when(i >= 2)(lambda: put(i - 2).wait())
            store_rows(work, wide, rows_out.at[lax.rem(i, 2)], live_scales(chunk_of(i) * BATCH, live))
            put(i).start()

        run(i, 1)
        return 0

    lax.fori_loop(0, most, other, 0)
    for move in moves[points]:
        move()
    attn_sum.final_relays()
    totals.small_total()
    for c in range(exchange):
        results.arrive(c, 1)
    for c in range(own):
        for n in range(1, shards):
            if n < 2 or n == shards - 1:
                grads.arrive(c, n)
    attn_sum.final_wait()
    feed_sum.final_wait()
    sends.finish()
    for c in range(own):
        results.local(c).wait()
        grads.local(c).wait()
    for back_by in (2, 1):
        pl.when(extras >= back_by)(lambda back_by=back_by: put(extras - back_by).wait())


def run_block(sizes, mesh_shape, exchange, early, live, offsets, singles, pair, table, unit, tokens, cotangent, *raw):
    d = tokens.shape[1]
    shards, width, units, groups = sizes.shards, sizes.width, sizes.units, sizes.groups
    heads = width // HEAD
    own = tokens.shape[0] // CHUNK // shards
    anywhere = pl.BlockSpec(memory_space=pl.ANY)
    here = pl.BlockSpec(memory_space=pltpu.VMEM)
    dma = pltpu.SemaphoreType.DMA
    total_shape = (8 + shards * units // d + heads, d)
    return pl.pallas_call(
        functools.partial(block_kernel, sizes, mesh_shape, exchange, early),
        out_shape=(
            jax.ShapeDtypeStruct(tokens.shape, BF16),
            jax.ShapeDtypeStruct(tokens.shape, BF16),
            jax.ShapeDtypeStruct((d, sizes.columns), BF16),
            jax.ShapeDtypeStruct(total_shape, F32),
        ),
        in_specs=[pl.BlockSpec(memory_space=pltpu.SMEM), here, [here] * 6, here, here, here, anywhere, anywhere, here, anywhere, here, anywhere],
        out_specs=(anywhere, anywhere, here, here),
        scratch_shapes=[
            pltpu.VMEM((PAD, LANES), jnp.int32),
            pltpu.VMEM((8, d), F32),
            pltpu.VMEM((max(early, 1), ROWS, d) if early else (1, 8, LANES), F32),
            pltpu.VMEM((shards, sizes.columns, d), BF16),
            pltpu.VMEM((shards, 8, d), F32),
            pltpu.VMEM((1, 3 * width), F32),
            pltpu.VMEM((heads, PAD, LANES), F32),
            pltpu.VMEM((heads, PAD, LANES), F32),
            pltpu.VMEM((shards, d, sizes.columns), F32),
            pltpu.VMEM((own, ROWS, d), F32),
            pltpu.VMEM((own, ROWS, 3 * width), F32),
            pltpu.VMEM((own, ROWS, width), F32),
            pltpu.VMEM((own, ROWS, d), F32),
            pltpu.VMEM((own, BATCH * groups, PAD, PACK * LANES), BF16),
            pltpu.VMEM((CHUNK, d), F32),
            pltpu.VMEM((ROWS, d), F32),
            pltpu.VMEM((ROWS, d), BF16),
            pltpu.VMEM((ROWS, d), BF16),
            pltpu.VMEM((ROWS, d), F32),
            pltpu.VMEM((ROWS, d), F32),
            pltpu.VMEM((8, d), F32),
            pltpu.VMEM((shards, 1, units), F32),
            pltpu.VMEM((TALL, heads * BLOCK), F32),
            pltpu.VMEM((own, CHUNK, d), BF16),
            pltpu.VMEM((own, CHUNK, d), BF16),
            pltpu.VMEM((2, CHUNK, d), BF16),
            pltpu.VMEM((2, CHUNK, d), BF16),
            dma((2,)),
            dma((own,)),
            dma((own,)),
            dma((2,)),
            dma((2,)),
            dma((2, own, 2, 2)),
            dma((2, own, 2, shards)),
            gather_scratch(mesh_shape, 2),
            reduce_scratch(mesh_shape, d, 2 * units),
            reduce_scratch(mesh_shape, d, 4 * sizes.loc),
            totals_scratch(mesh_shape, total_shape),
        ],
        compiler_params=pltpu.CompilerParams(collective_id=0, has_side_effects=True, vmem_limit_bytes=VMEM_LIMIT),
    )(live, offsets, singles, pair, table, unit, tokens, cotangent, *raw)


def finish_kernel(sizes, z, final, packed, *refs):
    triple, output, expand, shrink, pair, table, unit, *singles = refs
    loc, units = sizes.loc, sizes.units
    d = final.shape[0]
    count = sizes.width // HEAD // sizes.shards
    for c in range(3):
        triple[c] = final[:, c * loc : (c + 1) * loc].astype(F32)
    output[...] = final[:, 3 * loc : 4 * loc].astype(F32).T
    expand[...] = final[:, 4 * loc : 4 * loc + units].astype(F32)
    shrink[...] = final[:, 4 * loc + units :].astype(F32).T
    base = 8 + sizes.shards * units // d
    for s in range(sizes.shards):

        def take(s=s):
            pair[...] = packed[0:2, s * loc : (s + 1) * loc]
            table[...] = packed[base + s * count : base + (s + 1) * count, 0 : table.shape[1]]
            at = s * units % d
            line = 8 + s * units // d
            unit[...] = packed[line : line + 1, at : at + units]

        pl.when(z[0] == s)(take)
    for ref, line in zip(singles, (6, 7, 5, 3, 4, 2)):
        ref[...] = packed[line : line + 1, :]


def run_finish(sizes, table_rows, z, final, packed):
    loc, units, d = sizes.loc, sizes.units, final.shape[0]
    count = sizes.width // HEAD // sizes.shards
    shapes = [(3, d, loc), (loc, d), (d, units), (units, d), (2, loc), (count, table_rows), (1, units)] + [(1, d)] * 6
    here = pl.BlockSpec(memory_space=pltpu.VMEM)
    return pl.pallas_call(
        functools.partial(finish_kernel, sizes),
        out_shape=tuple(jax.ShapeDtypeStruct(shape, F32) for shape in shapes),
        in_specs=[pl.BlockSpec(memory_space=pltpu.SMEM), here, here],
        out_specs=tuple([here] * len(shapes)),
        compiler_params=pltpu.CompilerParams(vmem_limit_bytes=VMEM_LIMIT),
    )(z, final, packed)


def local(
    mesh_shape,
    tokens,
    cotangent,
    group_windows,
    offset_index,
    first_gain,
    first_shift,
    triple_weight,
    query_value_bias,
    bias_table,
    output_weight,
    output_bias,
    second_gain,
    second_shift,
    expand_weight,
    expand_bias,
    shrink_weight,
    shrink_bias,
):
    z = lax.axis_index("mp")
    shards = mesh_shape["mp"]
    d, _, loc = triple_weight.shape
    units = expand_weight.shape[1]
    table_rows, loc_heads = bias_table.shape
    heads = shards * loc_heads
    sizes = Sizes(shards, loc, units)
    early = EARLY if sizes.columns == 3 * sizes.width else 0
    singles = [first_gain, first_shift, output_bias, second_gain, second_shift, shrink_bias]
    result, grad_tokens, final, packed = run_block(
        sizes,
        mesh_shape,
        EXCHANGE,
        early,
        group_windows,
        offset_index,
        singles,
        query_value_bias,
        bias_table.T,
        expand_bias,
        tokens,
        cotangent,
        triple_weight.transpose(1, 0, 2),
        output_weight,
        expand_weight,
        shrink_weight,
    )
    triple, output, expand, shrink, pair, table, unit, *singles = run_finish(sizes, table_rows, z.reshape(1), final, packed)
    first_gain, first_shift, output_sum, second_gain, second_shift, shrink_sum = (v.reshape(d) for v in singles)
    return (
        result,
        grad_tokens,
        first_gain,
        first_shift,
        triple.transpose(1, 0, 2),
        pair,
        table.T,
        output,
        output_sum,
        second_gain,
        second_shift,
        expand,
        unit.reshape(units),
        shrink,
        shrink_sum,
    )


EXCHANGE = 0
EARLY = 0


def solution(mesh):
    in_specs = (
        P("dp", None),
        P("dp", None),
        P("dp"),
        P(),
        P(),
        P(),
        P(None, None, "mp"),
        P(None, "mp"),
        P(None, "mp"),
        P("mp", None),
        P(),
        P(),
        P(),
        P(None, "mp"),
        P("mp"),
        P("mp", None),
        P(),
    )
    out_specs = (
        P("dp", None),
        P("dp", None),
        P(),
        P(),
        P(None, None, "mp"),
        P(None, "mp"),
        P(None, "mp"),
        P("mp", None),
        P(),
        P(),
        P(),
        P(None, "mp"),
        P("mp"),
        P("mp", None),
        P(),
    )
    step = functools.partial(local, dict(mesh.shape))
    return jax.shard_map(step, mesh=mesh, in_specs=in_specs, out_specs=out_specs, check_vma=False)
```

```python
import functools
import math
import jax
import jax.numpy as jnp
from jax import lax
from jax.experimental import pallas as pl
from jax.experimental.pallas import tpu as pltpu
from jax.sharding import PartitionSpec as P

AREA = 100
PAD = 104
HEAD = 32
LANES = 128
PACK = LANES // HEAD
BATCH = 4
CHUNK = BATCH * AREA
ROWS = BATCH * PAD
EPSILON = 1e-05
DENSITY = 0.3989422804014327
LOG2E = 1.4426950408889634
F32 = jnp.float32
BF16 = jnp.bfloat16
MESH = pl.DeviceIdType.MESH
VMEM_LIMIT = 63 * 2**20


def dot(a, b):
    return jnp.dot(a, b, preferred_element_type=F32)


def dot_nt(a, b):
    return lax.dot_general(a, b, (((1,), (1,)), ((), ())), preferred_element_type=F32)


def dot_tn(a, b):
    return lax.dot_general(a, b, (((0,), (0,)), ((), ())), preferred_element_type=F32)


def normalize(values):
    centered = values - jnp.mean(values, axis=-1, keepdims=True)
    inv = lax.rsqrt(jnp.mean(centered * centered, axis=-1, keepdims=True) + EPSILON)
    return centered * inv, inv


def norm_back(grad, hat, inv):
    return inv * (
        grad
        - jnp.mean(grad, axis=-1, keepdims=True)
        - hat * jnp.mean(grad * hat, axis=-1, keepdims=True)
    )


def normal_cdf(hidden):
    bell = jnp.exp2(hidden * hidden * (-0.5 * LOG2E))
    return 0.5 + 0.5 * lax.erf(hidden * 0.7071067811865476), bell


def head_of(shape, axis):
    return lax.broadcasted_iota(jnp.int32, shape, axis) // HEAD


def pad_rows(v):
    return jnp.concatenate([v, jnp.zeros((LANES - PAD, v.shape[1]), v.dtype)], axis=0)


def spread_rows(v):
    head = head_of((LANES, LANES), 1)
    full = pad_rows(v)
    return jnp.concatenate([jnp.where(head == h, full, 0.0) for h in range(PACK)], axis=0).astype(BF16)


def spread_columns(v):
    head = head_of((LANES, LANES), 0)
    turned = pad_rows(v).T
    return jnp.concatenate([jnp.where(head == h, turned, 0.0) for h in range(PACK)], axis=1).astype(BF16)


def diagonal(full):
    head = head_of((LANES, LANES), 0)
    out = full[:, 0:LANES]
    for h in range(1, PACK):
        out = jnp.where(head == h, full[:, h * LANES : (h + 1) * LANES], out)
    return out


def span(w, size=PAD):
    return pl.ds(pl.multiple_of(w * PAD, 8), size)


def load_rows(source, wide, padded):
    wide[...] = source.astype(F32)
    for w in range(BATCH):
        padded[w * PAD : w * PAD + AREA, :] = wide[w * AREA : (w + 1) * AREA, :]


def store_rows(padded, wide, target, scales=None):
    for w in range(BATCH):
        rows = padded[w * PAD : w * PAD + AREA, :]
        wide[w * AREA : (w + 1) * AREA, :] = rows if scales is None else rows * scales[w]
    target[...] = wide[...].astype(BF16)


class Sizes:
    def __init__(self, shards, loc, units):
        self.shards, self.loc, self.units = shards, loc, units
        self.width = shards * loc
        self.groups = self.width // LANES
        self.columns = 4 * loc + 2 * units

    def attention_part(self, weights, c):
        at = slice(c * self.loc, (c + 1) * self.loc)
        return jnp.concatenate([weights[z, at, :] for z in range(self.shards)], axis=0)

    def expand_part(self, weights, i):
        return weights[i, pl.ds(4 * self.loc, self.units), :]

    def shrink_part(self, weights, i):
        return weights[i, pl.ds(4 * self.loc + self.units, self.units), :]

    def add_attention(self, dw, c, value):
        for z in range(self.shards):
            at = slice(c * self.loc, (c + 1) * self.loc)
            dw[z, :, at] += value[:, z * self.loc : (z + 1) * self.loc]


def attention(sizes, bias, vecs, wide_bias, weights, xs, work, low, qkv, mixed, middle, keep, between=None):
    width, groups = sizes.width, sizes.groups
    scale = HEAD ** (-0.5) * LOG2E
    for w in range(BATCH):
        hat, _ = normalize(xs[span(w), :])
        work[span(w), :] = hat * vecs[0:1, :] + vecs[1:2, :]
    low[...] = work[...].astype(BF16)
    for c in range(3):
        at = slice(c * width, (c + 1) * width)
        qkv[:, at] = dot_nt(low[...], sizes.attention_part(weights, c)) + wide_bias[:, at]

    if between is not None:
        between()

    def attend(w, _):
        row = span(w)
        for g in range(groups):
            col = g * LANES
            q = qkv[row, pl.ds(col, LANES)].astype(BF16)
            k = qkv[row, pl.ds(width + col, LANES)]
            v = qkv[row, pl.ds(2 * width + col, LANES)]
            scores = dot(q, spread_columns(k))
            parts = []
            for h in range(PACK):
                s = scores[:, h * LANES : (h + 1) * LANES] * scale + bias[g * PACK + h]
                e = jnp.exp2(s - jnp.max(s, axis=-1, keepdims=True))
                parts.append(e * (1.0 / jnp.sum(e, axis=-1, keepdims=True)))
            probs = jnp.concatenate(parts, axis=1).astype(BF16)
            if keep is not None:
                keep[w * groups + g] = probs
            mixed[row, pl.ds(col, LANES)] = dot(probs, spread_rows(v))
        return 0

    lax.fori_loop(0, BATCH, attend, 0)
    middle[...] = xs[...] + dot(mixed[...].astype(BF16), sizes.attention_part(weights, 3)) + vecs[2:3, :]


def second_norm(vecs, middle, work, low):
    for w in range(BATCH):
        hat, _ = normalize(middle[span(w), :])
        work[span(w), :] = hat * vecs[3:4, :] + vecs[4:5, :]
    low[...] = work[...].astype(BF16)


def feed(sizes, hid_bias, vecs, weights, middle, low, acc):
    acc[...] = middle[...] + vecs[5:6, :]

    def block(i, _):
        hidden = dot_nt(low[...], sizes.expand_part(weights, i)) + hid_bias[i, 0:1, 0 : sizes.units]
        cdf, _ = normal_cdf(hidden)
        acc[...] += dot((hidden * cdf).astype(BF16), sizes.shrink_part(weights, i))
        return 0

    lax.fori_loop(0, sizes.shards, block, 0, unroll=4)


def column_sum(v):
    return jnp.sum(v, axis=0, keepdims=True)


def feed_both(sizes, hid_bias, vecs, weights, middle, low, glow, acc, back, dw, unit_sums):
    base, units = 4 * sizes.loc, sizes.units
    acc[...] = middle[...] + vecs[5:6, :]
    back[...] = jnp.zeros_like(back)

    def block(i, _):
        w_in, w_out = sizes.expand_part(weights, i), sizes.shrink_part(weights, i)
        hidden = dot_nt(low[...], w_in) + hid_bias[i, 0:1, 0 : sizes.units]
        cdf, bell = normal_cdf(hidden)
        active = (hidden * cdf).astype(BF16)
        grad = (dot_nt(glow[...], w_out) * (cdf + hidden * bell * DENSITY))
        unit_sums[i] += column_sum(grad)
        grad = grad.astype(BF16)
        acc[...] += dot(active, w_out)
        back[...] += dot(grad, w_in)
        dw[i, :, base : base + units] += dot_tn(low[...], grad)
        dw[i, :, base + units : base + 2 * units] += dot_tn(glow[...], active)
        return 0

    lax.fori_loop(0, sizes.shards, block, 0, unroll=4)


def backward(sizes, vecs, weights, xs, work, low, qkv, mixed, middle, glow, back, gmid, keep, dw, dbias, sums, between):
    width, groups = sizes.width, sizes.groups
    scale = HEAD ** (-0.5)
    gmix, dqkv = work, qkv
    for w in range(BATCH):
        hat, inv = normalize(middle[span(w), :])
        grad = back[span(w), :]
        sums[3:4, :] += column_sum(grad * hat)
        sums[4:5, :] += column_sum(grad)
        gmid[span(w), :] += norm_back(grad * vecs[3:4, :], hat, inv)
    branch = gmid[...].astype(BF16)
    sums[5:6, :] += column_sum(gmid[...])
    sizes.add_attention(dw, 3, dot_tn(branch, mixed[...].astype(BF16)))
    gmix[...] = dot_nt(branch, sizes.attention_part(weights, 3))
    between()

    def attend(w, _):
        row = span(w)
        for g in range(groups):
            col = g * LANES
            q = qkv[row, pl.ds(col, LANES)]
            k = qkv[row, pl.ds(width + col, LANES)]
            v = qkv[row, pl.ds(2 * width + col, LANES)]
            grad = gmix[row, pl.ds(col, LANES)]
            probs = keep[w * groups + g]
            wide_grad = dot(grad.astype(BF16), spread_columns(v))
            parts = []
            for h in range(PACK):
                p = probs[:, h * LANES : (h + 1) * LANES].astype(F32)
                t = wide_grad[:, h * LANES : (h + 1) * LANES]
                s = p * (t - jnp.sum(p * t, axis=-1, keepdims=True))
                dbias[g * PACK + h] += s
                parts.append(s)
            score = jnp.concatenate(parts, axis=1).astype(BF16)
            turned = pad_rows(q).T[:, :PAD].astype(BF16)
            dqkv[row, pl.ds(col, LANES)] = dot(score, spread_rows(k)) * scale
            dqkv[row, pl.ds(width + col, LANES)] = diagonal(dot(turned, score)).T[:PAD] * scale
            turned = pad_rows(grad).T[:, :PAD].astype(BF16)
            dqkv[row, pl.ds(2 * width + col, LANES)] = diagonal(dot(turned, probs)).T[:PAD]
        return 0

    lax.fori_loop(0, BATCH, attend, 0)
    for w in range(BATCH):
        hat, _ = normalize(xs[span(w), :])
        work[span(w), :] = hat * vecs[0:1, :] + vecs[1:2, :]
    low[...] = work[...].astype(BF16)
    back[...] = jnp.zeros_like(back)
    for c in range(3):
        at = slice(c * width, (c + 1) * width)
        grad = dqkv[:, at]
        if c != 1:
            sums[c // 2 : c // 2 + 1, :] += column_sum(grad)
        grad = grad.astype(BF16)
        back[...] += dot(grad, sizes.attention_part(weights, c))
        sizes.add_attention(dw, c, dot_tn(low[...], grad))
    for w in range(BATCH):
        hat, inv = normalize(xs[span(w), :])
        grad = back[span(w), :]
        sums[6:7, :] += column_sum(grad * hat)
        sums[7:8, :] += column_sum(grad)
        gmid[span(w), :] += norm_back(grad * vecs[0:1, :], hat, inv)


def live_scales(first, live):
    return [jnp.where(first + w < live[0], 1.0, 0.0).astype(F32) for w in range(BATCH)]


class Place:
    def __init__(self, mesh_shape):
        self.shards, self.n_dp = mesh_shape["mp"], mesh_shape["dp"]
        self.chips = self.n_dp // 2
        self.bits = int(math.log2(self.chips))
        self.dp, self.z = lax.axis_index("dp"), lax.axis_index("mp")
        self.core, self.chip = lax.rem(self.dp, 2), lax.div(self.dp, 2)
        self.bit_values = [lax.rem(lax.div(self.chip, 1 << b), 2) for b in range(self.bits)]
        self.flips = [
            self.chip + sum((1 << b) * (1 - 2 * self.bit_values[b]) for b in range(self.bits) if m >> b & 1)
            for m in range(self.chips)
        ]
        self.rounds = [lax.rem(self.z + k, self.shards) for k in range(self.shards)]

    def mate(self):
        return (self.dp + 1 - 2 * self.core, self.z)

    def flip(self, m):
        return self.flips[m]

    def across(self, m):
        return (2 * self.flip(m) + self.core, self.z)

    def bit(self, b):
        return self.bit_values[b]

    def along(self, k):
        return (self.dp, self.rounds[k])

    def greet(self, targets):
        barrier = pltpu.get_barrier_semaphore()
        for target in targets:
            pl.semaphore_signal(barrier, inc=1, device_id=target, device_id_type=MESH)
        pl.semaphore_wait(barrier, len(targets))

    def everyone(self):
        return (
            [self.mate()]
            + [self.across(m) for m in range(1, self.chips)]
            + [self.along(k) for k in range(1, self.shards)]
        )


def remote(source, target, sent, received, device):
    return pltpu.make_async_remote_copy(source, target, sent, received, device_id=device, device_id_type=MESH)


class Sends:
    def __init__(self):
        self.sent = []

    def send(self, make, when=None):
        self.sent.append((make, when))
        if when is None:
            make().start()
        else:
            pl.when(when())(lambda: make().start())

    def finish(self):
        for make, when in self.sent:
            if when is None:
                make().wait_send()
            else:
                pl.when(when())(lambda make=make: make().wait_send())


class Gather:
    def __init__(self, here, sends, out, parts, small, scratch):
        self.here, self.sends, self.out, self.parts, self.small = here, sends, out, parts, small
        self.z_sem, self.s_sem, self.p_sem, self.m_sem = scratch

    def spot(self, part, shard, dp):
        first, rows = self.parts[part]
        rows //= self.here.n_dp
        return self.out.at[shard, pl.ds(pl.multiple_of(first + dp * rows, 16), rows)]

    def origin(self, way, step):
        return jnp.clip(self.here.z - (1 - 2 * way) * step, 0, self.here.shards - 1)

    def there(self, way, step, reach=0):
        held, onward = self.here.z - (1 - 2 * way) * step, self.here.z + (1 - 2 * way) * reach
        return (held >= 0) & (held < self.here.shards) & (onward >= 0) & (onward < self.here.shards)

    def along(self, part, way, step, arriving=False):
        here = self.here
        spot = self.spot(part, self.origin(way, step), here.dp)
        at = step - 1 if arriving else step
        target = (here.dp, jnp.clip(here.z + 1 - 2 * way, 0, here.shards - 1))
        return remote(spot, spot, self.z_sem.at[0, part, way, at], self.z_sem.at[1, part, way, at], target)

    def along_send(self, part, way, step):
        self.sends.send(functools.partial(self.along, part, way, step), functools.partial(self.there, way, step, 1))

    def small_along(self, k, arriving=False):
        here = self.here
        spot = self.small.at[here.rounds[here.shards - k] if arriving else here.z]
        return remote(spot, spot, self.s_sem.at[0, k], self.s_sem.at[1, k], here.along(k))

    def start(self):
        for k in range(1, self.here.shards):
            self.sends.send(functools.partial(self.small_along, k))

    def wait_small(self):
        for k in range(1, self.here.shards):
            self.small_along(k, True).wait_recv()

    def start_part(self, part):
        for way in range(2):
            self.along_send(part, way, 0)

    def piece(self, part, way, step, m, core, side=None):
        spot = self.spot(part, self.origin(way, step), 2 * self.here.flip(m) + core)
        if side is None:
            return spot
        half = self.out.shape[2] // 2
        return spot.at[:, pl.ds(side * half, half)]

    def hop(self, part, way, step, m, side, bit, arriving=False):
        here = self.here
        spot = self.piece(part, way, step, m | bit if arriving else m, here.core, side)
        slot = (part, way, step, m | bit, side or 0)
        return remote(spot, spot, self.p_sem.at[0, *slot], self.p_sem.at[1, *slot], here.across(bit))

    def mate(self, part, way, step, m, side, arriving=False):
        here = self.here
        spot = self.piece(part, way, step, m, 1 - here.core if arriving else here.core, side)
        slot = (part, way, step, m, side or 0)
        return remote(spot, spot, self.m_sem.at[0, *slot], self.m_sem.at[1, *slot], here.mate())

    def both(self, step, body):
        for way in range(2):
            makes = []

            def run(way=way, makes=makes):
                for make in body(way):
                    if make is not None:
                        make().start()
                        makes.append(make)

            pl.when(self.there(way, step))(run)
            for make in makes:
                self.sends.sent.append((make, functools.partial(self.there, way, step)))

    def advance(self, part, step):
        for way in range(2):
            pl.when(self.there(way, step))(lambda way=way: self.along(part, way, step, True).wait_recv())
            if step < self.here.shards - 1:
                self.along_send(part, way, step)

        def body(way):
            for b in range(self.here.bits):
                yield functools.partial(self.hop, part, way, step, 0, None, 1 << b)
            yield functools.partial(self.mate, part, way, step, 0, None)

        self.both(step, body)

    def pieces(self):
        bits = self.here.bits
        orders = (tuple(range(bits)), tuple(reversed(range(bits))))
        for m in sorted(range(1, self.here.chips), key=lambda m: m.bit_count()):
            if m.bit_count() == 1:
                yield m, None, m, [(s, [1 << b for b in o[o.index(m.bit_length() - 1) + 1 :]]) for s, o in enumerate(orders)]
            else:
                for s, o in enumerate(orders):
                    last = max(o.index(b) for b in range(bits) if m >> b & 1)
                    yield m, s, 1 << o[last], [(s, [1 << b for b in o[last + 1 :]])]

    def relay(self, part, step, far):
        def body(way):
            for m, side, bit, onward in self.pieces():
                if (m.bit_count() > 1) != far:
                    continue
                self.hop(part, way, step, m - bit, side, bit, True).wait_recv()
                for s, later in onward:
                    for nxt in later:
                        yield functools.partial(self.hop, part, way, step, m, s, nxt)
                yield functools.partial(self.mate, part, way, step, m, side)

        self.both(step, body)

    def wait(self, part):
        for step in range(1, self.here.shards):

            def body(way, step=step):
                self.mate(part, way, step, 0, None, True).wait_recv()
                for m, side, _, _ in self.pieces():
                    self.mate(part, way, step, m, side, True).wait_recv()
                return ()

            self.both(step, body)


def gather_scratch(mesh_shape, parts):
    shards, chips = mesh_shape["mp"], mesh_shape["dp"] // 2
    dma = pltpu.SemaphoreType.DMA
    return [
        dma((2, parts, 2, shards)),
        dma((2, shards)),
        dma((2, parts, 2, shards, chips, 2)),
        dma((2, parts, 2, shards, chips, 2)),
    ]


class Lines:
    def __init__(self, here, sends, source, target, sem, reach):
        self.here, self.sends, self.source, self.target, self.sem, self.reach = here, sends, source, target, sem, reach

    def block(self, z, c):
        chunks = self.source.shape[0]
        return self.target.at[pl.ds(pl.multiple_of((z * chunks + c) * CHUNK, 16), CHUNK)]

    def local(self, c):
        return pltpu.make_async_copy(self.source.at[c], self.block(self.here.z, c), self.sem.at[0, c, 0, self.reach])

    def copy(self, c, way, step, reach, arriving=False):
        here, sign = self.here, 1 - 2 * way
        held = jnp.clip(here.z - sign * step, 0, here.shards - 1)
        at = step - 1 if arriving else step + reach - 1
        source = self.source.at[c] if step == 0 else self.block(held, c)
        target = (here.dp, jnp.clip(here.z + sign * reach, 0, here.shards - 1))
        return remote(source, self.block(held, c), self.sem.at[0, c, way, at], self.sem.at[1, c, way, at], target)

    def there(self, way, step, reach):
        here, sign = self.here, 1 - 2 * way
        held, onward = here.z - sign * step, here.z + sign * reach
        return (held >= 0) & (held < here.shards) & (onward >= 0) & (onward < here.shards)

    def send(self, c, step, reach):
        for way in range(2):
            self.sends.send(
                functools.partial(self.copy, c, way, step, reach), functools.partial(self.there, way, step, reach)
            )

    def start(self, c):
        for reach in range(1, min(2, self.reach) + 1):
            self.send(c, 0, reach)

    def arrive(self, c, step):
        for way in range(2):
            pl.when(self.there(way, step, 0))(lambda way=way: self.copy(c, way, step, 1, True).wait_recv())

    def forward(self, c, step):
        self.arrive(c, step)
        self.send(c, step, 1)


class Reduction:
    def __init__(self, here, sends, dw, final, span, scratch):
        (self.acc, self.half, self.parts, self.lasts, self.h_sem, self.q_sem, self.l_sem, self.f_sem, self.g_sem) = scratch
        self.dw, self.final, self.here, self.sends = dw, final, here, sends
        self.d = dw.shape[1]
        self.first, self.columns = span
        split = self.columns // 2
        self.sides = (pl.ds(0, split), pl.ds(split, split))
        self.orders = (tuple(range(here.bits)), tuple(reversed(range(here.bits))))

    def send(self, make):
        self.sends.send(make)

    def rows_of(self, side, core, chip_bit, depth):
        size = self.d // 2
        first = core * size
        for b in self.orders[side][:depth]:
            size //= 2
            first = first + chip_bit(b) * size
        return pl.ds(pl.multiple_of(first, 16), size)

    def half_rows(self, core):
        return pl.ds(pl.multiple_of(core * (self.d // 2), 16), self.d // 2)

    def half_copy(self, s):
        rows = self.half_rows(1 - self.here.core)
        return remote(self.acc.at[s, rows], self.half.at[s], self.h_sem.at[0, s], self.h_sem.at[1, s], self.here.mate())

    def half_send(self, s):
        rows = self.half_rows(1 - self.here.core)
        self.acc[s, rows, :] = self.dw[s, rows, pl.ds(self.first, self.columns)].astype(BF16)
        self.send(functools.partial(self.half_copy, s))

    def half_add(self, s):
        self.half_copy(s).wait_recv()
        mine = self.half_rows(self.here.core)
        self.acc[s, mine, :] = (self.dw[s, mine, pl.ds(self.first, self.columns)] + self.half[s].astype(F32)).astype(BF16)

    def plane_copy(self, s, depth, side):
        here = self.here
        b = self.orders[side][depth]
        rows = self.rows_of(side, here.core, lambda c: 1 - here.bit(c) if c == b else here.bit(c), depth + 1)
        target = self.parts[side][depth].at[s]
        sems = self.q_sem
        return remote(
            self.acc.at[s, rows, self.sides[side]], target, sems.at[0, side, depth, s], sems.at[1, side, depth, s], here.across(1 << b)
        )

    def plane_send(self, s, depth):
        for side in range(2):
            self.send(functools.partial(self.plane_copy, s, depth, side))

    def plane_add(self, s, depth):
        for side in range(2):
            self.plane_copy(s, depth, side).wait_recv()
            rows = self.rows_of(side, self.here.core, self.here.bit, depth + 1)
            arrived = self.parts[side][depth][s]
            here = self.acc[s, rows, self.sides[side]]
            self.acc[s, rows, self.sides[side]] = (here.astype(F32) + arrived.astype(F32)).astype(BF16)

    def mine(self, side):
        return self.rows_of(side, self.here.core, self.here.bit, self.here.bits)

    def shard_copy(self, side, k):
        here = self.here
        s = here.rounds[k]
        return remote(
            self.acc.at[s, self.mine(side), self.sides[side]], self.lasts[side].at[k], self.l_sem.at[0, side, k], self.l_sem.at[1, side, k], here.along(k)
        )

    def shard_sends(self):
        for k in range(1, self.here.shards):
            for side in range(2):
                self.send(functools.partial(self.shard_copy, side, k))

    def shard_adds(self):
        for side in range(2):
            rows = self.mine(side)
            total = self.acc[self.here.z, rows, self.sides[side]].astype(F32)
            for k in range(1, self.here.shards):
                self.shard_copy(side, k).wait_recv()
                total = total + self.lasts[side][k].astype(F32)
            self.final[rows, self.final_side(side)] = total.astype(BF16)

    def final_side(self, side):
        split = self.columns // 2
        return pl.ds(self.first + side * split, split)

    def final_spot(self, side, m, core):
        here = self.here
        rows = self.rows_of(side, core, lambda b: 1 - here.bit(b) if m >> b & 1 else here.bit(b), here.bits)
        return self.final.at[rows, self.final_side(side)]

    def final_copy(self, side, m, arriving=False):
        here = self.here
        spot = self.final_spot(side, m if arriving else 0, here.core)
        return remote(spot, spot, self.f_sem.at[0, side, m], self.f_sem.at[1, side, m], here.across(m))

    def final_relay(self, side, m, arriving=False):
        here = self.here
        spot = self.final_spot(side, m, 1 - here.core if arriving else here.core)
        return remote(spot, spot, self.g_sem.at[0, side, m], self.g_sem.at[1, side, m], here.mate())

    def final_spread(self):
        for side in range(2):
            for m in range(1, self.here.chips):
                self.send(functools.partial(self.final_copy, side, m))
            self.send(functools.partial(self.final_relay, side, 0))

    def final_relays(self):
        for side in range(2):
            for m in range(1, self.here.chips):
                self.final_copy(side, m, True).wait_recv()
                self.send(functools.partial(self.final_relay, side, m))

    def final_wait(self):
        for side in range(2):
            for m in range(self.here.chips):
                self.final_relay(side, m, True).wait_recv()

    def start(self):
        for s in range(self.here.shards):
            self.half_send(s)

    def plane(self, depth):
        for s in range(self.here.shards):
            if depth == 0:
                self.half_add(s)
            else:
                self.plane_add(s, depth - 1)
            if depth < self.here.bits:
                self.plane_send(s, depth)
        if depth == self.here.bits:
            self.shard_sends()

    def close(self):
        self.shard_adds()
        self.final_spread()


def reduce_scratch(mesh_shape, d, columns):
    shards, chips = mesh_shape["mp"], mesh_shape["dp"] // 2
    bits = int(math.log2(chips))
    split, finish = columns // 2, d // (2 * chips)
    dma = pltpu.SemaphoreType.DMA
    return [
        pltpu.VMEM((shards, d, columns), BF16),
        pltpu.VMEM((shards, d // 2, columns), BF16),
        [[pltpu.VMEM((shards, d >> (depth + 2), split), BF16) for depth in range(bits)]] * 2,
        [pltpu.VMEM((shards, finish, split), BF16)] * 2,
        dma((2, shards)),
        dma((2, 2, bits, shards)),
        dma((2, 2, shards)),
        dma((2, 2, chips)),
        dma((2, 2, chips)),
    ]


class Totals:
    def __init__(self, here, sends, out, scratch):
        self.here, self.sends, self.small_out = here, sends, out
        self.sums, self.sums_in, self.t_sem = scratch
        self.stages = here.bits + 1

    def send(self, make):
        self.sends.send(make)

    def small_copy(self, i):
        here = self.here
        target = here.mate() if i == 0 else here.across(1 << (i - 1))
        return remote(self.sums.at[i], self.sums_in.at[i], self.t_sem.at[0, i], self.t_sem.at[1, i], target)

    def small_send(self, i):
        self.send(functools.partial(self.small_copy, i))

    def small_add(self, i):
        self.small_copy(i).wait_recv()
        self.sums[i + 1] = self.sums[i] + self.sums_in[i]

    def small_along(self, k):
        slot = self.stages + k - 1
        return remote(
            self.sums.at[self.stages], self.sums_in.at[slot], self.t_sem.at[0, slot], self.t_sem.at[1, slot], self.here.along(k)
        )

    def small_sends(self):
        for k in range(1, self.here.shards):
            self.send(functools.partial(self.small_along, k))

    def small_total(self):
        total = self.sums[self.stages]
        for k in range(1, self.here.shards):
            self.small_along(k).wait_recv()
            total = total + self.sums_in[self.stages + k - 1]
        self.small_out[...] = total


def totals_scratch(mesh_shape, shape):
    shards, chips = mesh_shape["mp"], mesh_shape["dp"] // 2
    bits = int(math.log2(chips))
    return [
        pltpu.VMEM((bits + 2, *shape), F32),
        pltpu.VMEM((bits + shards, *shape), F32),
        pltpu.SemaphoreType.DMA((2, bits + shards)),
    ]


TALL = 384
BLOCK = 8


def one_hot(index_row):
    return (lax.broadcasted_iota(jnp.int32, (TALL, LANES), 0) == index_row).astype(F32).astype(BF16)


def build_bias(index, table, bias):
    heads = table.shape[0]
    tall = jnp.broadcast_to(table[:, None, :], (heads, BLOCK, TALL)).reshape(heads * BLOCK, TALL).astype(BF16)
    row = lax.rem(lax.broadcasted_iota(jnp.int32, (heads * BLOCK, LANES), 0), BLOCK)
    blocked = jnp.where(lax.broadcasted_iota(jnp.int32, (heads * BLOCK, LANES), 1) < AREA, 0.0, -1e30)

    def block(r, _):
        at = pl.ds(pl.multiple_of(r * BLOCK, BLOCK), BLOCK)
        rows = index[at, :]
        out = blocked
        for i in range(BLOCK):
            values = dot(tall, one_hot(rows[i : i + 1, :]))
            out = jnp.where(row == i, values * LOG2E + blocked, out)
        bias[:, at, :] = out.reshape(heads, BLOCK, LANES)
        return 0

    lax.fori_loop(0, PAD // BLOCK, block, 0)


def sum_table(index, dbias, turned):
    heads = dbias.shape[0]
    row = lax.rem(lax.broadcasted_iota(jnp.int32, (heads * BLOCK, LANES), 0), BLOCK)
    turned[...] = jnp.zeros_like(turned)

    def block(r, _):
        at = pl.ds(pl.multiple_of(r * BLOCK, BLOCK), BLOCK)
        rows = index[at, :]
        values = dbias[:, at, :].reshape(heads * BLOCK, LANES)
        left = jnp.concatenate([one_hot(rows[i : i + 1, :]) for i in range(BLOCK)], axis=1)
        right = jnp.concatenate([jnp.where(row == i, values, 0.0) for i in range(BLOCK)], axis=1).astype(BF16)
        turned[...] += dot_nt(left, right)
        return 0

    lax.fori_loop(0, PAD // BLOCK, block, 0)


def block_kernel(sizes, mesh_shape, exchange, early, live, offsets, singles, pair, table_in, unit_in, tokens, cotangent,
                 triple_in, output_in, expand_in, shrink_in,
                 result, gtok, final, small_out,
                 index, vecs, saved, weights, smalls, wide_bias, bias, dbias, dw, xs, qkv, mixed, middle, keep,
                 wide, work, low, glow, back, gmid, sums, unit_sums, turned,
                 tok_in, cot_in, rows_in, rows_out,
                 own_sem, tok_sem, cot_sem, in_sem, out_sem, result_sem, gtok_sem,
                 gather_refs, feed_refs, attn_refs, total_refs):
    here = Place(mesh_shape)
    sends = Sends()
    own_out, own_grad = tok_in, cot_in
    shards, own = sizes.shards, tok_in.shape[0]
    chunks = shards * own
    loc, units = sizes.loc, sizes.units
    gather = Gather(here, sends, weights, ((0, 4 * loc), (4 * loc, 2 * units)), smalls, gather_refs)
    feed_sum = Reduction(here, sends, dw, final, (4 * loc, 2 * units), feed_refs)
    attn_sum = Reduction(here, sends, dw, final, (0, 4 * loc), attn_refs)
    totals = Totals(here, sends, small_out, total_refs)
    results = Lines(here, sends, own_out, result, result_sem, 1)
    grads = Lines(here, sends, own_grad, gtok, gtok_sem, shards - 1)

    def own_rows(c):
        return pl.ds(pl.multiple_of((here.z * own + c) * CHUNK, 16), CHUNK)

    def own_tokens(c):
        return pltpu.make_async_copy(tokens.at[own_rows(c)], tok_in.at[c], tok_sem.at[c])

    def own_cotangent(c):
        return pltpu.make_async_copy(cotangent.at[own_rows(c)], cot_in.at[c], cot_sem.at[c])

    mine = [
        pltpu.make_async_copy(output_in, weights.at[here.z, pl.ds(3 * loc, loc)], own_sem.at[0]),
        pltpu.make_async_copy(shrink_in, weights.at[here.z, pl.ds(4 * loc + units, units)], own_sem.at[1]),
    ]
    for copy in mine:
        copy.start()
    for c in range(own):
        own_tokens(c).start()
    for c in range(own):
        own_cotangent(c).start()
    for c in range(3):
        weights[here.z, c * loc : (c + 1) * loc, :] = triple_in[c].astype(F32).T.astype(BF16)
    heads = sizes.width // HEAD
    count = heads // shards
    smalls[here.z, 0:1, 0:units] = unit_in[...].astype(F32).reshape(1, units)
    smalls[here.z, 1:2, 0:loc] = pair[0:1, :].astype(F32)
    smalls[here.z, 1:2, loc : 2 * loc] = pair[1:2, :].astype(F32)
    smalls[here.z, 2 : 2 + count, 0:TALL] = jnp.zeros((count, TALL), F32)
    smalls[here.z, 2 : 2 + count, 0 : table_in.shape[1]] = table_in[...].astype(F32)
    here.greet(here.everyone())
    mine[0].wait()
    gather.start_part(0)
    gather.start()
    weights[here.z, 4 * loc : 4 * loc + units, :] = expand_in[...].astype(F32).T.astype(BF16)
    mine[1].wait()
    index[...] = jnp.full(index.shape, -1, jnp.int32)
    index[0:AREA, 0:AREA] = offsets[...]
    for line, single in enumerate(singles):
        vecs[line : line + 1, :] = single[...].astype(F32).reshape(1, vecs.shape[1])
    steps = range(1, shards)
    for step in steps:
        gather.advance(0, step)
        if step == 1:
            gather.start_part(1)
    for step in steps:
        gather.relay(0, step, False)
    gather.advance(1, 1)
    xs[...] = jnp.zeros_like(xs)
    dbias[...] = jnp.zeros_like(dbias)
    sums[...] = jnp.zeros_like(sums)
    unit_sums[...] = jnp.zeros_like(unit_sums)
    gather.wait_small()
    for z in range(shards):
        at = slice(z * loc, (z + 1) * loc)
        wide_bias[:, at] = smalls[z, 1:2, 0:loc]
        wide_bias[:, slice(2 * sizes.width + z * loc, 2 * sizes.width + (z + 1) * loc)] = smalls[z, 1:2, loc : 2 * loc]
    wide_bias[:, sizes.width : 2 * sizes.width] = jnp.zeros((1, sizes.width), F32)
    table = jnp.concatenate([smalls[z, 2 : 2 + count, 0:TALL] for z in range(shards)], axis=0)
    for step in steps:
        gather.relay(0, step, True)
    for step in steps[1:-1]:
        gather.advance(1, step)
    build_bias(index, table, bias)
    gather.wait(0)
    jobs = {}
    if shards > 2:
        jobs.setdefault(0, []).append(functools.partial(gather.advance, 1, shards - 1))
    for step in steps:
        at = min((step - 1) // 2, 2 * own - 2)
        jobs.setdefault(at, []).append(functools.partial(gather.relay, 1, step, False))
        jobs.setdefault(at + 1, []).append(functools.partial(gather.relay, 1, step, True))

    extra = chunks - own
    before = jnp.int32(0)
    if exchange == own:
        before = jnp.maximum(here.z - 1, 0) * own
        after = jnp.maximum(shards - 2 - here.z, 0) * own
        extras, most = before + after, extra - own

        def chunk_of(i):
            return jnp.where(i < before, i, i - before + (here.z + 2) * own)
    else:
        extras, most = jnp.int32(extra), extra

        def chunk_of(i):
            return lax.rem((here.z + 1) * own + i, chunks)

    def rows(i):
        return pl.ds(pl.multiple_of(chunk_of(i) * CHUNK, 16), CHUNK)

    def fetch(i):
        return pltpu.make_async_copy(tokens.at[rows(i)], rows_in.at[lax.rem(i, 2)], in_sem.at[lax.rem(i, 2)])

    def put(i):
        return pltpu.make_async_copy(rows_out.at[lax.rem(i, 2)], result.at[rows(i)], out_sem.at[lax.rem(i, 2)])

    def attend(c, _):
        own_tokens(c).wait()
        load_rows(tok_in[c], wide, xs.at[c])

        def relays(point):
            for at in sorted(jobs):
                if at % 2 == point:

                    def run(at=at):
                        for job in jobs[at]:
                            job()

                    pl.when(c == at // 2)(run)

        attention(
            sizes, bias, vecs, wide_bias, weights, xs.at[c], work, low, qkv.at[c], mixed.at[c], middle.at[c], keep.at[c],
            functools.partial(relays, 0),
        )
        relays(1)
        return 0

    lax.fori_loop(0, own, attend, 0)
    def clear(z, _):
        dw[z] = jnp.zeros_like(dw[z])
        return 0

    lax.fori_loop(0, shards, clear, 0)


    if early:
        first = dw.at[0, pl.ds(0, ROWS)], dw.at[1, pl.ds(0, ROWS), pl.ds(0, 512)], dw.at[1, pl.ds(0, ROWS), pl.ds(512, 512)]

        def ahead(e, _):
            at = most - early + e
            fetch(at).start()
            fetch(at).wait()
            load_rows(rows_in[lax.rem(at, 2)], wide, first[1])
            attention(sizes, bias, vecs, wide_bias, weights, first[1], work, low, first[0], first[2], saved.at[e], None)
            return 0

        lax.fori_loop(0, early, ahead, 0)
        for z in range(2):
            dw[z] = jnp.zeros_like(dw[z])
    gather.wait(1)

    def finish(c, _):
        scales = live_scales((here.z * own + c) * BATCH, live)
        own_cotangent(c).wait()
        second_norm(vecs, middle.at[c], work, low)
        wide[...] = cot_in[c].astype(F32)
        for w in range(BATCH):
            gmid[w * PAD : w * PAD + AREA, :] = wide[w * AREA : (w + 1) * AREA, :] * scales[w]
            gmid[w * PAD + AREA : (w + 1) * PAD, :] = jnp.zeros((PAD - AREA, gmid.shape[1]), F32)
        sums[2:3, :] += column_sum(gmid[...])
        glow[...] = gmid[...].astype(BF16)
        feed_both(sizes, smalls, vecs, weights, middle.at[c], low, glow, work, back, dw, unit_sums)
        store_rows(work, wide, own_out.at[c], scales)
        for i in range(own):

            def fed(i=i):
                results.local(i).start()
                if i < exchange:
                    results.start(i)
                if i == own - 1:
                    feed_sum.start()

            pl.when(c == i)(fed)

        def between():
            pl.when(c == own - 1)(lambda: feed_sum.plane(0))

        backward(sizes, vecs, weights, xs.at[c], work, low, qkv.at[c], mixed.at[c], middle.at[c], glow, back, gmid, keep.at[c], dw, dbias, sums, between)
        store_rows(gmid, wide, own_grad.at[c])
        for i in range(own):

            def done(i=i):
                grads.local(i).start()
                grads.send(i, 0, 1)
                grads.send(i, 0, 2)

            pl.when(c == i)(done)
        return 0

    lax.fori_loop(0, own, finish, 0)
    attn_sum.start()
    sum_table(index, dbias, turned)
    table = turned[...].T
    total = totals.sums
    total[0, 0:8, :] = sums[...]
    for z in range(shards):
        at = z * units % sizes.width
        line = 8 + z * units // sizes.width
        total[0, line : line + 1, at : at + units] = unit_sums[z]
    base = 8 + shards * units // sizes.width
    total[0, base : base + heads, 0:TALL] = jnp.sum(table.reshape(heads, BLOCK, TALL), axis=1)
    totals.small_send(0)

    pl.when(extras > 0)(lambda: fetch(0).start())
    bits = here.bits
    points = 2 * most
    moves = {p: [] for p in range(points + 1)}

    def place(p, step):
        moves[max(0, min(p, points))].append(step)

    place(0, functools.partial(attn_sum.plane, 0))
    for depth in range(1, bits + 1):
        place(3 * depth - 2, functools.partial(feed_sum.plane, depth))
        place(3 * depth - 1, functools.partial(attn_sum.plane, depth))
    for i in range(totals.stages):

        def small_step(i=i):
            totals.small_add(i)
            if i + 1 < totals.stages:
                totals.small_send(i + 1)
            else:
                totals.small_sends()

        place(2 * i + 1, small_step)
    for n in range(2, shards - 1):
        for c in range(own):
            place(2 * n - 2 + 8 * c, functools.partial(grads.forward, c, n))
    place(points - 4, feed_sum.close)
    place(points - 2, feed_sum.final_relays)
    place(points - 2, attn_sum.close)

    def run(i, half):
        for at in range(points):
            if at % 2 == half and moves[at]:

                def go(at=at):
                    for move in moves[at]:
                        move()

                pl.when(i == at // 2)(go)

    states = (xs.at[0], work, low, qkv.at[0], mixed.at[0], middle.at[0])

    def other(i, _):
        @pl.when(i < extras - early)
        def _():
            fetch(i).wait()
            pl.when(i + 1 < extras - early)(lambda: fetch(i + 1).start())
            load_rows(rows_in[lax.rem(i, 2)], wide, xs.at[0])
            attention(sizes, bias, vecs, wide_bias, weights, *states, None)

        run(i, 0)
        if early:

            @pl.when(i >= most - early)
            def _():
                middle[0] = saved[i - (most - early)]

        @pl.when(i < extras)
        def _():
            second_norm(vecs, middle.at[0], work, low)
            feed(sizes, smalls, vecs, weights, middle.at[0], low, work)
            pl.when(i >= 2)(lambda: put(i - 2).wait())
            store_rows(work, wide, rows_out.at[lax.rem(i, 2)], live_scales(chunk_of(i) * BATCH, live))
            put(i).start()

        run(i, 1)
        return 0

    lax.fori_loop(0, most, other, 0)
    for move in moves[points]:
        move()
    attn_sum.final_relays()
    totals.small_total()
    for c in range(exchange):
        results.arrive(c, 1)
    for c in range(own):
        for n in range(1, shards):
            if n < 2 or n == shards - 1:
                grads.arrive(c, n)
    attn_sum.final_wait()
    feed_sum.final_wait()
    sends.finish()
    for c in range(own):
        results.local(c).wait()
        grads.local(c).wait()
    for back_by in (2, 1):
        pl.when(extras >= back_by)(lambda back_by=back_by: put(extras - back_by).wait())


def run_block(sizes, mesh_shape, exchange, early, live, offsets, singles, pair, table, unit, tokens, cotangent, *raw):
    d = tokens.shape[1]
    shards, width, units, groups = sizes.shards, sizes.width, sizes.units, sizes.groups
    heads = width // HEAD
    own = tokens.shape[0] // CHUNK // shards
    anywhere = pl.BlockSpec(memory_space=pl.ANY)
    here = pl.BlockSpec(memory_space=pltpu.VMEM)
    dma = pltpu.SemaphoreType.DMA
    total_shape = (8 + shards * units // d + heads, d)
    return pl.pallas_call(
        functools.partial(block_kernel, sizes, mesh_shape, exchange, early),
        out_shape=(
            jax.ShapeDtypeStruct(tokens.shape, BF16),
            jax.ShapeDtypeStruct(tokens.shape, BF16),
            jax.ShapeDtypeStruct((d, sizes.columns), BF16),
            jax.ShapeDtypeStruct(total_shape, F32),
        ),
        in_specs=[pl.BlockSpec(memory_space=pltpu.SMEM), here, [here] * 6, here, here, here, anywhere, anywhere, here, anywhere, here, anywhere],
        out_specs=(anywhere, anywhere, here, here),
        scratch_shapes=[
            pltpu.VMEM((PAD, LANES), jnp.int32),
            pltpu.VMEM((8, d), F32),
            pltpu.VMEM((max(early, 1), ROWS, d) if early else (1, 8, LANES), F32),
            pltpu.VMEM((shards, sizes.columns, d), BF16),
            pltpu.VMEM((shards, 8, d), F32),
            pltpu.VMEM((1, 3 * width), F32),
            pltpu.VMEM((heads, PAD, LANES), F32),
            pltpu.VMEM((heads, PAD, LANES), F32),
            pltpu.VMEM((shards, d, sizes.columns), F32),
            pltpu.VMEM((own, ROWS, d), F32),
            pltpu.VMEM((own, ROWS, 3 * width), F32),
            pltpu.VMEM((own, ROWS, width), F32),
            pltpu.VMEM((own, ROWS, d), F32),
            pltpu.VMEM((own, BATCH * groups, PAD, PACK * LANES), BF16),
            pltpu.VMEM((CHUNK, d), F32),
            pltpu.VMEM((ROWS, d), F32),
            pltpu.VMEM((ROWS, d), BF16),
            pltpu.VMEM((ROWS, d), BF16),
            pltpu.VMEM((ROWS, d), F32),
            pltpu.VMEM((ROWS, d), F32),
            pltpu.VMEM((8, d), F32),
            pltpu.VMEM((shards, 1, units), F32),
            pltpu.VMEM((TALL, heads * BLOCK), F32),
            pltpu.VMEM((own, CHUNK, d), BF16),
            pltpu.VMEM((own, CHUNK, d), BF16),
            pltpu.VMEM((2, CHUNK, d), BF16),
            pltpu.VMEM((2, CHUNK, d), BF16),
            dma((2,)),
            dma((own,)),
            dma((own,)),
            dma((2,)),
            dma((2,)),
            dma((2, own, 2, 2)),
            dma((2, own, 2, shards)),
            gather_scratch(mesh_shape, 2),
            reduce_scratch(mesh_shape, d, 2 * units),
            reduce_scratch(mesh_shape, d, 4 * sizes.loc),
            totals_scratch(mesh_shape, total_shape),
        ],
        compiler_params=pltpu.CompilerParams(collective_id=0, has_side_effects=True, vmem_limit_bytes=VMEM_LIMIT),
    )(live, offsets, singles, pair, table, unit, tokens, cotangent, *raw)


def finish_kernel(sizes, z, final, packed, *refs):
    triple, output, expand, shrink, pair, table, unit, *singles = refs
    loc, units = sizes.loc, sizes.units
    d = final.shape[0]
    count = sizes.width // HEAD // sizes.shards
    for c in range(3):
        triple[c] = final[:, c * loc : (c + 1) * loc].astype(F32)
    output[...] = final[:, 3 * loc : 4 * loc].astype(F32).T
    expand[...] = final[:, 4 * loc : 4 * loc + units].astype(F32)
    shrink[...] = final[:, 4 * loc + units :].astype(F32).T
    base = 8 + sizes.shards * units // d
    for s in range(sizes.shards):

        def take(s=s):
            pair[...] = packed[0:2, s * loc : (s + 1) * loc]
            table[...] = packed[base + s * count : base + (s + 1) * count, 0 : table.shape[1]]
            at = s * units % d
            line = 8 + s * units // d
            unit[...] = packed[line : line + 1, at : at + units]

        pl.when(z[0] == s)(take)
    for ref, line in zip(singles, (6, 7, 5, 3, 4, 2)):
        ref[...] = packed[line : line + 1, :]


def run_finish(sizes, table_rows, z, final, packed):
    loc, units, d = sizes.loc, sizes.units, final.shape[0]
    count = sizes.width // HEAD // sizes.shards
    shapes = [(3, d, loc), (loc, d), (d, units), (units, d), (2, loc), (count, table_rows), (1, units)] + [(1, d)] * 6
    here = pl.BlockSpec(memory_space=pltpu.VMEM)
    return pl.pallas_call(
        functools.partial(finish_kernel, sizes),
        out_shape=tuple(jax.ShapeDtypeStruct(shape, F32) for shape in shapes),
        in_specs=[pl.BlockSpec(memory_space=pltpu.SMEM), here, here],
        out_specs=tuple([here] * len(shapes)),
        compiler_params=pltpu.CompilerParams(vmem_limit_bytes=VMEM_LIMIT),
    )(z, final, packed)


def local(
    mesh_shape,
    tokens,
    cotangent,
    group_windows,
    offset_index,
    first_gain,
    first_shift,
    triple_weight,
    query_value_bias,
    bias_table,
    output_weight,
    output_bias,
    second_gain,
    second_shift,
    expand_weight,
    expand_bias,
    shrink_weight,
    shrink_bias,
):
    z = lax.axis_index("mp")
    shards = mesh_shape["mp"]
    d, _, loc = triple_weight.shape
    units = expand_weight.shape[1]
    table_rows, loc_heads = bias_table.shape
    heads = shards * loc_heads
    sizes = Sizes(shards, loc, units)
    early = EARLY if sizes.columns == 3 * sizes.width else 0
    singles = [first_gain, first_shift, output_bias, second_gain, second_shift, shrink_bias]
    result, grad_tokens, final, packed = run_block(
        sizes,
        mesh_shape,
        EXCHANGE,
        early,
        group_windows,
        offset_index,
        singles,
        query_value_bias,
        bias_table.T,
        expand_bias,
        tokens,
        cotangent,
        triple_weight.transpose(1, 0, 2),
        output_weight,
        expand_weight,
        shrink_weight,
    )
    triple, output, expand, shrink, pair, table, unit, *singles = run_finish(sizes, table_rows, z.reshape(1), final, packed)
    first_gain, first_shift, output_sum, second_gain, second_shift, shrink_sum = (v.reshape(d) for v in singles)
    return (
        result,
        grad_tokens,
        first_gain,
        first_shift,
        triple.transpose(1, 0, 2),
        pair,
        table.T,
        output,
        output_sum,
        second_gain,
        second_shift,
        expand,
        unit.reshape(units),
        shrink,
        shrink_sum,
    )


EXCHANGE = 0
EARLY = 0


def solution(mesh):
    in_specs = (
        P("dp", None),
        P("dp", None),
        P("dp"),
        P(),
        P(),
        P(),
        P(None, None, "mp"),
        P(None, "mp"),
        P(None, "mp"),
        P("mp", None),
        P(),
        P(),
        P(),
        P(None, "mp"),
        P("mp"),
        P("mp", None),
        P(),
    )
    out_specs = (
        P("dp", None),
        P("dp", None),
        P(),
        P(),
        P(None, None, "mp"),
        P(None, "mp"),
        P(None, "mp"),
        P("mp", None),
        P(),
        P(),
        P(),
        P(None, "mp"),
        P("mp"),
        P("mp", None),
        P(),
    )
    step = functools.partial(local, dict(mesh.shape))
    return jax.shard_map(step, mesh=mesh, in_specs=in_specs, out_specs=out_specs, check_vma=False)
```
